32 devices in a mesh: wide: 8 (over z, y), narrow: 4 (over x, core).
Axes of the slice: x: 2, y: 2, z: 4, core: 2. Of those that a mesh axis runs over, the one named last changes fastest.
Arguments:
- captions: bfloat16 [64, 64, 768], P(('wide', 'narrow')), may hold values from -6 to 6
- images: bfloat16 [64, 576, 768], P('wide', 'narrow'), may hold values from -6 to 6
- lengths: int32 [64], P(('wide', 'narrow')), may hold values from 5 to 64, as said below
- out_grad: bfloat16 [64, 64, 768], P(('wide', 'narrow')), may hold values from -6 to 6
- self_proj: bfloat16 [768, 2304], P(('wide', 'narrow')), may hold values from -0.21875 to 0.21875
- self_output: bfloat16 [768, 768], P(('wide', 'narrow')), may hold values from -0.875 to 0.875
- cross_query: bfloat16 [768, 768], P(('wide', 'narrow')), may hold values from -0.21875 to 0.21875
- cross_memory: bfloat16 [768, 1536], P(('wide', 'narrow')), may hold values from -0.21875 to 0.21875
- cross_output: bfloat16 [768, 768], P(('wide', 'narrow')), may hold values from -3 to 3
- hidden_up: bfloat16 [768, 3072], P(('wide', 'narrow')), may hold values from -0.21875 to 0.21875
- hidden_down: bfloat16 [3072, 768], P(('wide', 'narrow')), may hold values from -0.109375 to 0.109375
- first_gain: bfloat16 [768], P(('wide', 'narrow')), may hold values from 0.099609375 to 1.8984375
- first_shift: bfloat16 [768], P(('wide', 'narrow')), may hold values from -3 to 3
- second_gain: bfloat16 [768], P(('wide', 'narrow')), may hold values from 0.099609375 to 1.8984375
- second_shift: bfloat16 [768], P(('wide', 'narrow')), may hold values from -3 to 3
- third_gain: bfloat16 [768], P(('wide', 'narrow')), may hold values from 0.099609375 to 1.8984375
- third_shift: bfloat16 [768], P(('wide', 'narrow')), may hold values from -3 to 3
Outputs:
- layer_out: bfloat16 [64, 64, 768], P(('wide', 'narrow'))
- input_grad: bfloat16 [64, 64, 768], P(('wide', 'narrow'))
- image_grad: bfloat16 [64, 576, 768], P('wide', 'narrow')
- self_proj_grad: float32 [768, 2304], P(('wide', 'narrow'))
- self_output_grad: float32 [768, 768], P(('wide', 'narrow'))
- cross_query_grad: float32 [768, 768], P(('wide', 'narrow'))
- cross_memory_grad: float32 [768, 1536], P(('wide', 'narrow'))
- cross_output_grad: float32 [768, 768], P(('wide', 'narrow'))
- hidden_up_grad: float32 [768, 3072], P(('wide', 'narrow'))
- hidden_down_grad: float32 [3072, 768], P(('wide', 'narrow'))
- first_gain_grad: float32 [768], P(('wide', 'narrow'))
- first_shift_grad: float32 [768], P(('wide', 'narrow'))
- second_gain_grad: float32 [768], P(('wide', 'narrow'))
- second_shift_grad: float32 [768], P(('wide', 'narrow'))
- third_gain_grad: float32 [768], P(('wide', 'narrow'))
- third_shift_grad: float32 [768], P(('wide', 'narrow'))
The draws below stay inside these ranges and needn't reach their ends.
Inputs may be any that keep to these rules, and one draw needn't show every extreme that they name: Tokens at positions of lengths or later are padding; some caption has 64 real tokens.
All inputs are finite; a program needn't handle non-finite values.
Results may differ from the reference program's by a relative error of at most 0.025.
Values may be sent and summed in bfloat16 or wider, within the bound.
A program may use at most 128 MiB of HBM per device.

```python
import math
import jax
import jax.numpy as jnp
from jax import lax

D = 768
HEADS = 12
FF = 3072
IMG = 576
SEQ = 64
CAPTIONS = 64


def draw_lengths(key, part):
    key = jax.random.fold_in(key, 11)
    key_len, key_top, key_bottom = jax.random.split(key, 3)
    counts = jax.random.randint(key_len, (CAPTIONS,), 5, SEQ + 1)
    places = jnp.arange(CAPTIONS)
    longest = jax.random.randint(key_top, (), 0, CAPTIONS)
    shortest = jax.random.randint(key_bottom, (), 0, CAPTIONS)
    counts = jnp.where(places == shortest, 5, counts)
    counts = jnp.where(places == longest, SEQ, counts)
    return counts.astype(jnp.int32)


def steps_of(rng, dims, shards, smallest, largest):
    level = 1.0
    for dim, parts in shards:
        heights = jax.random.uniform(jax.random.fold_in(jax.random.fold_in(rng, 6), dim), (parts,), jnp.float32, smallest / len(shards), largest / len(shards))
        level = level * jnp.repeat(jnp.exp(heights), dims[dim] // parts).reshape((-1,) + (1,) * (len(dims) - 1 - dim))
    return level


def normal_values(own_key, shape, scale, most, cuts=(), dtype=jnp.bfloat16):
    level = steps_of(own_key, shape, cuts, -0.22, 0.18) if cuts else 1.0
    entries = jax.random.normal(own_key, shape, jnp.float32) * scale * level
    return jnp.minimum(jnp.maximum(entries, -most), most).astype(dtype)


def setup_inputs(seed: int = 0) -> dict:
    key_of = jax.random.split(jax.random.key(seed), 18)
    captions = normal_values(key_of[0], (CAPTIONS, SEQ, D), 1.0, 6.0, ((0, 32),))
    images = normal_values(key_of[1], (CAPTIONS, IMG, D), 1.0, 6.0, ((0, 8), (1, 4)))
    lengths = draw_lengths(jax.random.fold_in(key_of[17], 71), 0)
    out_grad = normal_values(key_of[3], (CAPTIONS, SEQ, D), 1.0, 6.0, ((0, 32),))
    self_proj = normal_values(key_of[4], (D, 3 * D), D ** -0.5, 0.21875, ((0, 32),))
    self_output = normal_values(key_of[5], (D, D), (D // 16) ** -0.5, 0.875, ((0, 32),))
    cross_query = normal_values(key_of[6], (D, D), D ** -0.5, 0.21875, ((0, 32),))
    cross_memory = normal_values(key_of[7], (D, 2 * D), D ** -0.5, 0.21875, ((0, 32),))
    cross_output = normal_values(key_of[8], (D, D), (D // 192) ** -0.5, 3.0, ((0, 32),))
    hidden_up = normal_values(key_of[9], (D, FF), D ** -0.5, 0.21875, ((0, 32),))
    hidden_down = normal_values(key_of[10], (FF, D), FF ** -0.5, 0.109375, ((0, 32),))
    first_gain = jnp.clip(1.0 + 0.18 * jax.random.normal(key_of[11], (D,), jnp.float32), 0.099609375, 1.8984375).astype(jnp.bfloat16)
    first_shift = normal_values(key_of[12], (D,), 0.5, 3.0, ((0, 32),))
    second_gain = jnp.clip(1.0 + 0.18 * jax.random.normal(key_of[13], (D,), jnp.float32), 0.099609375, 1.8984375).astype(jnp.bfloat16)
    second_shift = normal_values(key_of[14], (D,), 0.5, 3.0, ((0, 32),))
    third_gain = jnp.clip(1.0 + 0.18 * jax.random.normal(key_of[15], (D,), jnp.float32), 0.099609375, 1.8984375).astype(jnp.bfloat16)
    third_shift = normal_values(key_of[16], (D,), 0.5, 3.0, ((0, 32),))
    return {"captions": captions, "images": images, "lengths": lengths, "out_grad": out_grad, "self_proj": self_proj, "self_output": self_output, "cross_query": cross_query, "cross_memory": cross_memory, "cross_output": cross_output, "hidden_up": hidden_up, "hidden_down": hidden_down, "first_gain": first_gain, "first_shift": first_shift, "second_gain": second_gain, "second_shift": second_shift, "third_gain": third_gain, "third_shift": third_shift}


@jax.custom_vjp
def low(v):
    return lax.optimization_barrier(v.astype(jnp.bfloat16)).astype(jnp.float32)

@jax.custom_vjp
def low_back(v):
    return v

def low_keep(v):
    return (low(v), None)

def low_pass(kept, grad):
    return (grad,)

def back_keep(v):
    return (v, None)

def back_low(kept, grad):
    return (low(grad),)
low.defvjp(low_keep, low_pass)
low_back.defvjp(back_keep, back_low)
EPSILON = 1e-05
HIGHEST = lax.Precision.HIGHEST

def both_round(value):
    return low_back(low(value))

def normalize(value, gain, shift):
    center = lax.optimization_barrier(jnp.mean(value, axis=-1, keepdims=True))
    centred = value - center
    spread = lax.optimization_barrier(jnp.mean(centred * centred, axis=-1, keepdims=True))
    return centred * lax.rsqrt(spread + EPSILON) * gain + shift

def layer(captions, images, lengths, self_proj, self_output, cross_query, cross_memory, cross_output, hidden_up, hidden_down, first_gain, first_shift, second_gain, second_shift, third_gain, third_shift):
    count, seq_len, width = captions.shape
    head_size = width // HEADS
    scale = head_size ** (-0.5)
    normed_one = low(normalize(captions, first_gain, first_shift))
    joint = jnp.matmul(normed_one, self_proj, precision=HIGHEST)
    queries = both_round(joint[..., :width]).reshape(count, seq_len, HEADS, head_size)
    keys_self = both_round(joint[..., width:2 * width]).reshape(count, seq_len, HEADS, head_size)
    values_self = both_round(joint[..., 2 * width:]).reshape(count, seq_len, HEADS, head_size)
    scores = low_back(jnp.einsum('cqhe,ckhe->chqk', queries, keys_self, precision=HIGHEST) * scale)
    places = jnp.arange(seq_len)
    allowed = (places[None, :] <= places[:, None])[None, None] & (places[None, None, None, :] < lengths[:, None, None, None])
    scores = jnp.where(allowed, scores, -1000000000.0)
    weights = low(jax.nn.softmax(scores, axis=-1))
    mixed = both_round(jnp.einsum('chqk,ckhe->cqhe', weights, values_self, precision=HIGHEST).reshape(count, seq_len, width))
    first_res = captions + low_back(jnp.matmul(mixed, self_output, precision=HIGHEST))
    normed_two = low(normalize(first_res, second_gain, second_shift))
    cross_q = both_round(jnp.matmul(normed_two, cross_query, precision=HIGHEST)).reshape(count, seq_len, HEADS, head_size)
    image_count = images.shape[1]
    memory = jnp.matmul(images, cross_memory, precision=HIGHEST)
    cross_k = both_round(memory[..., :width]).reshape(count, image_count, HEADS, head_size)
    cross_v = both_round(memory[..., width:]).reshape(count, image_count, HEADS, head_size)
    cross_s = low_back(jnp.einsum('cqhe,ckhe->chqk', cross_q, cross_k, precision=HIGHEST) * scale)
    row_top = lax.optimization_barrier(jnp.max(cross_s, axis=-1, keepdims=True))
    expo = jnp.exp(cross_s - row_top)
    totals = lax.optimization_barrier(jnp.sum(expo, axis=-1))
    numer = low_back(jnp.einsum('chqk,ckhe->cqhe', low(expo), cross_v, precision=HIGHEST))
    attended = low(numer / jnp.transpose(totals, (0, 2, 1))[..., None]).reshape(count, seq_len, width)
    second_res = first_res + low_back(jnp.matmul(attended, cross_output, precision=HIGHEST))
    normed_three = low(normalize(second_res, third_gain, third_shift))
    hidden = low_back(jnp.matmul(normed_three, hidden_up, precision=HIGHEST))
    activated = low(jax.nn.gelu(hidden))
    return second_res + jnp.matmul(activated, hidden_down, precision=HIGHEST)

def reference(captions, images, lengths, out_grad, self_proj, self_output, cross_query, cross_memory, cross_output, hidden_up, hidden_down, first_gain, first_shift, second_gain, second_shift, third_gain, third_shift):
    params = tuple((item.astype(jnp.float32) for item in (self_proj, self_output, cross_query, cross_memory, cross_output, hidden_up, hidden_down, first_gain, first_shift, second_gain, second_shift, third_gain, third_shift)))
    group = math.gcd(CAPTIONS, max(1, 4096 // SEQ))
    rounds = CAPTIONS // group

    def grouped(array):
        return array.reshape((rounds, group) + array.shape[1:])

    def advance(carry, portion):
        text_part, picture_part, length_part, cotangent = portion

        def forward(text_value, picture_value, *weight_values):
            return layer(text_value, picture_value, length_part, *weight_values)
        result, pull = jax.vjp(forward, text_part.astype(jnp.float32), picture_part.astype(jnp.float32), *params)
        grads = pull(cotangent.astype(jnp.float32))
        carry = tuple((total + grad for total, grad in zip(carry, grads[2:])))
        return (carry, (result.astype(jnp.bfloat16), grads[0].astype(jnp.bfloat16), grads[1].astype(jnp.bfloat16)))
    initial = tuple((jnp.zeros(item.shape, jnp.float32) for item in params))
    sums, (outputs, text_grads, picture_grads) = lax.scan(advance, initial, (grouped(captions), grouped(images), grouped(lengths), grouped(out_grad)))
    layer_out = outputs.reshape(captions.shape)
    input_grad = text_grads.reshape(captions.shape)
    image_grad = picture_grads.reshape(images.shape)
    return (layer_out, input_grad, image_grad, sums[0], sums[1], sums[2], sums[3], sums[4], sums[5], sums[6], sums[7], sums[8], sums[9], sums[10], sums[11], sums[12])
```

```python
import functools

import jax
import jax.numpy as jnp
from jax import lax
from jax.experimental import pallas as pl
from jax.experimental.pallas import tpu as pltpu
from jax.sharding import PartitionSpec as P

HEADS = 12
NODES = 32
UNITS = 8
MESH = pl.DeviceIdType.MESH
F32 = jnp.float32
LOW = jnp.bfloat16
EPSILON = 1e-05
GELU_A = 0.7978845608028654
GELU_B = 0.044715

QS, KS, VS, SO, CK, CV, CQ, CO, UP = 0, 1, 2, 3, 4, 5, 6, 7, 8


def mm(left, right):
    return jnp.dot(left, right, preferred_element_type=F32)


def mm_bt(left, right):
    return lax.dot_general(left, right, (((1,), (1,)), ((), ())), preferred_element_type=F32)


def mm_at(left, right):
    return lax.dot_general(left, right, (((0,), (0,)), ((), ())), preferred_element_type=F32)


def norm(value, gain, shift):
    centred = value - jnp.mean(value, axis=-1, keepdims=True)
    rstd = lax.rsqrt(jnp.mean(centred * centred, axis=-1, keepdims=True) + EPSILON)
    hat = centred * rstd
    return hat, rstd, hat * gain + shift


def norm_pull(grad, hat, rstd, gain):
    scaled = grad * gain
    inner = jnp.mean(scaled * hat, axis=-1, keepdims=True)
    back = rstd * (scaled - jnp.mean(scaled, axis=-1, keepdims=True) - hat * inner)
    gain_grad = jnp.sum(grad * hat, axis=0, keepdims=True)
    shift_grad = jnp.sum(grad, axis=0, keepdims=True)
    return back, gain_grad, shift_grad


class Layer:
    def __init__(self, refs, lanes, narrow):
        self.__dict__.update(refs)
        self.N = narrow
        self.lanes = lanes
        wide, nar = lax.axis_index("wide"), lax.axis_index("narrow")
        flat = wide * narrow + nar
        self.wide, self.nar = wide, nar
        self.node = lax.div(flat, lanes)
        self.lane = lax.rem(flat, lanes)
        node = self.node
        self.c = lax.rem(node, 2)
        self.x = lax.rem(lax.div(node, 2), 2)
        self.y = lax.rem(lax.div(node, 4), 2)
        self.z = lax.div(node, 8)
        self.started = []
        self.count, self.seq = self.captions.shape[0] // 64, 64
        self.tokens, self.width = self.captions.shape
        self.groups = self.QA.shape[0]
        self.image_rows = self.images.shape[0] // self.groups
        self.pairs = self.width // 128
        lane = lax.broadcasted_iota(jnp.int32, (1, 128), 1)
        self.first = (lane < 64).astype(F32).astype(LOW)
        self.second = (lane >= 64).astype(F32).astype(LOW)
        self.is_first = lane < 64

    def device(self, z, y, x, c):
        flat = (z * 8 + y * 4 + x * 2 + c) * self.lanes + self.lane
        return (lax.div(flat, self.N), lax.rem(flat, self.N))

    def sibling(self):
        return self.device(self.z, self.y, self.x, 1 - self.c)

    def x_peer(self):
        return self.device(self.z, self.y, 1 - self.x, self.c)

    def y_peer(self):
        return self.device(self.z, 1 - self.y, self.x, self.c)

    def z_index(self, k):
        return lax.rem(self.z + k, 4)

    def z_peer(self, k):
        return self.device(self.z_index(k), self.y, self.x, self.c)

    def n_index(self, k):
        return lax.rem(self.nar + k, self.N)

    def n_peer(self, k):
        return (self.wide, self.n_index(k))

    def enter(self):
        barrier = pltpu.get_barrier_semaphore()
        peers = [self.sibling(), self.x_peer(), self.y_peer()]
        peers += [self.z_peer(k) for k in (1, 2, 3)]
        peers += [self.n_peer(k) for k in range(1, self.N)]
        for peer in peers:
            pl.semaphore_signal(barrier, inc=1, device_id=peer, device_id_type=MESH)
        pl.semaphore_wait(barrier, len(peers))

    def copy(self, src, dst, sems, where, peer):
        send, recv = sems
        return pltpu.make_async_remote_copy(
            src_ref=src,
            dst_ref=dst,
            send_sem=send.at[where],
            recv_sem=recv.at[where],
            device_id=peer,
            device_id_type=MESH,
        )

    def start(self, copies):
        for item in copies:
            item.start()
        self.started += copies

    def finish_sends(self):
        for item in self.started:
            item.wait_send()
        self.started = []

    def part(self, unit, half, z, y, x):
        if unit < 6:
            if half is None:
                return self.W.at[2 * unit + self.c, z, y, x]
            return self.W.at[2 * unit + self.c, z, y, x, :, pl.ds(384 * half, 384)]
        first = 96 * (unit - 6)
        if half is None:
            return self.HD.at[self.c, z, y, x, pl.ds(first, 96)]
        return self.HD.at[self.c, z, y, x, pl.ds(first + 48 * half, 48)]

    def pair_copies(self):
        c = self.c
        other = pl.ds(pl.multiple_of(384 * (1 - c), 128), 384)
        rows = pl.ds(pl.multiple_of(96 * c, 32), 96)
        return [
            self.copy(self.pack.at[1 - c], self.PAIR, self.s_pair, 0, self.sibling()),
            self.copy(
                self.down.at[:, other],
                self.HD.at[1 - c, self.z, self.y, self.x, rows],
                self.s_pair,
                1,
                self.sibling(),
            ),
        ]

    def pair_merge(self):
        c = self.c
        copies = self.pair_copies()
        own = pl.ds(pl.multiple_of(384 * c, 128), 384)
        rows = pl.ds(pl.multiple_of(96 * c, 32), 96)
        self.HD[c, self.z, self.y, self.x, rows] = self.down[:, own]
        copies[0].wait_recv()
        mine = self.pack[c].astype(F32)
        theirs = self.PAIR[...].astype(F32)
        even = c == 0
        low = jnp.where(even, mine, theirs)
        high = jnp.where(even, theirs, mine)
        for unit in range(6):
            rows = slice(24 * unit, 24 * unit + 24)
            both = jnp.concatenate([low[rows], high[rows]], axis=0).astype(LOW)
            self.W[2 * unit + c, self.z, self.y, self.x] = both
        copies[1].wait_recv()

    def z_copies(self, unit):
        here = self.part(unit, None, self.z, self.y, self.x)
        return [
            self.copy(here, here, self.s_z, (unit, k - 1), self.z_peer(k)) for k in (1, 2, 3)
        ]

    def two_copies(self, unit):
        every = slice(None)
        a = self.part(unit, 0, every, self.y, self.x)
        b = self.part(unit, 1, every, self.y, self.x)
        return [
            self.copy(a, a, self.s_two, (unit, 0), self.x_peer()),
            self.copy(b, b, self.s_two, (unit, 1), self.y_peer()),
        ]

    def three_copies(self, unit):
        every = slice(None)
        a = self.part(unit, 0, every, self.y, every)
        b = self.part(unit, 1, every, every, self.x)
        return [
            self.copy(a, a, self.s_three, (unit, 0), self.y_peer()),
            self.copy(b, b, self.s_three, (unit, 1), self.x_peer()),
        ]

    def hand_copies(self, unit):
        every = slice(None)
        whole = self.part(unit, None, every, every, every)
        return [self.copy(whole, whole, self.s_hand, unit, self.sibling())]

    def arrived(self, copies):
        for item in copies:
            item.wait_recv()

    def gather_tick(self, tick):
        if 0 <= tick < UNITS:
            self.arrived(self.z_copies(tick))
            self.start(self.two_copies(tick))
        if 0 <= tick - 1 < UNITS:
            self.arrived(self.two_copies(tick - 1))
            self.start(self.three_copies(tick - 1))
        if 0 <= tick - 2 < UNITS:
            self.arrived(self.three_copies(tick - 2))
            self.start(self.hand_copies(tick - 2))
        if 0 <= tick - 3 < UNITS:
            self.arrived(self.hand_copies(tick - 3))

    def rs_one_copies(self, unit):
        every = slice(None)
        a = self.part(unit, 0, every, 1 - self.y, every)
        b = self.part(unit, 1, every, every, 1 - self.x)
        return [
            self.copy(a, self.R1.at[unit, 0], self.s_rs1, (unit, 0), self.y_peer()),
            self.copy(b, self.R1.at[unit, 1], self.s_rs1, (unit, 1), self.x_peer()),
        ]

    def rs_two_copies(self, unit):
        every = slice(None)
        a = self.part(unit, 0, every, self.y, 1 - self.x)
        b = self.part(unit, 1, every, 1 - self.y, self.x)
        return [
            self.copy(a, self.R2.at[unit, 0], self.s_rs2, (unit, 0), self.x_peer()),
            self.copy(b, self.R2.at[unit, 1], self.s_rs2, (unit, 1), self.y_peer()),
        ]

    def rs_three_copies(self, unit):
        out = []
        for k in (1, 2, 3):
            here = self.part(unit, None, self.z_index(k), self.y, self.x)
            there = self.R3.at[unit, k - 1] if unit < 6 else self.R3H.at[unit - 6, k - 1]
            out.append(self.copy(here, there, self.s_rs3, (unit, k - 1), self.z_peer(k)))
        return out

    def rs_four_copies(self, unit):
        if unit < 6:
            block = 2 * unit + self.c
            return [
                self.copy(self.SF.at[unit], self.block_grad.at[block], self.s_rs4, unit, self.sibling())
            ]
        half = pl.ds(pl.multiple_of(384 * self.c, 128), 384)
        return [
            self.copy(self.SFH, self.down_out.at[:, half], self.s_rs4, unit, self.sibling())
        ]

    def add_into(self, ref, term):
        ref[...] = (ref[...].astype(F32) + term.astype(F32)).astype(LOW)

    def rs_one(self, unit):
        self.start(self.rs_one_copies(unit))

    def rs_two(self, unit):
        self.arrived(self.rs_one_copies(unit))

        @pl.loop(0, 4)
        def _(z):
            self.add_into(self.part(unit, 0, z, self.y, slice(None)), self.R1[unit, 0, z])
            self.add_into(self.part(unit, 1, z, slice(None), self.x), self.R1[unit, 1, z])

        self.start(self.rs_two_copies(unit))

    def rs_three(self, unit):
        self.arrived(self.rs_two_copies(unit))

        @pl.loop(0, 4)
        def _(z):
            self.add_into(self.part(unit, 0, z, self.y, self.x), self.R2[unit, 0, z])
            self.add_into(self.part(unit, 1, z, self.y, self.x), self.R2[unit, 1, z])

        self.start(self.rs_three_copies(unit))

    def rs_total(self, unit):
        self.arrived(self.rs_three_copies(unit))
        total = self.part(unit, None, self.z, self.y, self.x)[...].astype(F32)
        for k in range(3):
            more = self.R3[unit, k] if unit < 6 else self.R3H[unit - 6, k]
            total = total + more.astype(F32)
        return total

    def rs_four(self, unit):
        even = self.c == 0
        if unit < 6:
            total = self.rs_total(unit)
            low, high = total[:24], total[24:]
            self.block_grad[2 * unit + self.c] = jnp.where(even, low, high)
            self.SF[unit] = jnp.where(even, high, low)
            self.start(self.rs_four_copies(unit))
        if unit == 7:
            low, high = self.rs_total(6), self.rs_total(7)
            half = pl.ds(pl.multiple_of(384 * self.c, 128), 384)
            self.down_out[:, half] = jnp.where(even, low, high)
            self.SFH[...] = jnp.where(even, high, low)
            self.start(self.rs_four_copies(7))

    def rs_done(self, unit):
        if unit != 6:
            self.arrived(self.rs_four_copies(unit))

    def scatter_tick(self, order, tick):
        def at(back):
            place = tick - back
            return order[place] if 0 <= place < len(order) else None

        if at(0) is not None:
            self.rs_one(at(0))
        if at(1) is not None:
            self.rs_two(at(1))
        if at(2) is not None:
            self.rs_three(at(2))
        if at(3) is not None:
            self.rs_four(at(3))

    def sum_all(self, which, value):
        def copies(stage):
            peers = [[self.sibling()], [self.x_peer()], [self.y_peer()]]
            peers += [[self.z_peer(k) for k in (1, 2, 3)]]
            return [
                self.copy(
                    self.V.at[which, stage],
                    self.VR.at[which, stage + i],
                    self.s_vec,
                    (which, stage + i),
                    peer,
                )
                for i, peer in enumerate(peers[stage])
            ]

        for stage in range(4):
            self.V[which, stage] = value
            now = copies(stage)
            self.start(now)
            self.arrived(now)
            for i in range(len(now)):
                value = value + self.VR[which, stage + i]
        return value

    def keep_left(self, place, value):
        self.LHS[place, self.c] = value
        here = self.LHS.at[place, self.c]
        self.start([self.copy(here, here, self.s_left, place, self.sibling())])

    def keep_right(self, place, value):
        self.RHS[place, self.c] = value
        here = self.RHS.at[place, self.c]
        self.start([self.copy(here, here, self.s_right, place, self.sibling())])

    def left_arrived(self, place):
        here = self.LHS.at[place, self.c]
        self.copy(here, here, self.s_left, place, self.sibling()).wait_recv()

    def right_arrived(self, place):
        here = self.RHS.at[place, self.c]
        self.copy(here, here, self.s_right, place, self.sibling()).wait_recv()

    def weight(self, block):
        return self.W[block].reshape(self.width, self.width)

    def weight_grad(self, unit, left, right):
        c = self.c
        li = jnp.where(c == 0, left[0], left[1])
        ri = jnp.where(c == 0, right[0], right[1])
        right_all = self.RHS[ri].reshape(2 * self.tokens, self.width)
        for t in range(2):
            left_all = self.LHS[li, :, :, pl.ds(384 * t, 384)].reshape(2 * self.tokens, 384)
            part = mm_at(left_all, right_all).astype(LOW)
            self.W[2 * unit + c, pl.ds(2 * t, 2)] = part.reshape(2, 2, 2, 48, self.width)

    def down_grad(self):
        c = self.c
        half = pl.ds(pl.multiple_of(384 * c, 128), 384)
        right_all = self.RHS[10, :, :, half].reshape(2 * self.tokens, 384)
        for j in range(4):
            for t in range(2):
                left_all = self.LHS[5 + j, :, :, pl.ds(384 * t, 384)].reshape(2 * self.tokens, 384)
                part = mm_at(left_all, right_all).astype(LOW)
                self.HD[c, j, t] = part.reshape(2, 192, 384)

    def memory_copy(self):
        return self.copy(self.W.at[CV - self.c], self.CM, self.s_memory, 0, self.sibling())

    def memory_grad_other(self):
        c = self.c

        @pl.loop(0, 2)
        def _(t):
            left = self.images[:, pl.ds(pl.multiple_of(384 * t, 128), 384)]
            part = mm_at(left, self.KV[1 - c]).astype(LOW)
            self.W[CV - c, pl.ds(2 * t, 2)] = part.reshape(2, 2, 2, 48, self.width)

        self.start([self.memory_copy()])

    def memory_grad_own(self):
        c = self.c
        self.memory_copy().wait_recv()

        @pl.loop(0, 2)
        def _(t):
            left = self.images[:, pl.ds(pl.multiple_of(384 * t, 128), 384)]
            part = mm_at(left, self.KV[c]).reshape(2, 2, 2, 48, self.width)
            part = part + self.CM[pl.ds(2 * t, 2)].astype(F32)
            self.W[CK + c, pl.ds(2 * t, 2)] = part.astype(LOW)

    def masked(self, value):
        return value * self.first, value * self.second

    def self_attention(self):
        rows = lax.broadcasted_iota(jnp.int32, (128, 128), 0)
        cols = lax.broadcasted_iota(jnp.int32, (128, 128), 1)
        length = jnp.where(cols < 64, self.lengths[0], self.lengths[1])
        allowed = (lax.div(rows, 64) == lax.div(cols, 64)) & (cols <= rows)
        allowed = allowed & (lax.rem(cols, 64) < length)
        parts = []
        for p in range(self.pairs):
            at = slice(128 * p, 128 * p + 128)
            q, k, v = self.QKV[0, :, at], self.QKV[1, :, at], self.QKV[2, :, at]
            total = None
            for h, (qm, vm) in enumerate(zip(self.masked(q), self.masked(v))):
                s = mm_bt(qm, k) * 0.125
                s = jnp.where(allowed, s, -1000000000.0)
                e = jnp.exp(s - jnp.max(s, axis=-1, keepdims=True))
                prob = e / jnp.sum(e, axis=-1, keepdims=True)
                self.PS[2 * p + h] = prob
                out = mm(prob.astype(LOW), vm)
                total = out if total is None else total + out
            parts.append(total.astype(LOW))
        return jnp.concatenate(parts, axis=1)

    def self_attention_back(self, grad):
        parts = ([], [], [])
        for p in range(self.pairs):
            at = slice(128 * p, 128 * p + 128)
            q, k, v = self.QKV[0, :, at], self.QKV[1, :, at], self.QKV[2, :, at]
            g = grad[:, at]
            dq = dk = dv = 0.0
            for h, (qm, km, gm) in enumerate(
                zip(self.masked(q), self.masked(k), self.masked(g))
            ):
                prob = self.PS[2 * p + h]
                dp = mm_bt(gm, v)
                ds = prob * (dp - jnp.sum(prob * dp, axis=-1, keepdims=True))
                ds = ds.astype(LOW)
                dq = dq + mm(ds, km)
                dk = dk + mm_at(ds, qm)
                dv = dv + mm_at(prob.astype(LOW), gm)
            for out, item in zip(parts, (dq * 0.125, dk * 0.125, dv)):
                out.append(item.astype(LOW))
        return [jnp.concatenate(item, axis=1) for item in parts]

    def stacked(self, value):
        a, b = self.masked(value)
        return jnp.concatenate([a, b], axis=0)

    def diagonal(self, value):
        return jnp.where(self.is_first, value[:64], value[64:])

    def memory_forward(self, which):
        w = self.weight(CK + which)

        @pl.loop(0, 3)
        def _(t):
            size = self.images.shape[0] // 3
            rows = pl.ds(pl.multiple_of(size * t, 16), size)
            self.KV[which, rows] = mm(self.images[rows], w).astype(LOW)

    def cross_forward(self, place):
        rows = pl.ds(pl.multiple_of(place * self.image_rows, 16), self.image_rows)
        for p in range(self.pairs):
            at = slice(128 * p, 128 * p + 128)
            k, v = self.KV[0, rows, at], self.KV[1, rows, at]
            q = self.stacked(self.QA[place, :, at])
            s = mm_bt(k, q) * 0.125
            top = jnp.max(s, axis=0, keepdims=True)
            e = jnp.exp(s - top)
            self.E[place, p] = e
            self.ST[place, p : p + 1] = jnp.sum(e, axis=0, keepdims=True)
            self.ST[place, 8 + p : 9 + p] = top
            num = mm_at(e.astype(LOW), v)
            self.NUM[place, :, at] = self.diagonal(num).astype(LOW)
        self.ST[place, 6:8] = jnp.ones((2, 128), F32)
        self.ST[place, 14:16] = jnp.zeros((2, 128), F32)

    def cross_backward(self, place):
        rows = pl.ds(pl.multiple_of(place * self.image_rows, 16), self.image_rows)
        for p in range(self.pairs):
            at = slice(128 * p, 128 * p + 128)
            k, v = self.KV[0, rows, at], self.KV[1, rows, at]
            q = self.stacked(self.QA[place, :, at])
            g = self.stacked(self.GA[place, :, at])
            e = self.E[place, p]
            ds = e * (mm_bt(v, g) + self.DL[place, p : p + 1])
            ds = ds.astype(LOW)
            dq = mm_at(ds, k)
            self.NUM[place, :, at] = (self.diagonal(dq) * 0.125).astype(LOW)
            self.KV[0, rows, at] = (mm(ds, q) * 0.125).astype(LOW)
            self.KV[1, rows, at] = mm(e.astype(LOW), g).astype(LOW)

    def own(self, k=0):
        return pl.ds(self.n_index(k) * self.count, self.count)

    def query_copies(self):
        here = self.QA.at[self.own()]
        return [self.copy(here, here, self.s_query, k - 1, self.n_peer(k)) for k in range(1, self.N)]

    def number_copies(self, k):
        return [
            self.copy(
                self.NUM.at[self.own(k)], self.NUMR.at[self.N - k], self.s_num, k - 1, self.n_peer(k)
            ),
            self.copy(
                self.ST.at[self.own(k)], self.STR.at[self.N - k], self.s_st, k - 1, self.n_peer(k)
            ),
        ]

    def grad_copies(self, k):
        return [
            self.copy(
                self.GS.at[k], self.GA.at[self.own()], self.s_g, k - 1, self.n_peer(k)
            ),
            self.copy(
                self.DS.at[k], self.DL.at[self.own()], self.s_dl, k - 1, self.n_peer(k)
            ),
        ]

    def back_copies(self, k):
        return [
            self.copy(self.NUM.at[self.own(k)], self.NUMR.at[k], self.s_dq, k - 1, self.n_peer(k))
        ]

    def column(self, turned, p):
        return jnp.where(self.is_first, turned[:64, p : p + 1], turned[64:, p : p + 1])

    def combine(self):
        self.NUMR[0] = self.NUM[self.own()]
        self.STR[0] = self.ST[self.own()]
        done = []
        for j in range(self.count):
            totals = [self.STR[k, j, :8] for k in range(self.N)]
            tops = [self.STR[k, j, 8:] for k in range(self.N)]
            top = functools.reduce(jnp.maximum, tops)
            shares = [jnp.exp(item - top) for item in tops]
            total = sum(a * b for a, b in zip(shares, totals))
            turned = []
            for k in range(self.N):
                scale = shares[k] / total
                self.SCR[k, j] = scale
                wide = jnp.concatenate([scale, jnp.zeros((120, 128), F32)], axis=0)
                turned.append(wide.T)
                self.SCT[k, j] = turned[k]
            parts = []
            for p in range(self.pairs):
                at = slice(128 * p, 128 * p + 128)
                parts.append(
                    sum(
                        self.NUMR[k, j, :, at].astype(F32) * self.column(turned[k], p)
                        for k in range(self.N)
                    )
                )
            done.append(jnp.concatenate(parts, axis=1))
        return jnp.concatenate(done, axis=0)

    def spread_grad(self, doc):
        lane = lax.broadcasted_iota(jnp.int32, (128, 128), 1)
        for j in range(self.count):
            rows = slice(64 * j, 64 * j + 64)
            inner = jnp.zeros((128, 128), F32)
            for p in range(self.pairs):
                at = slice(128 * p, 128 * p + 128)
                part = doc[rows, at]
                prod = part * self.OCF[rows, at]
                a = jnp.sum(jnp.where(self.is_first, prod, 0.0), axis=1, keepdims=True)
                b = jnp.sum(jnp.where(self.is_first, 0.0, prod), axis=1, keepdims=True)
                inner = jnp.where(lane == p, jnp.concatenate([a, b], axis=0), inner)
                for k in range(self.N):
                    scale = self.column(self.SCT[k, j], p)
                    self.GS[k, j, :, at] = (part * scale).astype(LOW)
            inner = inner.T[:8]
            for k in range(self.N):
                self.DS[k, j] = -inner * self.SCR[k, j]

    def run(self):
        c = self.c
        tokens, width, count = self.tokens, self.width, self.count
        self.enter()
        self.start(self.pair_copies())
        self.keep_right(10, self.out_grad[...])
        vectors = self.sum_all(0, self.vec[...])
        gain1, shift1 = vectors[0:1], vectors[1:2]
        gain2, shift2 = vectors[2:3], vectors[3:4]
        gain3, shift3 = vectors[4:5], vectors[5:6]
        self.pair_merge()
        for unit in range(UNITS):
            self.start(self.z_copies(unit))
        for tick in range(UNITS + 3):
            self.gather_tick(tick)
        self.finish_sends()

        inputs = self.captions[...].astype(F32)
        hat1, rstd1, a1 = norm(inputs, gain1, shift1)
        self.HAT[0] = hat1
        a1 = a1.astype(LOW)
        self.keep_left(0, a1)
        for j in range(3):
            self.QKV[j] = mm(a1, self.weight(j)).astype(LOW)
        mixed = self.self_attention()
        self.keep_left(1, mixed)
        r1 = inputs + mm(mixed, self.weight(SO))
        hat2, rstd2, a2 = norm(r1, gain2, shift2)
        self.HAT[1] = hat2
        a2 = a2.astype(LOW)
        self.keep_left(2, a2)
        self.QA[self.own()] = mm(a2, self.weight(CQ)).astype(LOW).reshape(count, 64, width)
        queries = self.query_copies()
        self.start(queries)
        self.memory_forward(0)
        self.memory_forward(1)
        self.arrived(queries)
        pl.loop(0, self.groups)(self.cross_forward)
        for k in range(1, self.N):
            self.start(self.number_copies(k))
        for k in range(1, self.N):
            self.arrived(self.number_copies(k))
        full = self.combine()
        self.OCF[...] = full
        oc = full.astype(LOW)
        self.keep_left(3, oc)
        r2 = r1 + mm(oc, self.weight(CO))
        hat3, rstd3, a3 = norm(r2, gain3, shift3)
        self.HAT[2] = hat3
        a3 = a3.astype(LOW)
        self.keep_left(4, a3)
        out = [r2[:, :384], r2[:, 384:]]
        grad = self.out_grad[...]
        e3 = 0.0
        for j in range(4):
            hidden = mm(a3, self.weight(UP + j))
            square = hidden * hidden
            tanh = jnp.tanh(GELU_A * hidden * (1.0 + GELU_B * square))
            act = (0.5 * hidden * (1.0 + tanh)).astype(LOW)
            slope = 0.5 * (1.0 + tanh) + 0.5 * hidden * (1.0 - tanh * tanh) * (
                GELU_A * (1.0 + 3.0 * GELU_B * square)
            )
            self.keep_left(5 + j, act)
            down = [self.HD[i, j].reshape(width, 384) for i in range(2)]
            for i in range(2):
                out[i] = out[i] + mm(act, down[i])
            back = mm_bt(grad[:, :384], down[0]) + mm_bt(grad[:, 384:], down[1])
            dhp = (back * slope).astype(LOW)
            self.keep_right(6 + j, dhp)
            e3 = e3 + mm_bt(dhp, self.weight(UP + j))
        self.layer_out[...] = jnp.concatenate(out, axis=1).astype(LOW)

        order = [6, 7, 4, 5, 3, 2, 1, 0]
        back3, gain3_grad, shift3_grad = norm_pull(e3, self.HAT[2], rstd3, gain3)
        dr2 = grad.astype(F32) + back3
        dcat = dr2.astype(LOW)
        self.keep_right(5, dcat)
        self.spread_grad(mm_bt(dcat, self.weight(CO)))
        for k in range(1, self.N):
            self.start(self.grad_copies(k))
        self.GA[self.own()] = self.GS[0]
        self.DL[self.own()] = self.DS[0]
        for k in range(1, self.N):
            self.arrived(self.grad_copies(k))
        self.finish_sends()
        pl.loop(0, self.groups)(self.cross_backward)
        for k in range(1, self.N):
            self.start(self.back_copies(k))
        self.NUMR[0] = self.NUM[self.own()]
        for k in range(1, self.N):
            self.arrived(self.back_copies(k))
        dqc = sum(self.NUMR[k].astype(F32) for k in range(self.N))
        dqc = dqc.astype(LOW).reshape(tokens, width)
        self.keep_right(4, dqc)
        back2, gain2_grad, shift2_grad = norm_pull(
            mm_bt(dqc, self.weight(CQ)), self.HAT[1], rstd2, gain2
        )
        dr1 = dr2 + back2
        dattn = dr1.astype(LOW)
        self.keep_right(3, dattn)
        dos = mm_bt(dattn, self.weight(SO)).astype(LOW)
        e1 = 0.0
        for j, item in enumerate(self.self_attention_back(dos)):
            self.keep_right(j, item)
            e1 = e1 + mm_bt(item, self.weight(j))
        back1, gain1_grad, shift1_grad = norm_pull(e1, self.HAT[0], rstd1, gain1)
        self.input_grad[...] = (dr1 + back1).astype(LOW)

        @pl.loop(0, 3)
        def _(t):
            size = self.images.shape[0] // 3
            rows = pl.ds(pl.multiple_of(size * t, 16), size)
            part = mm_bt(self.KV[0, rows], self.weight(CK))
            part = part + mm_bt(self.KV[1, rows], self.weight(CV))
            self.image_grad[rows] = part.astype(LOW)

        grads = [gain1_grad, shift1_grad, gain2_grad, shift2_grad, gain3_grad, shift3_grad]
        grads = jnp.concatenate(grads + [jnp.zeros((2, width), F32)], axis=0)

        for place in range(9):
            self.left_arrived(place)
        for place in range(11):
            self.right_arrived(place)
        self.finish_sends()
        self.down_grad()
        self.weight_grad(4, (4, 4), (6, 7))
        self.weight_grad(5, (4, 4), (8, 9))
        self.weight_grad(3, (2, 3), (4, 5))
        self.memory_grad_other()
        self.memory_grad_own()
        self.weight_grad(1, (0, 1), (2, 3))
        self.weight_grad(0, (0, 0), (0, 1))
        for tick in range(UNITS + 3):
            self.scatter_tick(order, tick)
        self.vec_grad[...] = self.sum_all(1, grads)
        for unit in range(UNITS):
            self.rs_done(unit)
        self.finish_sends()


def layer_call(lanes, narrow, captions, images, lengths, out_grad, pack, down, vec):
    tokens, width = captions.shape
    count = tokens // 64
    groups = narrow * count
    image_rows = images.shape[0]
    pairs = width // 128
    ins = ["captions", "images", "lengths", "out_grad", "pack", "down", "vec"]
    outs = {
        "layer_out": ((tokens, width), LOW),
        "input_grad": ((tokens, width), LOW),
        "image_grad": ((image_rows, width), LOW),
        "block_grad": ((12, 24, width), F32),
        "down_out": ((96, width), F32),
        "vec_grad": ((8, width), F32),
    }
    memory = {
        "W": ((12, 4, 2, 2, 48, width), LOW),
        "HD": ((2, 4, 2, 2, 192, 384), LOW),
        "PAIR": ((144, width), LOW),
        "KV": ((2, image_rows, width), LOW),
        "E": ((groups, pairs, image_rows // groups, 128), F32),
        "LHS": ((9, 2, tokens, width), LOW),
        "RHS": ((11, 2, tokens, width), LOW),
        "R1": ((UNITS, 2, 4, 2, 48, 384), LOW),
        "R2": ((UNITS, 2, 4, 48, 384), LOW),
        "R3": ((6, 3, 48, width), LOW),
        "R3H": ((2, 3, 96, 384), LOW),
        "CM": ((4, 2, 2, 48, width), LOW),
        "SF": ((6, 24, width), F32),
        "SFH": ((96, 384), F32),
        "V": ((2, 4, 8, width), F32),
        "VR": ((2, 6, 8, width), F32),
        "QKV": ((3, tokens, width), LOW),
        "PS": ((HEADS, 128, 128), F32),
        "HAT": ((3, tokens, width), F32),
        "OCF": ((tokens, width), F32),
        "QA": ((groups, 64, width), LOW),
        "NUM": ((groups, 64, width), LOW),
        "ST": ((groups, 16, 128), F32),
        "NUMR": ((narrow, count, 64, width), LOW),
        "STR": ((narrow, count, 16, 128), F32),
        "SCR": ((narrow, count, 8, 128), F32),
        "SCT": ((narrow, count, 128, 128), F32),
        "GS": ((narrow, count, 64, width), LOW),
        "DS": ((narrow, count, 8, 128), F32),
        "GA": ((groups, 64, width), LOW),
        "DL": ((groups, 8, 128), F32),
    }
    signals = {
        "s_pair": (2,),
        "s_z": (UNITS, 3),
        "s_two": (UNITS, 2),
        "s_three": (UNITS, 2),
        "s_hand": (UNITS,),
        "s_rs1": (UNITS, 2),
        "s_rs2": (UNITS, 2),
        "s_rs3": (UNITS, 3),
        "s_rs4": (UNITS,),
        "s_vec": (2, 6),
        "s_left": (9,),
        "s_right": (11,),
        "s_memory": (1,),
        "s_query": (narrow - 1,),
        "s_num": (narrow - 1,),
        "s_st": (narrow - 1,),
        "s_g": (narrow - 1,),
        "s_dl": (narrow - 1,),
        "s_dq": (narrow - 1,),
    }
    scratch = [pltpu.VMEM(shape, kind) for shape, kind in memory.values()]
    for shape in signals.values():
        scratch += [pltpu.SemaphoreType.DMA(shape)] * 2

    def body(*refs):
        named = dict(zip(ins + list(outs) + list(memory), refs))
        rest = refs[len(named) :]
        for i, name in enumerate(signals):
            named[name] = (rest[2 * i], rest[2 * i + 1])
        Layer(named, lanes, narrow).run()

    vmem = pl.BlockSpec(memory_space=pltpu.VMEM)
    in_specs = [vmem] * len(ins)
    in_specs[2] = pl.BlockSpec(memory_space=pltpu.SMEM)
    return pl.pallas_call(
        body,
        out_shape=[jax.ShapeDtypeStruct(shape, kind) for shape, kind in outs.values()],
        in_specs=in_specs,
        out_specs=[vmem] * len(outs),
        scratch_shapes=scratch,
        compiler_params=pltpu.CompilerParams(
            collective_id=0, has_side_effects=True, vmem_limit_bytes=64 * 1024 * 1024 - 65536
        ),
        cost_estimate=pl.CostEstimate(
            flops=17 * 10**9, bytes_accessed=8 * 10**6, transcendentals=2 * 10**6
        ),
        name="layer",
    )(captions, images, lengths, out_grad, pack, down, vec)


def lane_gather(value, lanes, narrow, axis):
    if lanes == 1:
        return value
    assert lanes % narrow == 0
    value = lax.all_gather(value, "narrow", axis=axis, tiled=True)
    step = 1
    wide_count = lax.axis_size("wide")
    while step * narrow < lanes:
        swap = [(i, i ^ step) for i in range(wide_count)]
        other = lax.ppermute(value, "wide", swap)
        low = (lax.axis_index("wide") // step) % 2 == 0
        first = jnp.where(low, value, other)
        second = jnp.where(low, other, value)
        value = jnp.concatenate([first, second], axis=axis)
        step *= 2
    return value


def lane_scatter(value, lanes, narrow, axis):
    if lanes == 1:
        return value
    wide_count = lax.axis_size("wide")
    step = lanes // narrow
    while step > 1:
        step //= 2
        swap = [(i, i ^ step) for i in range(wide_count)]
        first, second = jnp.split(value, 2, axis=axis)
        low = (lax.axis_index("wide") // step) % 2 == 0
        other = lax.ppermute(jnp.where(low, second, first), "wide", swap)
        value = jnp.where(low, first, second) + other
    return lax.psum_scatter(value, "narrow", scatter_dimension=axis, tiled=True)


def per_device(captions, images, lengths, out_grad, *params):
    narrow = lax.axis_size("narrow")
    devices = lax.axis_size("wide") * narrow
    lanes = devices // NODES
    count, seq_len, width = captions.shape
    tokens = count * seq_len
    flat = lax.axis_index("wide") * narrow + lax.axis_index("narrow")
    params = [lane_gather(item, lanes, narrow, 0) for item in params]
    joint, self_out, query, memory, cross, up, down = params[:7]
    blocks = [joint[:, width * j : width * (j + 1)] for j in range(3)] + [self_out]
    blocks += [memory[:, :width], memory[:, width:], query, cross]
    blocks += [up[:, width * j : width * (j + 1)] for j in range(4)]
    pack = jnp.stack([jnp.concatenate(blocks[i::2], axis=0) for i in range(2)])
    own = width // NODES
    start = lax.div(flat, lanes) * own
    vec = jnp.zeros((8, width), F32)
    vec = lax.dynamic_update_slice(vec, jnp.stack(params[7:]).astype(F32), (0, start))
    out, input_grad, image_grad, block_grad, down_grad, vec_grad = layer_call(
        lanes,
        narrow,
        captions.reshape(tokens, width),
        images.reshape(-1, width),
        lengths,
        out_grad.reshape(tokens, width),
        pack,
        down,
        vec,
    )
    vec_own = lax.dynamic_slice(vec_grad, (0, start), (6, own))
    block_grad = lane_scatter(block_grad, lanes, narrow, 1)
    down_grad = lane_scatter(down_grad, lanes, narrow, 0)
    vec_own = lane_scatter(vec_own, lanes, narrow, 1)

    def columns(*places):
        return jnp.concatenate([block_grad[i] for i in places], axis=1)

    return (
        out.reshape(captions.shape),
        input_grad.reshape(captions.shape),
        image_grad.reshape(images.shape),
        columns(QS, KS, VS),
        block_grad[SO],
        block_grad[CQ],
        columns(CK, CV),
        block_grad[CO],
        columns(UP, UP + 1, UP + 2, UP + 3),
        down_grad,
        *[vec_own[i] for i in range(6)],
    )


def solution(mesh):
    both = ("wide", "narrow")
    rows = P(both, None)
    text = P(both, None, None)
    vector = P(both)
    image = P("wide", "narrow", None)
    in_specs = (text, image, vector, text) + (rows,) * 7 + (vector,) * 6
    out_specs = (text, text, image) + (rows,) * 7 + (vector,) * 6
    return jax.shard_map(
        per_device, mesh=mesh, in_specs=in_specs, out_specs=out_specs, check_vma=False
    )
```

```python
import functools

import jax
import jax.numpy as jnp
from jax import lax
from jax.experimental import pallas as pl
from jax.experimental.pallas import tpu as pltpu
from jax.sharding import PartitionSpec as P

HEADS = 12
NODES = 32
UNITS = 11
MESH = pl.DeviceIdType.MESH
F32 = jnp.float32
LOW = jnp.bfloat16
EPSILON = 1e-05
GELU_A = 0.7978845608028654
GELU_B = 0.044715

QS, KS, VS, SO, CK, CV, CQ, CO, UP = 0, 1, 2, 3, 4, 5, 6, 7, 8
DOWN = UP + 1
GATHER = (256,) * 8
SCATTER = (256, 128, 256, 128, 256, 128, 256, 128)


def mm(left, right):
    return jnp.dot(left, right, preferred_element_type=F32)


def mm_bt(left, right):
    return lax.dot_general(left, right, (((1,), (1,)), ((), ())), preferred_element_type=F32)


def mm_at(left, right):
    return lax.dot_general(left, right, (((0,), (0,)), ((), ())), preferred_element_type=F32)


def norm(value, gain, shift):
    centred = value - jnp.mean(value, axis=-1, keepdims=True)
    rstd = lax.rsqrt(jnp.mean(centred * centred, axis=-1, keepdims=True) + EPSILON)
    hat = centred * rstd
    return hat, rstd, hat * gain + shift


def norm_pull(grad, hat, rstd, gain):
    scaled = grad * gain
    inner = jnp.mean(scaled * hat, axis=-1, keepdims=True)
    back = rstd * (scaled - jnp.mean(scaled, axis=-1, keepdims=True) - hat * inner)
    gain_grad = jnp.sum(grad * hat, axis=0, keepdims=True)
    shift_grad = jnp.sum(grad, axis=0, keepdims=True)
    return back, gain_grad, shift_grad


class Layer:
    def __init__(self, refs, lanes, narrow):
        self.__dict__.update(refs)
        self.N = narrow
        self.lanes = lanes
        wide, nar = lax.axis_index("wide"), lax.axis_index("narrow")
        flat = wide * narrow + nar
        self.wide, self.nar = wide, nar
        self.node = lax.div(flat, lanes)
        self.lane = lax.rem(flat, lanes)
        node = self.node
        self.c = lax.rem(node, 2)
        self.x = lax.rem(lax.div(node, 2), 2)
        self.y = lax.rem(lax.div(node, 4), 2)
        self.z = lax.div(node, 8)
        self.started = []
        self.count, self.seq = self.captions.shape[0] // 64, 64
        self.tokens, self.width = self.captions.shape
        self.groups = self.QA.shape[0]
        self.image_rows = self.images.shape[0] // self.groups
        self.pairs = self.width // 128
        lane = lax.broadcasted_iota(jnp.int32, (1, 128), 1)
        self.low_lanes = (lane < 64).astype(F32).astype(LOW)
        self.high_lanes = (lane >= 64).astype(F32).astype(LOW)
        self.is_first = lane < 64

    def device(self, z, y, x, c):
        flat = (z * 8 + y * 4 + x * 2 + c) * self.lanes + self.lane
        return (lax.div(flat, self.N), lax.rem(flat, self.N))

    def sibling(self):
        return self.device(self.z, self.y, self.x, 1 - self.c)

    def x_peer(self):
        return self.device(self.z, self.y, 1 - self.x, self.c)

    def y_peer(self):
        return self.device(self.z, 1 - self.y, self.x, self.c)

    def z_index(self, k):
        return lax.rem(self.z + k, 4)

    def z_peer(self, k):
        return self.device(self.z_index(k), self.y, self.x, self.c)

    def n_index(self, k):
        return lax.rem(self.nar + k, self.N)

    def n_peer(self, k):
        return (self.wide, self.n_index(k))

    def enter(self):
        barrier = pltpu.get_barrier_semaphore()
        peers = [self.sibling(), self.x_peer(), self.y_peer()]
        peers += [self.z_peer(k) for k in (1, 2, 3)]
        peers += [self.n_peer(k) for k in range(1, self.N)]
        for peer in peers:
            pl.semaphore_signal(barrier, inc=1, device_id=peer, device_id_type=MESH)
        pl.semaphore_wait(barrier, len(peers))

    def copy(self, src, dst, sems, where, peer):
        send, recv = sems
        return pltpu.make_async_remote_copy(
            src_ref=src,
            dst_ref=dst,
            send_sem=send.at[where],
            recv_sem=recv.at[where],
            device_id=peer,
            device_id_type=MESH,
        )

    def start(self, copies):
        for item in copies:
            item.start()
        self.started += copies

    def finish_sends(self):
        for item in self.started:
            item.wait_send()
        self.started = []

    def finish_early(self):
        for item in self.started[: self.gathered]:
            item.wait_send()
        self.started = self.started[self.gathered :]

    def part(self, unit, half, z, y, x, grad=False):
        every = slice(None)
        if unit < UP:
            first = (SCATTER if grad else GATHER)[unit]
            low, size = ((0, 384), (0, first), (first, 384 - first))[0 if half is None else half + 1]
            if grad and unit in (CK, CV):
                return self.CP.at[unit - CK, z, y, x, every, pl.ds(low, size)]
            columns = pl.ds(pl.multiple_of(384 * self.c + low, 128), size)
            return self.W.at[unit, z, y, x, every, columns]
        if unit == UP:
            return self.W.at[UP + self.c, z, y, x]
        ref = self.HG if grad else self.HD.at[self.c]
        return ref.at[z, x, pl.ds(96 * (unit - DOWN), 96)]

    def half_columns(self, c):
        return pl.ds(pl.multiple_of(384 * c, 128), 384)

    def shards(self):
        found = [(self.self_proj, self.width * j) for j in range(3)] + [(self.self_output, 0)]
        found += [(self.cross_memory, self.width * j) for j in range(2)]
        return found + [(self.cross_query, 0), (self.cross_output, 0)]

    def half_block(self, block, c):
        ref, start = self.shards()[block]
        return ref[:, pl.ds(pl.multiple_of(start + 384 * c, 128), 384)].astype(F32)

    def up_block(self, y, c):
        runs = []
        for j in range(2):
            start = self.width * (2 * c + j) + 384 * y
            runs.append(self.hidden_up[:, pl.ds(pl.multiple_of(start, 128), 384)].astype(F32))
        return jnp.concatenate(runs, axis=1)

    def pair_copies(self):
        c = self.c
        rows = pl.ds(pl.multiple_of(96 * c, 32), 96)
        there = self.HD.at[1 - c, self.z, self.x, rows]
        down = self.hidden_down.at[:, self.half_columns(1 - c)]
        return [
            self.copy(self.PA.at[0], self.PA.at[1], self.s_pair, 0, self.sibling()),
            self.copy(self.PB.at[0], self.PB.at[1], self.s_pair, 1, self.sibling()),
            self.copy(down, there, self.s_pair, 2, self.sibling()),
        ]

    def pair_pack(self):
        c = 1 - self.c
        blocks = [self.half_block(block, c) for block in range(UP)]
        self.PA[0] = jnp.concatenate(blocks, axis=0).astype(LOW)
        both = [self.up_block(y, c) for y in range(2)]
        self.PB[0] = jnp.concatenate(both, axis=0).astype(LOW)

    def in_order(self, mine, theirs):
        even = self.c == 0
        low, high = jnp.where(even, mine, theirs), jnp.where(even, theirs, mine)
        return jnp.concatenate([low, high], axis=0)

    def pair_merge(self):
        c = self.c
        copies = self.pair_copies()
        rows = pl.ds(pl.multiple_of(96 * c, 32), 96)
        self.HD[c, self.z, self.x, rows] = self.hidden_down[:, self.half_columns(c)]
        columns = pl.ds(pl.multiple_of(384 * c, 128), 384)
        copies[0].wait_recv()
        theirs = self.PA[1].astype(F32)
        for block in range(UP):
            both = self.in_order(self.half_block(block, c), theirs[24 * block : 24 * block + 24])
            self.W[block, self.z, self.y, self.x, :, columns] = both.astype(LOW)
        copies[1].wait_recv()
        theirs = self.PB[1].astype(F32)
        both = [self.in_order(self.up_block(y, c), theirs[24 * y : 24 * y + 24]) for y in range(2)]
        south = self.y == 0
        self.W[UP + c, self.z, self.y, self.x] = jnp.where(south, both[0], both[1]).astype(LOW)
        self.UPS[...] = jnp.where(south, both[1], both[0]).astype(LOW)
        copies[2].wait_recv()

    def up_copies(self):
        there = self.W.at[UP + self.c, self.z, self.y, self.x]
        return [self.copy(self.UPS, there, self.s_up, 0, self.y_peer())]

    def z_copies(self, unit):
        y = slice(None) if unit == UP else self.y
        here = self.part(unit, None, self.z, y, self.x)
        return [
            self.copy(here, here, self.s_z, (unit, k - 1), self.z_peer(k)) for k in (1, 2, 3)
        ]

    def two_copies(self, unit):
        every = slice(None)
        a = self.part(unit, 0, every, self.y, self.x)
        b = self.part(unit, 1, every, self.y, self.x)
        return [
            self.copy(a, a, self.s_two, (unit, 0), self.x_peer()),
            self.copy(b, b, self.s_two, (unit, 1), self.y_peer()),
        ]

    def three_copies(self, unit):
        every = slice(None)
        if unit >= UP:
            here = self.part(unit, None, every, every, self.x)
            return [self.copy(here, here, self.s_three, (unit, 0), self.x_peer())]
        a = self.part(unit, 0, every, self.y, every)
        b = self.part(unit, 1, every, every, self.x)
        return [
            self.copy(a, a, self.s_three, (unit, 0), self.y_peer()),
            self.copy(b, b, self.s_three, (unit, 1), self.x_peer()),
        ]

    def hand_copies(self, unit):
        every = slice(None)
        whole = self.part(unit, None, every, every, every)
        return [self.copy(whole, whole, self.s_hand, unit, self.sibling())]

    def arrived(self, copies):
        for item in copies:
            item.wait_recv()

    def first(self, unit):
        self.start(self.z_copies(unit))

    def second(self, unit):
        self.arrived(self.z_copies(unit))
        if unit < UP:
            self.start(self.two_copies(unit))

    def third(self, unit):
        if unit < UP:
            self.arrived(self.two_copies(unit))
        self.start(self.three_copies(unit))

    def hand(self, unit):
        self.arrived(self.three_copies(unit))
        self.start(self.hand_copies(unit))

    def done(self, unit):
        self.arrived(self.hand_copies(unit))

    def term(self, unit, half, z=slice(None)):
        first = SCATTER[unit]
        return (unit, z, ..., pl.ds(*((0, first), (first, 384 - first))[half]))

    def rs_one_copies(self, unit):
        every = slice(None)
        if unit >= UP:
            here = self.part(unit, None, every, every, 1 - self.x, grad=True)
            there = self.RU1 if unit == UP else self.RH1.at[unit - DOWN]
            return [self.copy(here, there, self.s_rs1, (unit, 0), self.x_peer())]
        a = self.part(unit, 0, every, 1 - self.y, every, grad=True)
        b = self.part(unit, 1, every, every, 1 - self.x, grad=True)
        return [
            self.copy(a, self.R1.at[self.term(unit, 0)], self.s_rs1, (unit, 0), self.y_peer()),
            self.copy(b, self.R1.at[self.term(unit, 1)], self.s_rs1, (unit, 1), self.x_peer()),
        ]

    def rs_two_copies(self, unit):
        every = slice(None)
        a = self.part(unit, 0, every, self.y, 1 - self.x, grad=True)
        b = self.part(unit, 1, every, 1 - self.y, self.x, grad=True)
        return [
            self.copy(a, self.R2.at[self.term(unit, 0)], self.s_rs2, (unit, 0), self.x_peer()),
            self.copy(b, self.R2.at[self.term(unit, 1)], self.s_rs2, (unit, 1), self.y_peer()),
        ]

    def rs_three_copies(self, unit):
        out = []
        y = slice(None) if unit == UP else self.y
        for k in (1, 2, 3):
            here = self.part(unit, None, self.z_index(k), y, self.x, grad=True)
            if unit < UP:
                there = self.R3.at[unit, k - 1]
            elif unit == UP:
                there = self.RU3.at[k - 1]
            else:
                there = self.RH3.at[unit - DOWN, k - 1]
            out.append(self.copy(here, there, self.s_rs3, (unit, k - 1), self.z_peer(k)))
        return out

    def up_back_copies(self):
        return [self.copy(self.UPS, self.UPR, self.s_up, 1, self.y_peer())]

    def grad_columns(self, block):
        return pl.ds(pl.multiple_of(self.width * block + 384 * self.c, 128), 384)

    def rs_four_copies(self, unit):
        c = self.c
        if unit < UP:
            there = self.block_grad.at[:, self.grad_columns(unit)]
            return [self.copy(self.SF.at[unit], there, self.s_rs4, unit, self.sibling())]
        if unit == UP:
            out = []
            for i in range(2):
                for h in range(2):
                    there = self.block_grad.at[:, self.up_columns(i, h)]
                    here = self.SFU.at[i, :, pl.ds(384 * h, 384)]
                    out.append(self.copy(here, there, self.s_rs5, (i, h), self.sibling()))
            return out
        there = self.down_out.at[:, self.half_columns(c)]
        return [self.copy(self.SFH, there, self.s_rs4, unit, self.sibling())]

    def up_columns(self, i, h):
        y = self.y if i == 0 else 1 - self.y
        start = self.width * (UP + 2 * self.c + h) + 384 * y
        return pl.ds(pl.multiple_of(start, 128), 384)

    def add_into(self, ref, term):
        ref[...] = (ref[...].astype(F32) + term.astype(F32)).astype(LOW)

    def rs_one(self, unit):
        self.start(self.rs_one_copies(unit))

    def rs_two(self, unit):
        self.arrived(self.rs_one_copies(unit))
        every = slice(None)

        @pl.loop(0, 4)
        def _(z):
            if unit < UP:
                a, b = self.R1[self.term(unit, 0, z)], self.R1[self.term(unit, 1, z)]
                self.add_into(self.part(unit, 0, z, self.y, every, grad=True), a)
                self.add_into(self.part(unit, 1, z, every, self.x, grad=True), b)
            else:
                more = self.RU1[z] if unit == UP else self.RH1[unit - DOWN, z]
                self.add_into(self.part(unit, None, z, every, self.x, grad=True), more)

        if unit < UP:
            self.start(self.rs_two_copies(unit))
        else:
            self.start(self.rs_three_copies(unit))

    def rs_three(self, unit):
        self.arrived(self.rs_two_copies(unit))

        @pl.loop(0, 4)
        def _(z):
            a, b = self.R2[self.term(unit, 0, z)], self.R2[self.term(unit, 1, z)]
            self.add_into(self.part(unit, 0, z, self.y, self.x, grad=True), a)
            self.add_into(self.part(unit, 1, z, self.y, self.x, grad=True), b)

        self.start(self.rs_three_copies(unit))

    def rs_total(self, unit):
        self.arrived(self.rs_three_copies(unit))
        y = slice(None) if unit == UP else self.y
        total = self.part(unit, None, self.z, y, self.x, grad=True)[...].astype(F32)
        for k in range(3):
            if unit < UP:
                more = self.R3[unit, k]
            else:
                more = self.RU3[k] if unit == UP else self.RH3[unit - DOWN, k]
            total = total + more.astype(F32)
        return total

    def rs_four(self, unit):
        even = self.c == 0
        if unit < UP:
            total = self.rs_total(unit)
            low, high = total[:24], total[24:]
            self.block_grad[:, self.grad_columns(unit)] = jnp.where(even, low, high)
            self.SF[unit] = jnp.where(even, high, low)
            self.start(self.rs_four_copies(unit))
        if unit == UP:
            total = self.rs_total(unit)
            south = self.y == 0
            self.UPS[...] = jnp.where(south, total[1], total[0]).astype(LOW)
            self.start(self.up_back_copies())
            self.up_rows(0, jnp.where(south, total[0], total[1]))
        if unit == DOWN + 1:
            low, high = self.rs_total(DOWN), self.rs_total(DOWN + 1)
            self.down_out[:, self.half_columns(self.c)] = jnp.where(even, low, high)
            self.SFH[...] = jnp.where(even, high, low)
            self.start(self.rs_four_copies(DOWN + 1))

    def up_rows(self, i, total):
        even = self.c == 0
        low, high = total[:24], total[24:]
        own = jnp.where(even, low, high)
        for h in range(2):
            self.block_grad[:, self.up_columns(i, h)] = own[:, 384 * h : 384 * h + 384]
        self.SFU[i] = jnp.where(even, high, low)

    def rs_up(self):
        self.arrived(self.up_back_copies())
        self.up_rows(1, self.UPR[...].astype(F32))
        self.start(self.rs_four_copies(UP))

    def rs_done(self, unit):
        if unit != DOWN:
            self.arrived(self.rs_four_copies(unit))

    def sum_copies(self, which, stage):
        peers = [[self.sibling()], [self.x_peer()], [self.y_peer()]]
        peers += [[self.z_peer(k) for k in (1, 2, 3)]]
        return [
            self.copy(
                self.V.at[which, stage],
                self.VR.at[which, stage + i],
                self.s_vec,
                (which, stage + i),
                peer,
            )
            for i, peer in enumerate(peers[stage])
        ]

    def placement(self, dtype):
        own = self.width // NODES
        at = lax.broadcasted_iota(jnp.int32, (128, self.width), 0)
        feature = lax.broadcasted_iota(jnp.int32, (128, self.width), 1)
        return ((at < own) & (feature == at + own * self.node)).astype(F32).astype(dtype)

    def sum_start(self, which, stage, value):
        self.V[which, stage] = value
        self.start(self.sum_copies(which, stage))

    def sum_end(self, which, stage):
        now = self.sum_copies(which, stage)
        self.arrived(now)
        value = self.V[which, stage]
        for i in range(len(now)):
            value = value + self.VR[which, stage + i]
        return value

    def keep_left(self, place, value):
        self.LHS[place, self.c] = value
        here = self.LHS.at[place, self.c]
        self.start([self.copy(here, here, self.s_left, place, self.sibling())])

    def keep_right(self, place, value):
        self.RHS[place, self.c] = value
        here = self.RHS.at[place, self.c]
        self.start([self.copy(here, here, self.s_right, place, self.sibling())])

    def left_arrived(self, place):
        here = self.LHS.at[place, self.c]
        self.copy(here, here, self.s_left, place, self.sibling()).wait_recv()

    def right_arrived(self, place):
        here = self.RHS.at[place, self.c]
        self.copy(here, here, self.s_right, place, self.sibling()).wait_recv()

    def weight(self, block):
        return self.W[block].reshape(self.width, self.width)

    def weight_grad(self, unit):
        left, right = {QS: (0, 0), KS: (0, 1), VS: (0, 2), SO: (1, 3), CQ: (2, 4), CO: (3, 5)}[unit]
        columns = self.half_columns(self.c)
        right_all = self.RHS[right, :, :, columns].reshape(2 * self.tokens, 384)
        for t in range(2):
            left_all = self.LHS[left, :, :, pl.ds(384 * t, 384)].reshape(2 * self.tokens, 384)
            part = mm_at(left_all, right_all).astype(LOW)
            self.W[unit, pl.ds(2 * t, 2), :, :, :, columns] = part.reshape(2, 2, 2, 48, 384)

    def up_grad(self):
        c = self.c
        right_all = self.DH[c].reshape(4 * self.tokens, self.width)
        for t in range(2):
            left_all = self.A3[:, :, :, pl.ds(384 * t, 384)].reshape(4 * self.tokens, 384)
            part = mm_at(left_all, right_all).astype(LOW)
            self.W[UP + c, pl.ds(2 * t, 2)] = part.reshape(2, 2, 2, 48, self.width)

    def down_grad(self):
        right_all = self.G4[:, :, :, self.half_columns(self.c)].reshape(4 * self.tokens, 384)
        for z in range(4):
            j, t = z // 2, z % 2
            left_all = self.U[j, :, :, :, pl.ds(384 * t, 384)].reshape(4 * self.tokens, 384)
            part = mm_at(left_all, right_all).astype(LOW)
            self.HG[z] = part.reshape(2, 192, 384)

    def memory_copy(self, which):
        return self.copy(
            self.CS.at[which], self.CM.at[which], self.s_memory, which, self.sibling()
        )

    def memory_term(self, which, c, t):
        left = self.IMG[:, pl.ds(384 * t, 384)]
        part = mm_at(left, self.KV[which, :, self.half_columns(c)])
        return part.reshape(2, 2, 2, 48, 384)

    def memory_grad_other(self, which):
        for t in range(2):
            part = self.memory_term(which, 1 - self.c, t)
            self.CS[which, pl.ds(2 * t, 2)] = part.astype(LOW)
        self.start([self.memory_copy(which)])

    def memory_grad_own(self, which):
        self.memory_copy(which).wait_recv()
        for t in range(2):
            part = self.memory_term(which, self.c, t)
            part = part + self.CM[which, pl.ds(2 * t, 2)].astype(F32)
            self.CP[which, pl.ds(2 * t, 2)] = part.astype(LOW)

    def masked(self, value):
        return value * self.low_lanes, value * self.high_lanes

    def self_attention(self):
        rows = lax.broadcasted_iota(jnp.int32, (128, 128), 0)
        cols = lax.broadcasted_iota(jnp.int32, (128, 128), 1)
        length = jnp.where(cols < 64, self.lengths[0], self.lengths[1])
        allowed = (lax.div(rows, 64) == lax.div(cols, 64)) & (cols <= rows)
        allowed = allowed & (lax.rem(cols, 64) < length)
        parts = []
        for p in range(self.pairs):
            at = slice(128 * p, 128 * p + 128)
            q, k, v = self.QKV[0, :, at], self.QKV[1, :, at], self.QKV[2, :, at]
            total = None
            for h, (qm, vm) in enumerate(zip(self.masked(q), self.masked(v))):
                s = mm_bt(qm, k) * 0.125
                s = jnp.where(allowed, s, -1000000000.0)
                e = jnp.exp(s - jnp.max(s, axis=-1, keepdims=True))
                prob = e / jnp.sum(e, axis=-1, keepdims=True)
                self.PS[2 * p + h] = prob
                out = mm(prob.astype(LOW), vm)
                total = out if total is None else total + out
            parts.append(total.astype(LOW))
        return jnp.concatenate(parts, axis=1)

    def self_attention_back(self, grad):
        parts = ([], [], [])
        for p in range(self.pairs):
            at = slice(128 * p, 128 * p + 128)
            q, k, v = self.QKV[0, :, at], self.QKV[1, :, at], self.QKV[2, :, at]
            g = grad[:, at]
            dq = dk = dv = 0.0
            for h, (qm, km, gm) in enumerate(
                zip(self.masked(q), self.masked(k), self.masked(g))
            ):
                prob = self.PS[2 * p + h]
                dp = mm_bt(gm, v)
                ds = prob * (dp - jnp.sum(prob * dp, axis=-1, keepdims=True))
                ds = ds.astype(LOW)
                dq = dq + mm(ds, km)
                dk = dk + mm_at(ds, qm)
                dv = dv + mm_at(prob.astype(LOW), gm)
            for out, item in zip(parts, (dq * 0.125, dk * 0.125, dv)):
                out.append(item.astype(LOW))
        return [jnp.concatenate(item, axis=1) for item in parts]

    def stacked(self, value):
        a, b = self.masked(value)
        return jnp.concatenate([a, b], axis=0)

    def diagonal(self, value):
        return jnp.where(self.is_first, value[:64], value[64:])

    def memory_forward(self, which):
        w = self.weight(CK + which)

        @pl.loop(0, 3)
        def _(t):
            size = self.images.shape[0] // 3
            rows = pl.ds(pl.multiple_of(size * t, 16), size)
            self.KV[which, rows] = mm(self.IMG[rows], w).astype(LOW)

    def cross_forward(self, place):
        rows = pl.ds(pl.multiple_of(place * self.image_rows, 16), self.image_rows)
        for p in range(self.pairs):
            at = slice(128 * p, 128 * p + 128)
            k, v = self.KV[0, rows, at], self.KV[1, rows, at]
            q = self.stacked(self.QA[place, :, at])
            s = mm_bt(k, q) * 0.125
            top = jnp.max(s, axis=0, keepdims=True)
            e = jnp.exp(s - top)
            low = e.astype(LOW)
            self.E[place, p] = low
            self.ST[place, p : p + 1] = jnp.sum(e, axis=0, keepdims=True)
            self.ST[place, 8 + p : 9 + p] = top
            self.TOP[place, p : p + 1] = top
            num = mm_at(low, v)
            self.NUM[place, :, at] = self.diagonal(num).astype(LOW)
        self.ST[place, 6:8] = jnp.ones((2, 128), F32)
        self.ST[place, 14:16] = jnp.zeros((2, 128), F32)

    def cross_backward(self, place):
        rows = pl.ds(pl.multiple_of(place * self.image_rows, 16), self.image_rows)
        for p in range(self.pairs):
            at = slice(128 * p, 128 * p + 128)
            k, v = self.KV[0, rows, at], self.KV[1, rows, at]
            q = self.stacked(self.QA[place, :, at])
            g = self.stacked(self.GA[place, :, at])
            share = jnp.exp(self.TOP[place, p : p + 1] - self.DL[place, 8 + p : 9 + p])
            e = self.E[place, p].astype(F32) * share
            ds = e * (mm_bt(v, g) + self.DL[place, p : p + 1])
            ds = ds.astype(LOW)
            dq = mm_at(ds, k)
            self.NUM[place, :, at] = (self.diagonal(dq) * 0.125).astype(LOW)
            self.KV[0, rows, at] = (mm(ds, q) * 0.125).astype(LOW)
            self.KV[1, rows, at] = mm(e.astype(LOW), g).astype(LOW)

    def captions_of(self, owner):
        return pl.ds(owner * self.count, self.count)

    def partner(self, bit):
        return (self.wide, jnp.bitwise_xor(self.nar, bit))

    def owner(self, bits):
        return jnp.bitwise_xor(self.nar, bits)

    def share_copies(self, ref, sems, bit, bits):
        here = ref.at[self.captions_of(self.owner(bits))]
        return self.copy(here, here, sems, (self.N + bits) // (2 * bit) - 1, self.partner(bit))

    def share_steps(self):
        bit = self.N // 2
        while bit:
            yield bit, range(0, self.N, 2 * bit)
            bit //= 2

    def share_start(self, refs):
        for bit, held in self.share_steps():
            self.start([self.share_copies(ref, sems, bit, 0) for ref, sems in refs])

    def share_end(self, refs):
        for bit, held in self.share_steps():
            for bits in held:
                if bits:
                    self.start([self.share_copies(ref, sems, bit, bits) for ref, sems in refs])
            for bits in held:
                self.arrived([self.share_copies(ref, sems, bit, bits) for ref, sems in refs])

    def merge_slot(self, bit, bits):
        return self.N - self.N // bit + bits // (2 * bit)

    def merge_copies(self, refs, bit, bits):
        slot = self.merge_slot(bit, bits)
        owner = self.captions_of(self.owner(bits + bit))
        return [
            self.copy(ref.at[owner], there.at[slot], sems, slot, self.partner(bit))
            for ref, there, sems in refs
        ]

    def merge_steps(self):
        bit = 1
        while bit < self.N:
            yield bit, range(0, self.N, 2 * bit)
            bit *= 2

    def merge_start(self, refs):
        for bits in range(0, self.N, 2):
            self.start(self.merge_copies(refs, 1, bits))

    def merge_end(self, refs, join):
        for bit, kept in self.merge_steps():
            for bits in reversed(kept):
                self.arrived(self.merge_copies(refs, bit, bits))
                for j in range(self.count):
                    join(self.owner(bits) * self.count + j, self.merge_slot(bit, bits), j)
                if bits % (4 * bit):
                    self.start(self.merge_copies(refs, 2 * bit, bits - 2 * bit))

    def column(self, turned, p):
        return jnp.where(self.is_first, turned[:64, p : p + 1], turned[64:, p : p + 1])

    def turn(self, *rows):
        have = 8 * len(rows)
        return jnp.concatenate([*rows, jnp.zeros((128 - have, 128), F32)], axis=0).T

    def join_softmax(self, place, slot, j):
        total_a, top_a = self.ST[place, :8], self.ST[place, 8:]
        total_b, top_b = self.STR[slot, j, :8], self.STR[slot, j, 8:]
        top = jnp.maximum(top_a, top_b)
        share_a, share_b = jnp.exp(top_a - top), jnp.exp(top_b - top)
        self.ST[place, :8] = share_a * total_a + share_b * total_b
        self.ST[place, 8:] = top
        turned = self.turn(share_a, share_b)
        for p in range(self.pairs):
            at = slice(128 * p, 128 * p + 128)
            a = self.NUM[place, :, at].astype(F32) * self.column(turned, p)
            b = self.NUMR[slot, j, :, at].astype(F32) * self.column(turned, 8 + p)
            self.NUM[place, :, at] = (a + b).astype(LOW)

    def join_sum(self, place, slot, j):
        self.add_into(self.NUM.at[place], self.NUMR[slot, j])

    def attended(self):
        done = []
        for j in range(self.count):
            place = self.nar * self.count + j
            turned = self.turn(1.0 / self.ST[place, :8])
            self.SCT[j] = turned
            parts = []
            for p in range(self.pairs):
                at = slice(128 * p, 128 * p + 128)
                parts.append(self.NUM[place, :, at].astype(F32) * self.column(turned, p))
            done.append(jnp.concatenate(parts, axis=1))
        return jnp.concatenate(done, axis=0)

    def spread_grad(self, doc):
        lane = lax.broadcasted_iota(jnp.int32, (128, 128), 1)
        for j in range(self.count):
            place = self.nar * self.count + j
            rows = slice(64 * j, 64 * j + 64)
            turned = self.SCT[j]
            inner = jnp.zeros((128, 128), F32)
            for p in range(self.pairs):
                at = slice(128 * p, 128 * p + 128)
                part = doc[rows, at] * self.column(turned, p)
                self.GA[place, :, at] = part.astype(LOW)
                prod = part * self.OCF[rows, at]
                a = jnp.sum(jnp.where(self.is_first, prod, 0.0), axis=1, keepdims=True)
                b = jnp.sum(jnp.where(self.is_first, 0.0, prod), axis=1, keepdims=True)
                inner = jnp.where(lane == p, jnp.concatenate([a, b], axis=0), inner)
            self.DL[place, :8] = -inner.T[:8]
            self.DL[place, 8:] = self.ST[place, 8:]

    def weight_images(self):
        return pltpu.make_async_copy(self.images, self.IMG, self.s_image[0].at[0])

    def keep_wide(self, ref, value, sems):
        ref[self.c, self.y] = value
        here = ref.at[self.c, self.y]
        self.start([self.copy(here, here, sems, 0, self.y_peer())])
        self.start([self.copy(here, here, sems, 1, self.sibling())])

    def wide_across(self, ref, sems):
        here = ref.at[self.c, self.y]
        self.copy(here, here, sems, 0, self.y_peer()).wait_recv()
        here = ref.at[self.c, 1 - self.y]
        self.start([self.copy(here, here, sems, 2, self.sibling())])

    def wide_arrived(self, ref, sems):
        for i in (1, 2):
            here = ref.at[self.c, self.y]
            self.copy(here, here, sems, i, self.sibling()).wait_recv()

    def hidden_copy(self, ref, j, sems):
        here = ref.at[j, self.c]
        return self.copy(here, here, sems, j, self.sibling())

    def fold_copy(self, which):
        return self.copy(self.FS.at[which], self.FR.at[which], self.s_fold, which, self.y_peer())

    def run(self):
        tokens, width, count = self.tokens, self.width, self.count
        image_copy = pltpu.make_async_copy(self.images, self.IMG, self.s_image[0].at[0])
        image_copy.start()
        self.pair_pack()
        self.enter()
        self.start(self.pair_copies())
        self.sum_start(0, 0, mm(self.vec[...], self.placement(LOW)))
        self.pair_merge()
        self.first(CK)
        self.start(self.up_copies())
        self.sum_start(0, 1, self.sum_end(0, 0))
        inputs = self.captions[...].astype(F32)
        self.second(CK)
        self.first(CV)
        self.first(QS)
        self.sum_start(0, 2, self.sum_end(0, 1))
        self.third(CK)
        self.second(CV)
        self.first(KS)
        self.sum_start(0, 3, self.sum_end(0, 2))
        self.hand(CK)
        self.third(CV)
        self.second(QS)
        self.first(VS)
        image_copy.wait()
        self.hand(CV)
        self.third(QS)
        self.second(KS)
        self.first(SO)
        self.done(CK)
        self.memory_forward(0)
        self.hand(QS)
        self.third(KS)
        self.second(VS)
        self.first(CQ)
        self.first(DOWN)
        self.done(CV)
        self.memory_forward(1)
        vectors = self.sum_end(0, 3)
        gain1, shift1 = vectors[0:1], vectors[1:2]
        gain2, shift2 = vectors[2:3], vectors[3:4]
        gain3, shift3 = vectors[4:5], vectors[5:6]
        hat1, rstd1, a1 = norm(inputs, gain1, shift1)
        self.HAT[0] = hat1
        a1 = a1.astype(LOW)
        self.keep_left(0, a1)
        self.hand(KS)
        self.third(VS)
        self.second(SO)
        self.first(CO)
        self.done(QS)
        self.QKV[0] = mm(a1, self.weight(QS)).astype(LOW)
        self.hand(VS)
        self.third(SO)
        self.second(CQ)
        self.second(DOWN)
        self.third(DOWN)
        self.first(DOWN + 1)
        self.done(KS)
        self.QKV[1] = mm(a1, self.weight(KS)).astype(LOW)
        self.hand(SO)
        self.third(CQ)
        self.second(CO)
        self.arrived(self.up_copies())
        self.first(UP)
        self.keep_wide(self.G4, self.out_grad[...], self.s_g4)
        self.done(VS)
        self.QKV[2] = mm(a1, self.weight(VS)).astype(LOW)
        mixed = self.self_attention()
        self.keep_left(1, mixed)
        self.hand(CQ)
        self.third(CO)
        self.hand(DOWN)
        self.second(DOWN + 1)
        self.third(DOWN + 1)
        self.done(SO)
        r1 = inputs + mm(mixed, self.weight(SO))
        hat2, rstd2, a2 = norm(r1, gain2, shift2)
        self.HAT[1] = hat2
        a2 = a2.astype(LOW)
        self.keep_left(2, a2)
        self.done(CQ)
        self.QA[self.captions_of(self.nar)] = (
            mm(a2, self.weight(CQ)).astype(LOW).reshape(count, 64, width)
        )
        queries = [(self.QA, self.s_query)]
        self.share_start(queries)
        self.hand(CO)
        self.wide_across(self.G4, self.s_g4)
        self.second(UP)
        self.third(UP)
        self.share_end(queries)
        pl.loop(0, self.groups)(self.cross_forward)
        numbers = [(self.NUM, self.NUMR, self.s_num), (self.ST, self.STR, self.s_st)]
        self.merge_start(numbers)
        self.hand(DOWN + 1)
        self.done(CO)
        self.done(DOWN)
        self.merge_end(numbers, self.join_softmax)
        full = self.attended()
        self.OCF[...] = full
        oc = full.astype(LOW)
        self.keep_left(3, oc)
        r2 = r1 + mm(oc, self.weight(CO))
        hat3, rstd3, a3 = norm(r2, gain3, shift3)
        self.HAT[2] = hat3
        self.keep_wide(self.A3, a3.astype(LOW), self.s_a3)
        self.hand(UP)
        self.done(DOWN + 1)
        self.wide_arrived(self.G4, self.s_g4)
        grad = self.G4[self.c].reshape(2 * tokens, width)
        self.done(UP)
        self.wide_across(self.A3, self.s_a3)
        a3 = self.A3[self.c].reshape(2 * tokens, width)
        for j in range(2):
            hidden = mm(a3, self.weight(UP + j))
            square = hidden * hidden
            tanh = jnp.tanh(GELU_A * hidden * (1.0 + GELU_B * square))
            act = (0.5 * hidden * (1.0 + tanh)).astype(LOW)
            slope = 0.5 * (1.0 + tanh) + 0.5 * hidden * (1.0 - tanh * tanh) * (
                GELU_A * (1.0 + 3.0 * GELU_B * square)
            )
            self.SLOPE[j] = slope
            self.U[j, self.c] = act.reshape(2, tokens, width)
            self.start([self.hidden_copy(self.U, j, self.s_u)])
        self.wide_arrived(self.A3, self.s_a3)
        for j in range(2):
            self.hidden_copy(self.U, j, self.s_u).wait_recv()
        self.gathered = len(self.started)
        self.down_grad()
        self.rs_one(DOWN)
        self.rs_one(DOWN + 1)
        e3 = 0.0
        for j in range(2):
            down = [self.HD[i, 2 * j : 2 * j + 2].reshape(width, 384) for i in range(2)]
            back = mm_bt(grad[:, :384], down[0]) + mm_bt(grad[:, 384:], down[1])
            dhp = (back * self.SLOPE[j]).astype(LOW)
            self.DH[j, self.c] = dhp.reshape(2, tokens, width)
            self.start([self.hidden_copy(self.DH, j, self.s_dh)])
            e3 = e3 + mm_bt(dhp, self.weight(UP + j))
        south = self.y == 0
        self.FS[0] = jnp.where(south, e3[tokens:], e3[:tokens]).astype(LOW)
        self.start([self.fold_copy(0)])
        e3 = jnp.where(south, e3[:tokens], e3[tokens:])
        out = [0.0, 0.0]
        for j in range(2):
            act = self.U[j, self.c].reshape(2 * tokens, width)
            for i in range(2):
                out[i] = out[i] + mm(act, self.HD[i, 2 * j : 2 * j + 2].reshape(width, 384))
        out = jnp.concatenate(out, axis=1)
        self.FS[1] = jnp.where(south, out[tokens:], out[:tokens]).astype(LOW)
        self.start([self.fold_copy(1)])
        out = r2 + jnp.where(south, out[:tokens], out[tokens:])
        for j in range(2):
            self.hidden_copy(self.DH, j, self.s_dh).wait_recv()
        self.finish_early()
        self.up_grad()
        self.rs_one(UP)
        self.fold_copy(0).wait_recv()
        e3 = e3 + self.FR[0].astype(F32)
        back3, gain3_grad, shift3_grad = norm_pull(e3, self.HAT[2], rstd3, gain3)
        dr2 = self.out_grad[...].astype(F32) + back3
        dcat = dr2.astype(LOW)
        self.keep_right(5, dcat)
        self.spread_grad(mm_bt(dcat, self.weight(CO)))
        grads = [(self.GA, self.s_g), (self.DL, self.s_dl)]
        self.share_start(grads)
        self.left_arrived(3)
        self.right_arrived(5)
        self.weight_grad(CO)
        self.rs_one(CO)
        self.rs_two(DOWN)
        self.rs_two(DOWN + 1)
        self.fold_copy(1).wait_recv()
        self.layer_out[...] = (out + self.FR[1].astype(F32)).astype(LOW)
        self.share_end(grads)
        pl.loop(0, self.groups)(self.cross_backward)
        back = [(self.NUM, self.NUMR, self.s_dq)]
        self.merge_start(back)
        self.memory_grad_other(0)
        self.memory_grad_other(1)
        self.rs_two(UP)
        self.rs_two(CO)
        self.memory_grad_own(0)
        self.rs_one(CK)
        self.memory_grad_own(1)
        self.rs_one(CV)
        self.rs_four(DOWN + 1)
        self.merge_end(back, self.join_sum)
        dqc = self.NUM[self.captions_of(self.nar)].reshape(tokens, width)
        self.keep_right(4, dqc)
        back2, gain2_grad, shift2_grad = norm_pull(
            mm_bt(dqc, self.weight(CQ)), self.HAT[1], rstd2, gain2
        )
        dr1 = dr2 + back2
        dattn = dr1.astype(LOW)
        self.keep_right(3, dattn)
        dos = mm_bt(dattn, self.weight(SO)).astype(LOW)
        self.rs_three(CO)
        self.left_arrived(2)
        self.right_arrived(4)
        self.weight_grad(CQ)
        self.rs_one(CQ)
        self.left_arrived(1)
        self.right_arrived(3)
        self.weight_grad(SO)
        self.rs_one(SO)
        self.rs_two(CK)
        self.rs_two(CV)
        e1 = 0.0
        for j, item in enumerate(self.self_attention_back(dos)):
            self.keep_right(j, item)
            e1 = e1 + mm_bt(item, self.weight(j))
        back1, gain1_grad, shift1_grad = norm_pull(e1, self.HAT[0], rstd1, gain1)
        self.input_grad[...] = (dr1 + back1).astype(LOW)
        self.left_arrived(0)
        for place, unit in enumerate((QS, KS, VS)):
            self.right_arrived(place)
            self.weight_grad(unit)
            self.rs_one(unit)
        vec = [gain1_grad, shift1_grad, gain2_grad, shift2_grad, gain3_grad, shift3_grad]
        vec = jnp.concatenate(vec + [jnp.zeros((2, width), F32)], axis=0)
        self.sum_start(1, 0, vec)
        self.rs_four(UP)
        self.rs_two(CQ)
        self.rs_three(CK)
        self.rs_four(CO)
        self.sum_start(1, 1, self.sum_end(1, 0))
        self.rs_two(SO)
        self.rs_three(CV)
        self.rs_up()
        self.sum_start(1, 2, self.sum_end(1, 1))

        @pl.loop(0, 3)
        def _(t):
            size = self.images.shape[0] // 3
            rows = pl.ds(pl.multiple_of(size * t, 16), size)
            part = mm_bt(self.KV[0, rows], self.weight(CK))
            part = part + mm_bt(self.KV[1, rows], self.weight(CV))
            self.IMG[rows] = part.astype(LOW)

        image_copy = pltpu.make_async_copy(self.IMG, self.image_grad, self.s_image[0].at[0])
        image_copy.start()
        self.rs_two(QS)
        self.rs_three(CQ)
        self.rs_four(CK)
        self.sum_start(1, 3, self.sum_end(1, 2))
        self.rs_two(KS)
        self.rs_three(SO)
        self.rs_four(CV)
        self.rs_two(VS)
        self.rs_three(QS)
        self.rs_four(CQ)
        self.rs_three(KS)
        self.rs_four(SO)
        self.rs_three(VS)
        self.rs_four(QS)
        total = self.sum_end(1, 3)
        self.vec_grad[...] = lax.dot_general(
            total,
            self.placement(F32),
            (((1,), (1,)), ((), ())),
            precision=lax.Precision.HIGHEST,
            preferred_element_type=F32,
        )
        self.rs_four(KS)
        self.rs_four(VS)
        for unit in range(UNITS):
            self.rs_done(unit)
        image_copy.wait()
        self.finish_sends()


def layer_call(lanes, narrow, captions, images, lengths, out_grad, vec, *weights):
    tokens, width = captions.shape
    count = tokens // 64
    groups = narrow * count
    image_rows = images.shape[0]
    pairs = width // 128
    ins = ["captions", "images", "lengths", "out_grad", "vec", "self_proj", "self_output"]
    ins += ["cross_query", "cross_memory", "cross_output", "hidden_up", "hidden_down"]
    outs = {
        "layer_out": ((tokens, width), LOW),
        "input_grad": ((tokens, width), LOW),
        "image_grad": ((image_rows, width), LOW),
        "block_grad": ((24, 12 * width), F32),
        "down_out": ((96, width), F32),
        "vec_grad": ((8, 128), F32),
    }
    memory = {
        "W": ((10, 4, 2, 2, 48, width), LOW),
        "HD": ((2, 4, 2, 192, 384), LOW),
        "HG": ((4, 2, 192, 384), LOW),
        "UPS": ((48, width), LOW),
        "UPR": ((48, width), LOW),
        "PA": ((2, 24 * UP, 384), LOW),
        "PB": ((2, 48, width), LOW),
        "IMG": ((image_rows, width), LOW),
        "KV": ((2, image_rows, width), LOW),
        "E": ((groups, pairs, image_rows // groups, 128), LOW),
        "LHS": ((4, 2, tokens, width), LOW),
        "RHS": ((6, 2, tokens, width), LOW),
        "A3": ((2, 2, tokens, width), LOW),
        "G4": ((2, 2, tokens, width), LOW),
        "U": ((2, 2, 2, tokens, width), LOW),
        "DH": ((2, 2, 2, tokens, width), LOW),
        "FS": ((2, tokens, width), LOW),
        "FR": ((2, tokens, width), LOW),
        "R1": ((UP, 4, 2, 48, 384), LOW),
        "R2": ((UP, 4, 48, 384), LOW),
        "R3": ((UP, 3, 48, 384), LOW),
        "RU1": ((4, 2, 48, width), LOW),
        "RU3": ((3, 2, 48, width), LOW),
        "RH1": ((2, 4, 96, 384), LOW),
        "RH3": ((2, 3, 96, 384), LOW),
        "CM": ((2, 4, 2, 2, 48, 384), LOW),
        "CS": ((2, 4, 2, 2, 48, 384), LOW),
        "CP": ((2, 4, 2, 2, 48, 384), LOW),
        "SF": ((UP, 24, 384), F32),
        "SFU": ((2, 24, width), F32),
        "SFH": ((96, 384), F32),
        "V": ((2, 4, 8, width), F32),
        "VR": ((2, 6, 8, width), F32),
        "QKV": ((3, tokens, width), LOW),
        "PS": ((HEADS, 128, 128), F32),
        "HAT": ((3, tokens, width), F32),
        "SLOPE": ((2, 2 * tokens, width), F32),
        "OCF": ((tokens, width), F32),
        "QA": ((groups, 64, width), LOW),
        "NUM": ((groups, 64, width), LOW),
        "ST": ((groups, 16, 128), F32),
        "TOP": ((groups, 8, 128), F32),
        "NUMR": ((narrow - 1, count, 64, width), LOW),
        "STR": ((narrow - 1, count, 16, 128), F32),
        "SCT": ((count, 128, 128), F32),
        "GA": ((groups, 64, width), LOW),
        "DL": ((groups, 16, 128), F32),
    }
    signals = {
        "s_pair": (3,),
        "s_up": (2,),
        "s_z": (UNITS, 3),
        "s_two": (UP, 2),
        "s_three": (UNITS, 2),
        "s_hand": (UNITS,),
        "s_rs1": (UNITS, 2),
        "s_rs2": (UP, 2),
        "s_rs3": (UNITS, 3),
        "s_rs4": (UNITS,),
        "s_rs5": (2, 2),
        "s_vec": (2, 6),
        "s_left": (4,),
        "s_right": (6,),
        "s_a3": (3,),
        "s_g4": (3,),
        "s_u": (2,),
        "s_dh": (2,),
        "s_fold": (2,),
        "s_memory": (2,),
        "s_query": (narrow - 1,),
        "s_num": (narrow - 1,),
        "s_st": (narrow - 1,),
        "s_g": (narrow - 1,),
        "s_dl": (narrow - 1,),
        "s_dq": (narrow - 1,),
        "s_image": (1,),
    }
    scratch = [pltpu.VMEM(shape, kind) for shape, kind in memory.values()]
    for shape in signals.values():
        scratch += [pltpu.SemaphoreType.DMA(shape)] * 2

    def body(*refs):
        named = dict(zip(ins + list(outs) + list(memory), refs))
        rest = refs[len(named) :]
        for i, name in enumerate(signals):
            named[name] = (rest[2 * i], rest[2 * i + 1])
        Layer(named, lanes, narrow).run()

    vmem = pl.BlockSpec(memory_space=pltpu.VMEM)
    in_specs = [vmem] * len(ins)
    in_specs[1] = pl.BlockSpec(memory_space=pl.ANY)
    in_specs[2] = pl.BlockSpec(memory_space=pltpu.SMEM)
    out_specs = [vmem] * len(outs)
    out_specs[2] = pl.BlockSpec(memory_space=pl.ANY)
    return pl.pallas_call(
        body,
        out_shape=[jax.ShapeDtypeStruct(shape, kind) for shape, kind in outs.values()],
        in_specs=in_specs,
        out_specs=out_specs,
        scratch_shapes=scratch,
        compiler_params=pltpu.CompilerParams(
            collective_id=0, has_side_effects=True, vmem_limit_bytes=64 * 1024 * 1024 - 65536
        ),
        cost_estimate=pl.CostEstimate(
            flops=17 * 10**9, bytes_accessed=8 * 10**6, transcendentals=2 * 10**6
        ),
        name="layer",
    )(captions, images, lengths, out_grad, vec, *weights)


def lane_gather(value, lanes, narrow, axis):
    if lanes == 1:
        return value
    assert lanes % narrow == 0
    value = lax.all_gather(value, "narrow", axis=axis, tiled=True)
    step = 1
    wide_count = lax.axis_size("wide")
    while step * narrow < lanes:
        swap = [(i, i ^ step) for i in range(wide_count)]
        other = lax.ppermute(value, "wide", swap)
        low = (lax.axis_index("wide") // step) % 2 == 0
        first = jnp.where(low, value, other)
        second = jnp.where(low, other, value)
        value = jnp.concatenate([first, second], axis=axis)
        step *= 2
    return value


def lane_scatter(value, lanes, narrow, axis):
    if lanes == 1:
        return value
    wide_count = lax.axis_size("wide")
    step = lanes // narrow
    while step > 1:
        step //= 2
        swap = [(i, i ^ step) for i in range(wide_count)]
        first, second = jnp.split(value, 2, axis=axis)
        low = (lax.axis_index("wide") // step) % 2 == 0
        other = lax.ppermute(jnp.where(low, second, first), "wide", swap)
        value = jnp.where(low, first, second) + other
    return lax.psum_scatter(value, "narrow", scatter_dimension=axis, tiled=True)


def per_device(captions, images, lengths, out_grad, *params):
    narrow = lax.axis_size("narrow")
    devices = lax.axis_size("wide") * narrow
    lanes = devices // NODES
    count, seq_len, width = captions.shape
    tokens = count * seq_len
    params = [lane_gather(item, lanes, narrow, 0) for item in params]
    own = width // NODES
    vec = jnp.pad(jnp.stack(params[7:]), ((0, 2), (0, 128 - own)))
    out, input_grad, image_grad, block_grad, down_grad, vec_grad = layer_call(
        lanes,
        narrow,
        captions.reshape(tokens, width),
        images.reshape(-1, width),
        lengths,
        out_grad.reshape(tokens, width),
        vec,
        *params[:7],
    )
    vec_own = vec_grad[:6, :own]
    block_grad = lane_scatter(block_grad, lanes, narrow, 0)
    down_grad = lane_scatter(down_grad, lanes, narrow, 0)
    vec_own = lane_scatter(vec_own, lanes, narrow, 1)

    def columns(start, stop):
        return block_grad[:, start * width : stop * width]

    return (
        out.reshape(captions.shape),
        input_grad.reshape(captions.shape),
        image_grad.reshape(images.shape),
        columns(QS, SO),
        columns(SO, CK),
        columns(CQ, CO),
        columns(CK, CQ),
        columns(CO, UP),
        columns(UP, UP + 4),
        down_grad,
        *[vec_own[i] for i in range(6)],
    )


def solution(mesh):
    both = ("wide", "narrow")
    rows = P(both, None)
    text = P(both, None, None)
    vector = P(both)
    image = P("wide", "narrow", None)
    in_specs = (text, image, vector, text) + (rows,) * 7 + (vector,) * 6
    out_specs = (text, text, image) + (rows,) * 7 + (vector,) * 6
    return jax.shard_map(
        per_device, mesh=mesh, in_specs=in_specs, out_specs=out_specs, check_vma=False
    )
```

```python
import functools

import jax
import jax.numpy as jnp
from jax import lax
from jax.experimental import pallas as pl
from jax.experimental.pallas import tpu as pltpu
from jax.sharding import PartitionSpec as P

HEADS = 12
NODES = 32
UNITS = 11
VMEM_LIMIT = 64 * 1024 * 1024 - 65536
MESH = pl.DeviceIdType.MESH
F32 = jnp.float32
LOW = jnp.bfloat16
EPSILON = 1e-05
GELU_A = 0.7978845608028654
GELU_B = 0.044715

QS, KS, VS, SO, CK, CV, CQ, CO, UP = 0, 1, 2, 3, 4, 5, 6, 7, 8
DOWN = UP + 1
LATE = DOWN + 1
GATHER = (128, 256) * 4
SCATTER = (256, 128) * 4


VECTORS = ["first_gain", "first_shift", "second_gain", "second_shift"]
VECTORS += ["third_gain", "third_shift"]


class Step:
    (
        begin,
        up0,
        vec,
        g0,
        g1,
        mem,
        a1,
        qkv,
        sa,
        r1,
        cq,
        q1,
        cf,
        m1,
        m2,
        a3,
        x1,
        hp,
        dg,
        e3,
        out,
        lo,
        ug,
        dr2,
        p1,
        cb,
        n1,
        n2,
        dq,
        mo,
        mw,
        wg,
        sb,
        sum,
        img,
        end,
        F,
        S,
        TA,
        TB,
        H,
        R1,
        RA,
        RB,
        R3,
        R4,
        RU,
    ) = range(47)


ORDER = [
    (Step.begin,), (Step.F, 0), (Step.g0,), (Step.vec, 1), (Step.F, 1), (Step.vec, 2), (Step.F, 3),
    (Step.up0,), (Step.S, 0), (Step.F, 2), (Step.F, 5), (Step.S, 1), (Step.TA, 0), (Step.S, 3),
    (Step.TA, 1), (Step.TB, 1), (Step.F, 6), (Step.TB, 0), (Step.TA, 3), (Step.TB, 3),
    (Step.vec, 3), (Step.g1,), (Step.S, 2), (Step.F, 4), (Step.H, 1), (Step.S, 6), (Step.S, 5),
    (Step.F, 7), (Step.a1,), (Step.TA, 2), (Step.TB, 2), (Step.qkv, 1), (Step.F, 8), (Step.S, 4),
    (Step.F, 10), (Step.TA, 6), (Step.TB, 6), (Step.H, 0), (Step.H, 2), (Step.S, 7), (Step.TB, 5),
    (Step.TA, 5), (Step.qkv, 0), (Step.TB, 4), (Step.qkv, 2), (Step.H, 3), (Step.sa,), (Step.F, 9),
    (Step.r1,), (Step.H, 6), (Step.TA, 4), (Step.H, 5), (Step.S, 10), (Step.S, 8), (Step.cq,),
    (Step.TA, 7), (Step.H, 4), (Step.mem, 1), (Step.TB, 7), (Step.mem, 0), (Step.q1,),
    (Step.cf, 1), (Step.m1,), (Step.S, 9), (Step.cf, 0), (Step.H, 7), (Step.m2,), (Step.a3,),
    (Step.H, 8), (Step.H, 9), (Step.H, 10), (Step.x1,), (Step.hp,), (Step.e3,), (Step.dg,),
    (Step.ug,), (Step.R1, 10), (Step.R1, 9), (Step.R1, 8), (Step.out,), (Step.dr2,), (Step.wg, 7),
    (Step.cb, 0), (Step.R1, 7), (Step.p1,), (Step.cb, 1), (Step.n1,), (Step.mo, 0), (Step.mo, 1),
    (Step.mw, 0), (Step.R1, 4), (Step.RA, 9), (Step.RA, 7), (Step.n2,), (Step.RA, 8), (Step.RB, 7),
    (Step.mw, 1), (Step.R1, 5), (Step.dq,), (Step.sb,), (Step.wg, 3), (Step.R1, 3), (Step.wg, 0),
    (Step.RA, 4), (Step.wg, 2), (Step.R1, 2), (Step.sum, 1), (Step.RA, 5), (Step.RB, 4),
    (Step.wg, 6), (Step.img,), (Step.wg, 1), (Step.RB, 5), (Step.R1, 0), (Step.RA, 2),
    (Step.R1, 1), (Step.R3, 7), (Step.R3, 4), (Step.RB, 3), (Step.sum, 2), (Step.RA, 3),
    (Step.RB, 2), (Step.R3, 5), (Step.RA, 10), (Step.sum, 3), (Step.R1, 6), (Step.R3, 2),
    (Step.RA, 0), (Step.RB, 0), (Step.R4, 9), (Step.R3, 3), (Step.R4, 8), (Step.RB, 1),
    (Step.RA, 1), (Step.R3, 0), (Step.RA, 6), (Step.RU, 8), (Step.RB, 6), (Step.R4, 2),
    (Step.R3, 1), (Step.R4, 4), (Step.R4, 7), (Step.R4, 5), (Step.lo,), (Step.R3, 6), (Step.R4, 3),
    (Step.R4, 0), (Step.R4, 1), (Step.R4, 6), (Step.end,),
]


def mm(left, right):
    return jnp.dot(left, right, preferred_element_type=F32)


def mm_bt(left, right):
    return lax.dot_general(left, right, (((1,), (1,)), ((), ())), preferred_element_type=F32)


def mm_at(left, right):
    return lax.dot_general(left, right, (((0,), (0,)), ((), ())), preferred_element_type=F32)


def norm(value, gain, shift):
    centred = value - jnp.mean(value, axis=-1, keepdims=True)
    rstd = lax.rsqrt(jnp.mean(centred * centred, axis=-1, keepdims=True) + EPSILON)
    hat = centred * rstd
    return hat, rstd, hat * gain + shift


def norm_pull(grad, hat, rstd, gain):
    scaled = grad * gain
    inner = jnp.mean(scaled * hat, axis=-1, keepdims=True)
    back = rstd * (scaled - jnp.mean(scaled, axis=-1, keepdims=True) - hat * inner)
    gain_grad = jnp.sum(grad * hat, axis=0, keepdims=True)
    shift_grad = jnp.sum(grad, axis=0, keepdims=True)
    return back, gain_grad, shift_grad


class Layer:
    def __init__(self, refs, lanes, narrow):
        self.__dict__.update(refs)
        self.N = narrow
        self.lanes = lanes
        wide, nar = lax.axis_index("wide"), lax.axis_index("narrow")
        flat = wide * narrow + nar
        self.wide, self.nar = wide, nar
        self.node = lax.div(flat, lanes)
        self.lane = lax.rem(flat, lanes)
        node = self.node
        self.c = lax.rem(node, 2)
        self.x = lax.rem(lax.div(node, 2), 2)
        self.y = lax.rem(lax.div(node, 4), 2)
        self.z = lax.div(node, 8)
        self.started = {}
        self.here = set()
        self.count, self.seq = self.captions.shape[0] // 64, 64
        self.tokens, self.width = self.captions.shape
        self.groups = self.QA.shape[0]
        self.image_rows = self.images.shape[0] // self.groups
        self.pairs = self.width // 128
        lane = lax.broadcasted_iota(jnp.int32, (1, 128), 1)
        self.low_lanes = (lane < 64).astype(F32).astype(LOW)
        self.high_lanes = (lane >= 64).astype(F32).astype(LOW)
        self.is_first = lane < 64

    def device(self, z, y, x, c):
        flat = (z * 8 + y * 4 + x * 2 + c) * self.lanes + self.lane
        return (lax.div(flat, self.N), lax.rem(flat, self.N))

    def sibling(self):
        return self.device(self.z, self.y, self.x, 1 - self.c)

    def x_peer(self):
        return self.device(self.z, self.y, 1 - self.x, self.c)

    def y_peer(self):
        return self.device(self.z, 1 - self.y, self.x, self.c)

    def z_index(self, k):
        return lax.rem(self.z + k, 4)

    def z_peer(self, k):
        return self.device(self.z_index(k), self.y, self.x, self.c)

    def n_index(self, k):
        return lax.rem(self.nar + k, self.N)

    def n_peer(self, k):
        return (self.wide, self.n_index(k))

    def enter(self):
        barrier = pltpu.get_barrier_semaphore()
        peers = [self.sibling(), self.x_peer(), self.y_peer()]
        peers += [self.z_peer(k) for k in (1, 2, 3)]
        peers += [self.n_peer(k) for k in range(1, self.N)]
        for peer in peers:
            pl.semaphore_signal(barrier, inc=1, device_id=peer, device_id_type=MESH)
        pl.semaphore_wait(barrier, len(peers))

    def copy(self, src, dst, sems, where, peer):
        send, recv = sems
        return pltpu.make_async_remote_copy(
            src_ref=src,
            dst_ref=dst,
            send_sem=send.at[where],
            recv_sem=recv.at[where],
            device_id=peer,
            device_id_type=MESH,
        )

    def start(self, copies, group=None):
        for item in copies:
            item.start()
        self.started.setdefault(group, []).extend(copies)

    def sent(self, group):
        for item in self.started.pop(group, []):
            item.wait_send()

    def part(self, unit, half, z, y, x, grad=False):
        every = slice(None)
        if unit < UP:
            first = (SCATTER if grad else GATHER)[unit]
            low, size = ((0, 384), (0, first), (first, 384 - first))[0 if half is None else half + 1]
            if grad and unit in (CK, CV):
                return self.CP.at[unit - CK, z, y, x, every, pl.ds(low, size)]
            columns = pl.ds(pl.multiple_of(384 * self.c + low, 128), size)
            return self.W.at[unit, z, y, x, every, columns]
        if unit == UP:
            return self.W.at[UP + self.c, z, y, x]
        ref = self.HG if grad else self.HD.at[self.c]
        return ref.at[z, y, pl.ds(96 * (unit - DOWN), 96)]

    def half_columns(self, c):
        return pl.ds(pl.multiple_of(384 * c, 128), 384)

    def shards(self):
        found = [(self.self_proj, self.width * j) for j in range(3)] + [(self.self_output, 0)]
        found += [(self.cross_memory, self.width * j) for j in range(2)]
        return found + [(self.cross_query, 0), (self.cross_output, 0)]

    def half_block(self, block, c):
        ref, start = self.shards()[block]
        return ref[:, pl.ds(pl.multiple_of(start + 384 * c, 128), 384)].astype(F32)

    def swapped(self, value):
        return pltpu.roll(value, 64, 1)

    def split_runs(self, whole):
        n = [whole[:, 128 * i : 128 * i + 128] for i in range(6)]
        r = [self.swapped(item) for item in n]
        low = self.is_first
        a = [n[0], jnp.where(low, n[1], r[3]), jnp.where(low, r[3], r[4])]
        b = [jnp.where(low, r[1], r[2]), jnp.where(low, r[2], n[4]), n[5]]
        return jnp.concatenate(a, axis=1), jnp.concatenate(b, axis=1)

    def join_runs(self, left, right):
        a = [left[:, 128 * i : 128 * i + 128] for i in range(3)]
        b = [right[:, 128 * i : 128 * i + 128] for i in range(3)]
        ra, rb = [self.swapped(item) for item in a], [self.swapped(item) for item in b]
        low = self.is_first
        out = [a[0], jnp.where(low, a[1], rb[0]), jnp.where(low, rb[0], rb[1])]
        out += [jnp.where(low, ra[1], ra[2]), jnp.where(low, ra[2], b[1]), b[2]]
        return jnp.concatenate(out, axis=1)

    def up_blocks(self, c):
        found = []
        for j in range(2):
            start = pl.multiple_of(self.width * (2 * c + j), 128)
            found.append(self.split_runs(self.hidden_up[:, pl.ds(start, self.width)].astype(F32)))
        return [jnp.concatenate(item, axis=1) for item in zip(*found)]

    def pair_copies(self):
        c = self.c
        rows = pl.ds(pl.multiple_of(96 * c, 32), 96)
        there = self.HD.at[1 - c, self.z, self.y, rows]
        down = self.hidden_down.at[:, self.half_columns(1 - c)]
        return [
            self.copy(self.PA.at[0], self.PA.at[1], self.s_pair, 0, self.sibling()),
            self.copy(self.PB.at[0], self.PB.at[1], self.s_pair, 1, self.sibling()),
            self.copy(down, there, self.s_pair, 2, self.sibling()),
        ]

    def pair_pack(self):
        c = 1 - self.c
        blocks = [self.half_block(block, c) for block in range(UP)]
        self.PA[0] = jnp.concatenate(blocks, axis=0).astype(LOW)
        self.PB[0] = jnp.concatenate(self.up_blocks(c), axis=0).astype(LOW)

    def in_order(self, mine, theirs):
        even = self.c == 0
        low, high = jnp.where(even, mine, theirs), jnp.where(even, theirs, mine)
        return jnp.concatenate([low, high], axis=0)

    def pair_merge(self):
        c = self.c
        copies = self.pair_copies()
        rows = pl.ds(pl.multiple_of(96 * c, 32), 96)
        self.HD[c, self.z, self.y, rows] = self.hidden_down[:, self.half_columns(c)]
        columns = pl.ds(pl.multiple_of(384 * c, 128), 384)
        copies[0].wait_recv()
        theirs = self.PA[1].astype(F32)
        for block in range(UP):
            both = self.in_order(self.half_block(block, c), theirs[24 * block : 24 * block + 24])
            self.W[block, self.z, self.y, self.x, :, columns] = both.astype(LOW)
        copies[1].wait_recv()
        theirs = self.PB[1].astype(F32)
        both = [
            self.in_order(mine, theirs[24 * i : 24 * i + 24])
            for i, mine in enumerate(self.up_blocks(c))
        ]
        west = self.x == 0
        self.W[UP + c, self.z, self.y, self.x] = jnp.where(west, both[0], both[1]).astype(LOW)
        self.UPS[...] = jnp.where(west, both[1], both[0]).astype(LOW)
        copies[2].wait_recv()

    def up_copies(self):
        there = self.W.at[UP + self.c, self.z, self.y, self.x]
        return [self.copy(self.UPS, there, self.s_up, 0, self.x_peer())]

    def z_copies(self, unit):
        x = slice(None) if unit == UP else self.x
        y = slice(None) if unit == LATE else self.y
        here = self.part(unit, None, self.z, y, x)
        return [
            self.copy(here, here, self.s_z, (unit, k - 1), self.z_peer(k)) for k in (1, 2, 3)
        ]

    def halves(self, unit, table):
        return range(1 if table[unit] == 384 else 2)

    def two_copy(self, unit, half):
        here = self.part(unit, half, slice(None), self.y, self.x)
        peer = (self.x_peer, self.y_peer)[half]()
        return self.copy(here, here, self.s_two, (unit, half), peer)

    def three_copy(self, unit, half):
        every = slice(None)
        if unit >= UP:
            z = self.z if unit == LATE else every
            here = self.part(unit, None, z, self.y, every)
            return self.copy(here, here, self.s_three, (unit, 0), self.y_peer())
        y, x = ((self.y, every), (every, self.x))[half]
        here = self.part(unit, half, every, y, x)
        peer = (self.y_peer, self.x_peer)[half]()
        return self.copy(here, here, self.s_three, (unit, half), peer)

    def three_copies(self, unit):
        halves = (0,) if unit >= UP else self.halves(unit, GATHER)
        return [self.three_copy(unit, half) for half in halves]

    def hand_copies(self, unit):
        every = slice(None)
        whole = self.part(unit, None, every, every, every)
        return [self.copy(whole, whole, self.s_hand, unit, self.sibling())]

    def arrived(self, copies):
        for item in copies:
            item.wait_recv()

    def first(self, unit):
        if unit == UP:
            self.arrived(self.up_copies())
        self.start(self.three_copies(unit) if unit == LATE else self.z_copies(unit), unit)

    def second(self, unit):
        if unit == LATE:
            self.arrived(self.three_copies(unit))
            self.start(self.z_copies(unit), unit)
            return
        self.arrived(self.z_copies(unit))
        if unit < UP:
            copies = [self.two_copy(unit, half) for half in self.halves(unit, GATHER)]
        else:
            copies = self.three_copies(unit)
        self.start(copies, unit)

    def third(self, unit, half):
        if half in self.halves(unit, GATHER):
            self.arrived([self.two_copy(unit, half)])
            self.start([self.three_copy(unit, half)], unit)

    def hand(self, unit):
        self.arrived(self.z_copies(unit) if unit == LATE else self.three_copies(unit))
        self.start(self.hand_copies(unit), unit)

    def done(self, unit):
        self.arrived(self.hand_copies(unit))

    def term(self, unit, half, z=slice(None)):
        first = SCATTER[unit]
        return (unit, z, ..., pl.ds(*((0, first), (first, 384 - first))[half]))

    def rs_one_copy(self, unit, half):
        every = slice(None)
        if unit == LATE:
            here = self.part(unit, None, self.z, 1 - self.y, every, grad=True)
            return self.copy(here, self.RL1, self.s_rs1, (unit, 0), self.y_peer())
        if unit >= UP:
            here = self.part(unit, None, every, 1 - self.y, every, grad=True)
            there = self.RU1 if unit == UP else self.RH1
            return self.copy(here, there, self.s_rs1, (unit, 0), self.y_peer())
        y, x = ((1 - self.y, every), (every, 1 - self.x))[half]
        here = self.part(unit, half, every, y, x, grad=True)
        there = self.R1.at[self.term(unit, half)]
        peer = (self.y_peer, self.x_peer)[half]()
        return self.copy(here, there, self.s_rs1, (unit, half), peer)

    def rs_two_copy(self, unit, half):
        y, x = ((self.y, 1 - self.x), (1 - self.y, self.x))[half]
        here = self.part(unit, half, slice(None), y, x, grad=True)
        there = self.R2.at[self.term(unit, half)]
        peer = (self.x_peer, self.y_peer)[half]()
        return self.copy(here, there, self.s_rs2, (unit, half), peer)

    def rs_three_copies(self, unit):
        out = []
        x = slice(None) if unit == UP else self.x
        y = slice(None) if unit == LATE else self.y
        for k in (1, 2, 3):
            here = self.part(unit, None, self.z_index(k), y, x, grad=True)
            if unit < UP:
                there = self.R3.at[unit, k - 1]
            elif unit == UP:
                there = self.RU3.at[k - 1]
            else:
                there = (self.RL3 if unit == LATE else self.RH3).at[k - 1]
            out.append(self.copy(here, there, self.s_rs3, (unit, k - 1), self.z_peer(k)))
        return out

    def up_back_copies(self):
        return [self.copy(self.UPS, self.UPR, self.s_up, 1, self.x_peer())]

    def grad_columns(self, block):
        return pl.ds(pl.multiple_of(self.width * block + 384 * self.c, 128), 384)

    def rs_four_copies(self, unit):
        c = self.c
        if unit < UP:
            there = self.block_grad.at[:, self.grad_columns(unit)]
            return [self.copy(self.SF.at[unit], there, self.s_rs4, unit, self.sibling())]
        if unit == UP:
            columns = self.half_columns_up()
            return [
                self.copy(
                    self.SFU.at[i],
                    self.UPG.at[self.up_side(i), :, columns],
                    self.s_rs5,
                    i,
                    self.sibling(),
                )
                for i in range(2)
            ]
        there = self.down_out.at[:, self.half_columns(c)]
        return [self.copy(self.SFH, there, self.s_rs4, unit, self.sibling())]

    def up_side(self, i):
        return self.x if i == 0 else 1 - self.x

    def half_columns_up(self):
        return pl.ds(pl.multiple_of(self.width * self.c, 128), self.width)

    def add_into(self, ref, term):
        ref[...] = (ref[...].astype(F32) + term.astype(F32)).astype(LOW)

    def rs_one(self, unit):
        halves = (0,) if unit >= UP else self.halves(unit, SCATTER)
        if unit == LATE:
            self.start(self.rs_three_copies(unit))
        else:
            self.start([self.rs_one_copy(unit, half) for half in halves])

    def rs_two(self, unit, half=0):
        every = slice(None)
        if unit < UP and half not in self.halves(unit, SCATTER):
            return
        if unit == LATE:
            self.arrived(self.rs_three_copies(unit))
            here = self.part(unit, None, self.z, every, self.x, grad=True)
            here[...] = self.sum_of(here[...], [self.RL3[k] for k in range(3)]).astype(LOW)
            self.start([self.rs_one_copy(unit, 0)])
            return
        self.arrived([self.rs_one_copy(unit, half)])

        @pl.loop(0, 4)
        def _(z):
            if unit < UP:
                y, x = ((self.y, every), (every, self.x))[half]
                more = self.R1[self.term(unit, half, z)]
                self.add_into(self.part(unit, half, z, y, x, grad=True), more)
            else:
                more = self.RU1[z] if unit == UP else self.RH1[z]
                self.add_into(self.part(unit, None, z, self.y, every, grad=True), more)

        if unit < UP:
            self.start([self.rs_two_copy(unit, half)])
        else:
            self.start(self.rs_three_copies(unit))

    def rs_three(self, unit):
        halves = self.halves(unit, SCATTER)
        self.arrived([self.rs_two_copy(unit, half) for half in halves])

        @pl.loop(0, 4)
        def _(z):
            for half in halves:
                more = self.R2[self.term(unit, half, z)]
                self.add_into(self.part(unit, half, z, self.y, self.x, grad=True), more)

        self.start(self.rs_three_copies(unit))

    def sum_of(self, value, terms):
        return sum((item.astype(F32) for item in terms), value.astype(F32))

    def rs_total(self, unit):
        x = slice(None) if unit == UP else self.x
        own = self.part(unit, None, self.z, self.y, x, grad=True)
        if unit == LATE:
            self.arrived([self.rs_one_copy(unit, 0)])
            return self.sum_of(own[...], [self.RL1[...]])
        self.arrived(self.rs_three_copies(unit))
        if unit < UP:
            return self.sum_of(own[...], [self.R3[unit, k] for k in range(3)])
        ref = self.RU3 if unit == UP else self.RH3
        return self.sum_of(own[...], [ref[k] for k in range(3)])

    def rs_four(self, unit):
        even = self.c == 0
        if unit < UP:
            total = self.rs_total(unit)
            low, high = total[:24], total[24:]
            self.block_grad[:, self.grad_columns(unit)] = jnp.where(even, low, high)
            self.SF[unit] = jnp.where(even, high, low)
            self.start(self.rs_four_copies(unit))
        if unit == UP:
            total = self.rs_total(unit)
            west = self.x == 0
            self.sent("up")
            self.UPS[...] = jnp.where(west, total[1], total[0]).astype(LOW)
            self.start(self.up_back_copies())
            self.up_rows(0, jnp.where(west, total[0], total[1]))
        if unit == DOWN:
            low, high = self.rs_total(DOWN), self.rs_total(DOWN + 1)
            self.down_out[:, self.half_columns(self.c)] = jnp.where(even, low, high)
            self.SFH[...] = jnp.where(even, high, low)
            self.start(self.rs_four_copies(DOWN))

    def up_rows(self, i, total):
        even = self.c == 0
        low, high = total[:24], total[24:]
        self.UPG[self.up_side(i), :, self.half_columns_up()] = jnp.where(even, low, high)
        self.SFU[i] = jnp.where(even, high, low)

    def rs_up(self):
        self.arrived(self.up_back_copies())
        self.up_rows(1, self.UPR[...].astype(F32))
        self.start(self.rs_four_copies(UP))

    def rs_done(self, unit):
        if unit != DOWN + 1:
            self.arrived(self.rs_four_copies(unit))
        if unit == UP:
            for z in range(4):
                at = slice(384 * z, 384 * z + 384)
                start = self.width * (UP + z)
                both = self.join_runs(self.UPG[0, :, at], self.UPG[1, :, at])
                self.block_grad[:, start : start + self.width] = both

    def sum_copies(self, which, stage):
        peers = [[self.sibling()], [self.x_peer()], [self.y_peer()]]
        peers += [[self.z_peer(k) for k in (1, 2, 3)]]
        return [
            self.copy(
                self.V.at[which, stage],
                self.VR.at[which, stage + i],
                self.s_vec,
                (which, stage + i),
                peer,
            )
            for i, peer in enumerate(peers[stage])
        ]

    def placement(self, dtype, rows):
        own = self.width // NODES
        at = lax.broadcasted_iota(jnp.int32, (rows, self.width), 0)
        feature = lax.broadcasted_iota(jnp.int32, (rows, self.width), 1)
        return ((at < own) & (feature == at + own * self.node)).astype(F32).astype(dtype)

    def sum_start(self, which, stage, value):
        self.V[which, stage] = value
        self.start(self.sum_copies(which, stage))

    def sum_end(self, which, stage):
        now = self.sum_copies(which, stage)
        self.arrived(now)
        value = self.V[which, stage]
        for i in range(len(now)):
            value = value + self.VR[which, stage + i]
        return value

    def keep_left(self, place, value):
        self.LHS[place, self.c] = value
        here = self.LHS.at[place, self.c]
        self.start([self.copy(here, here, self.s_left, place, self.sibling())])

    def keep_right(self, place, value):
        self.RHS[place, self.c] = value
        here = self.RHS.at[place, self.c]
        self.start([self.copy(here, here, self.s_right, place, self.sibling())])

    def left_arrived(self, place):
        if ("left", place) not in self.here:
            self.here.add(("left", place))
            here = self.LHS.at[place, self.c]
            self.copy(here, here, self.s_left, place, self.sibling()).wait_recv()

    def right_arrived(self, place):
        if ("right", place) not in self.here:
            self.here.add(("right", place))
            here = self.RHS.at[place, self.c]
            self.copy(here, here, self.s_right, place, self.sibling()).wait_recv()

    def weight(self, block):
        return self.W[block].reshape(self.width, self.width)

    def weight_grad(self, unit):
        left, right = {QS: (0, 0), KS: (0, 1), VS: (0, 2), SO: (1, 3), CQ: (2, 4), CO: (3, 5)}[unit]
        self.sent(unit)
        self.left_arrived(left)
        self.right_arrived(right)
        columns = self.half_columns(self.c)
        right_all = self.RHS[right, :, :, columns].reshape(2 * self.tokens, 384)
        for t in range(2):
            left_all = self.LHS[left, :, :, pl.ds(384 * t, 384)].reshape(2 * self.tokens, 384)
            part = mm_at(left_all, right_all).astype(LOW)
            self.W[unit, pl.ds(2 * t, 2), :, :, :, columns] = part.reshape(2, 2, 2, 48, 384)

    def up_grad(self):
        c = self.c
        self.sent(UP)
        right_all = self.DH[c].reshape(4 * self.tokens, self.width)
        for t in range(2):
            left_all = self.A3[:, :, :, pl.ds(384 * t, 384)].reshape(4 * self.tokens, 384)
            part = mm_at(left_all, right_all).astype(LOW)
            self.W[UP + c, pl.ds(2 * t, 2)] = part.reshape(2, 2, 2, 48, self.width)

    def down_grad(self):
        right_all = self.G4[:, :, :, self.half_columns(self.c)].reshape(4 * self.tokens, 384)
        for z in range(4):
            j, t = z // 2, z % 2
            left_all = self.U[j, :, :, :, pl.ds(384 * t, 384)].reshape(4 * self.tokens, 384)
            part = mm_at(left_all, right_all).astype(LOW)
            self.HG[z] = part.reshape(2, 192, 384)

    def memory_copy(self, which):
        return self.copy(
            self.CS.at[which], self.CM.at[which], self.s_memory, which, self.sibling()
        )

    def memory_term(self, which, c, t):
        left = self.IMG[:, pl.ds(384 * t, 384)]
        part = mm_at(left, self.KV[which, :, self.half_columns(c)])
        return part.reshape(2, 2, 2, 48, 384)

    def memory_grad_other(self, which):
        for t in range(2):
            part = self.memory_term(which, 1 - self.c, t)
            self.CS[which, pl.ds(2 * t, 2)] = part.astype(LOW)
        self.start([self.memory_copy(which)])

    def memory_grad_own(self, which):
        self.memory_copy(which).wait_recv()
        for t in range(2):
            part = self.memory_term(which, self.c, t)
            part = part + self.CM[which, pl.ds(2 * t, 2)].astype(F32)
            self.CP[which, pl.ds(2 * t, 2)] = part.astype(LOW)

    def masked(self, value):
        return value * self.low_lanes, value * self.high_lanes

    def self_attention(self):
        rows = lax.broadcasted_iota(jnp.int32, (128, 128), 0)
        cols = lax.broadcasted_iota(jnp.int32, (128, 128), 1)
        length = jnp.where(cols < 64, self.lengths[0], self.lengths[1])
        allowed = (lax.div(rows, 64) == lax.div(cols, 64)) & (cols <= rows)
        allowed = allowed & (lax.rem(cols, 64) < length)
        parts = []
        for p in range(self.pairs):
            at = slice(128 * p, 128 * p + 128)
            q, k, v = self.QKV[0, :, at], self.QKV[1, :, at], self.QKV[2, :, at]
            both = mm_bt(q, self.stacked(k)) * 0.125
            probs = []
            for h in range(2):
                s = jnp.where(allowed, both[:, 128 * h : 128 * h + 128], -1000000000.0)
                e = jnp.exp(s - jnp.max(s, axis=-1, keepdims=True))
                probs.append(e / jnp.sum(e, axis=-1, keepdims=True))
            prob = jnp.concatenate(probs, axis=1)
            self.PS[p] = prob
            parts.append(mm(prob.astype(LOW), self.stacked(v)).astype(LOW))
        return jnp.concatenate(parts, axis=1)

    def self_attention_back(self, grad):
        parts = ([], [], [])
        for p in range(self.pairs):
            at = slice(128 * p, 128 * p + 128)
            q, k, v = self.QKV[0, :, at], self.QKV[1, :, at], self.QKV[2, :, at]
            g = grad[:, at]
            prob = self.PS[p]
            dp = mm_bt(g, self.stacked(v))
            prod = prob * dp
            parts_ds = []
            for h in range(2):
                lanes = slice(128 * h, 128 * h + 128)
                inner = jnp.sum(prod[:, lanes], axis=-1, keepdims=True)
                parts_ds.append(prob[:, lanes] * (dp[:, lanes] - inner))
            ds = jnp.concatenate(parts_ds, axis=1).astype(LOW)
            dq = mm(ds, self.stacked(k))
            dk = self.diagonal(mm_at(ds, q), 128)
            dv = self.diagonal(mm_at(prob.astype(LOW), g), 128)
            for out, item in zip(parts, (dq * 0.125, dk * 0.125, dv)):
                out.append(item.astype(LOW))
        return [jnp.concatenate(item, axis=1) for item in parts]

    def stacked(self, value):
        a, b = self.masked(value)
        return jnp.concatenate([a, b], axis=0)

    def diagonal(self, value, rows):
        return jnp.where(self.is_first, value[:rows], value[rows:])

    def stacked_four(self, value):
        zero = jnp.zeros((value.shape[0], 128), LOW)
        left = [jnp.concatenate([item, zero], axis=1) for item in self.masked(value[:, :128])]
        right = [jnp.concatenate([zero, item], axis=1) for item in self.masked(value[:, 128:])]
        return jnp.concatenate(left + right, axis=0)

    def diagonal_four(self, value):
        left = jnp.where(self.is_first, value[:64, :128], value[64:128, :128])
        right = jnp.where(self.is_first, value[128:192, 128:], value[192:, 128:])
        return jnp.concatenate([left, right], axis=1)

    def row_pair(self, ref, place, row):
        return jnp.concatenate([ref[place, row : row + 1], ref[place, row + 1 : row + 2]], axis=1)

    def put_pair(self, ref, place, row, value):
        ref[place, row : row + 1] = value[:, :128]
        ref[place, row + 1 : row + 2] = value[:, 128:]

    def memory_forward(self, which):
        w = self.weight(CK + which)

        @pl.loop(0, 3)
        def _(t):
            size = self.images.shape[0] // 3
            rows = pl.ds(pl.multiple_of(size * t, 16), size)
            self.KV[which, rows] = mm(self.IMG[rows], w).astype(LOW)

    def cross_forward(self, place):
        rows = pl.ds(pl.multiple_of(place * self.image_rows, 16), self.image_rows)
        for f in range(self.pairs // 2):
            at = slice(256 * f, 256 * f + 256)
            k, v = self.KV[0, rows, at], self.KV[1, rows, at]
            q = self.stacked_four(self.QA[place, :, at])
            s = mm_bt(k, q) * 0.125
            top = jnp.max(s, axis=0, keepdims=True)
            e = jnp.exp(s - top)
            low = e.astype(LOW)
            self.E[place, f] = low
            self.put_pair(self.ST, place, 2 * f, jnp.sum(e, axis=0, keepdims=True))
            self.put_pair(self.ST, place, 8 + 2 * f, top)
            self.put_pair(self.TOP, place, 2 * f, top)
            num = mm_at(low, v)
            self.NUM[place, :, at] = self.diagonal_four(num).astype(LOW)
        self.ST[place, 6:8] = jnp.ones((2, 128), F32)
        self.ST[place, 14:16] = jnp.zeros((2, 128), F32)

    def cross_backward(self, place):
        rows = pl.ds(pl.multiple_of(place * self.image_rows, 16), self.image_rows)
        for f in range(self.pairs // 2):
            at = slice(256 * f, 256 * f + 256)
            k, v = self.KV[0, rows, at], self.KV[1, rows, at]
            q = self.stacked_four(self.QA[place, :, at])
            g = self.stacked_four(self.GA[place, :, at])
            top = self.row_pair(self.TOP, place, 2 * f)
            share = jnp.exp(top - self.row_pair(self.DL, place, 8 + 2 * f))
            e = self.E[place, f].astype(F32) * share
            ds = e * (mm_bt(v, g) + self.row_pair(self.DL, place, 2 * f))
            ds = ds.astype(LOW)
            dq = mm_at(ds, k)
            self.NUM[place, :, at] = (self.diagonal_four(dq) * 0.125).astype(LOW)
            self.KV[0, rows, at] = (mm(ds, q) * 0.125).astype(LOW)
            self.KV[1, rows, at] = mm(e.astype(LOW), g).astype(LOW)

    def captions_of(self, owner):
        return pl.ds(owner * self.count, self.count)

    def partner(self, bit):
        return (self.wide, jnp.bitwise_xor(self.nar, bit))

    def owner(self, bits):
        return jnp.bitwise_xor(self.nar, bits)

    def share_copies(self, ref, sems, bit, bits):
        here = ref.at[self.captions_of(self.owner(bits))]
        return self.copy(here, here, sems, (self.N + bits) // (2 * bit) - 1, self.partner(bit))

    def share_steps(self):
        bit = self.N // 2
        while bit:
            yield bit, range(0, self.N, 2 * bit)
            bit //= 2

    def share_start(self, refs):
        for bit, held in self.share_steps():
            self.start([self.share_copies(ref, sems, bit, 0) for ref, sems in refs])

    def share_pass(self, refs):
        for bit, held in self.share_steps():
            for bits in held:
                if bits:
                    self.start([self.share_copies(ref, sems, bit, bits) for ref, sems in refs])
            if bit > 1:
                for bits in held:
                    self.arrived([self.share_copies(ref, sems, bit, bits) for ref, sems in refs])

    def share_wait(self, refs, far):
        for bits in range(far, far + self.N // 2, 2):
            self.arrived([self.share_copies(ref, sems, 1, bits) for ref, sems in refs])

    def captions_loop(self, far, step):
        @pl.loop(0, self.groups // 2)
        def _(i):
            bits = far + lax.div(i, self.count)
            step(self.owner(bits) * self.count + lax.rem(i, self.count))

    def merge_slot(self, bit, bits):
        return self.N - self.N // bit + bits // (2 * bit)

    def merge_copies(self, refs, bit, bits):
        slot = self.merge_slot(bit, bits)
        owner = self.captions_of(self.owner(bits + bit))
        return [
            self.copy(ref.at[owner], there.at[slot], sems, slot, self.partner(bit))
            for ref, there, sems in refs
        ]

    def merge_steps(self):
        bit = 1
        while bit < self.N:
            yield bit, range(0, self.N, 2 * bit)
            bit *= 2

    def merge_start(self, refs, group, far):
        for bits in range(far, far + self.N // 2, 2):
            self.start(self.merge_copies(refs, 1, bits), group)

    def merge_part(self, refs, join, bit, bits, group):
        self.arrived(self.merge_copies(refs, bit, bits))
        for j in range(self.count):
            join(self.owner(bits) * self.count + j, self.merge_slot(bit, bits), j)
        if bits % (4 * bit):
            self.start(self.merge_copies(refs, 2 * bit, bits - 2 * bit), group)

    def merge_far(self, refs, join, group):
        for bit, kept in self.merge_steps():
            for bits in reversed(kept):
                if bits:
                    self.merge_part(refs, join, bit, bits, group)

    def merge_own(self, refs, join, group, steps):
        for bit, kept in self.merge_steps():
            if bit in steps:
                self.merge_part(refs, join, bit, 0, group)

    def column(self, turned, p):
        return jnp.where(self.is_first, turned[:64, p : p + 1], turned[64:, p : p + 1])

    def turn(self, *rows):
        have = 8 * len(rows)
        return jnp.concatenate([*rows, jnp.zeros((128 - have, 128), F32)], axis=0).T

    def join_softmax(self, place, slot, j):
        total_a, top_a = self.ST[place, :8], self.ST[place, 8:]
        total_b, top_b = self.STR[slot, j, :8], self.STR[slot, j, 8:]
        top = jnp.maximum(top_a, top_b)
        share_a, share_b = jnp.exp(top_a - top), jnp.exp(top_b - top)
        self.ST[place, :8] = share_a * total_a + share_b * total_b
        self.ST[place, 8:] = top
        turned = self.turn(share_a, share_b)
        for p in range(self.pairs):
            at = slice(128 * p, 128 * p + 128)
            a = self.NUM[place, :, at].astype(F32) * self.column(turned, p)
            b = self.NUMR[slot, j, :, at].astype(F32) * self.column(turned, 8 + p)
            self.NUM[place, :, at] = (a + b).astype(LOW)

    def join_sum(self, place, slot, j):
        self.add_into(self.NUM.at[place], self.NUMR[slot, j])

    def attended(self):
        done = []
        for j in range(self.count):
            place = self.nar * self.count + j
            turned = self.turn(1.0 / self.ST[place, :8])
            self.SCT[j] = turned
            parts = []
            for p in range(self.pairs):
                at = slice(128 * p, 128 * p + 128)
                parts.append(self.NUM[place, :, at].astype(F32) * self.column(turned, p))
            done.append(jnp.concatenate(parts, axis=1))
        return jnp.concatenate(done, axis=0)

    def spread_grad(self, doc):
        lane = lax.broadcasted_iota(jnp.int32, (128, 128), 1)
        for j in range(self.count):
            place = self.nar * self.count + j
            rows = slice(64 * j, 64 * j + 64)
            turned = self.SCT[j]
            inner = jnp.zeros((128, 128), F32)
            for p in range(self.pairs):
                at = slice(128 * p, 128 * p + 128)
                part = doc[rows, at] * self.column(turned, p)
                self.GA[place, :, at] = part.astype(LOW)
                prod = part * self.OCF[rows, at]
                a = jnp.sum(jnp.where(self.is_first, prod, 0.0), axis=1, keepdims=True)
                b = jnp.sum(jnp.where(self.is_first, 0.0, prod), axis=1, keepdims=True)
                inner = jnp.where(lane == p, jnp.concatenate([a, b], axis=0), inner)
            self.DL[place, :8] = -inner.T[:8]
            self.DL[place, 8:] = self.ST[place, 8:]

    def weight_images(self):
        return pltpu.make_async_copy(self.images, self.IMG, self.s_image[0].at[0])

    def keep_wide(self, ref, value, sems):
        ref[self.c, self.x] = value
        here = ref.at[self.c, self.x]
        self.start([self.copy(here, here, sems, 0, self.x_peer())])
        self.start([self.copy(here, here, sems, 1, self.sibling())])

    def wide_across(self, ref, sems):
        here = ref.at[self.c, self.x]
        self.copy(here, here, sems, 0, self.x_peer()).wait_recv()
        here = ref.at[self.c, 1 - self.x]
        self.start([self.copy(here, here, sems, 2, self.sibling())])

    def wide_arrived(self, ref, sems):
        for i in (1, 2):
            here = ref.at[self.c, self.x]
            self.copy(here, here, sems, i, self.sibling()).wait_recv()

    def hidden_copy(self, ref, j, sems):
        here = ref.at[j, self.c]
        return self.copy(here, here, sems, j, self.sibling())

    def fold_copy(self, which):
        return self.copy(self.FS.at[which], self.FR.at[which], self.s_fold, which, self.x_peer())

    def image_copy(self, back):
        src, dst = (self.IMG, self.image_grad) if back else (self.images, self.IMG)
        return pltpu.make_async_copy(src, dst, self.s_image[0].at[0])

    def both_halves(self, value):
        low, high = value[: self.tokens], value[self.tokens :]
        west = self.x == 0
        return jnp.where(west, low, high), jnp.where(west, high, low)

    def do_begin(self):
        self.image_copy(False).start()
        self.pair_pack()
        self.enter()
        self.start(self.pair_copies())
        rows = [getattr(self, name)[...].astype(F32) for name in VECTORS]
        rows = jnp.concatenate(rows + [jnp.zeros((2, rows[0].shape[1]), F32)], axis=0)
        self.sum_start(0, 0, mm(rows.astype(LOW), self.placement(LOW, rows.shape[1])))
        self.pair_merge()
        self.inputs = self.captions[...].astype(F32)
        self.queries = [(self.QA, self.s_query)]
        self.numbers = [(self.NUM, self.NUMR, self.s_num), (self.ST, self.STR, self.s_st)]
        self.grads = [(self.GA, self.s_g), (self.DL, self.s_dl)]
        self.back = [(self.NUM, self.NUMR, self.s_dq)]

    def do_up0(self):
        self.start(self.up_copies(), "up")

    def do_vec(self, stage):
        self.sum_start(0, stage, self.sum_end(0, stage - 1))

    def do_g0(self):
        self.keep_wide(self.G4, self.out_grad[...], self.s_g4)

    def do_g1(self):
        self.wide_across(self.G4, self.s_g4)

    def do_mem(self, which):
        if "images" not in self.here:
            self.here.add("images")
            self.image_copy(False).wait()
        self.done(CK + which)
        self.memory_forward(which)

    def do_a1(self):
        vectors = self.sum_end(0, 3)
        self.gains = [vectors[i : i + 1] for i in (0, 2, 4)]
        self.shifts = [vectors[i : i + 1] for i in (1, 3, 5)]
        self.rstds = [None] * 3
        self.a1 = self.normed(0, self.inputs)
        self.keep_left(0, self.a1)

    def normed(self, which, value):
        hat, self.rstds[which], out = norm(value, self.gains[which], self.shifts[which])
        self.HAT[which] = hat
        return out.astype(LOW)

    def pulled(self, which, grad):
        return norm_pull(grad, self.HAT[which], self.rstds[which], self.gains[which])

    def do_qkv(self, which):
        self.done(which)
        self.QKV[which] = mm(self.a1, self.weight(which)).astype(LOW)

    def do_sa(self):
        self.mixed = self.self_attention()
        self.keep_left(1, self.mixed)

    def do_r1(self):
        self.done(SO)
        self.r1 = self.inputs + mm(self.mixed, self.weight(SO))
        self.a2 = self.normed(1, self.r1)
        self.keep_left(2, self.a2)

    def do_cq(self):
        self.done(CQ)
        query = mm(self.a2, self.weight(CQ)).astype(LOW)
        self.QA[self.captions_of(self.nar)] = query.reshape(self.count, 64, self.width)
        self.share_start(self.queries)

    def do_q1(self):
        self.share_pass(self.queries)

    def do_cf(self, far):
        far = far * self.N // 2
        self.share_wait(self.queries, far)
        self.captions_loop(far, self.cross_forward)
        self.merge_start(self.numbers, "numbers", far)

    def do_m1(self):
        self.merge_far(self.numbers, self.join_softmax, "numbers")

    def do_m2(self):
        self.merge_own(self.numbers, self.join_softmax, "numbers", (1,))

    def do_a3(self):
        steps = [2**i for i in range(1, self.N.bit_length() - 1)]
        self.merge_own(self.numbers, self.join_softmax, "numbers", steps)
        full = self.attended()
        self.OCF[...] = full
        oc = full.astype(LOW)
        self.keep_left(3, oc)
        self.done(CO)
        self.r2 = self.r1 + mm(oc, self.weight(CO))
        self.keep_wide(self.A3, self.normed(2, self.r2), self.s_a3)

    def do_x1(self):
        self.wide_across(self.A3, self.s_a3)

    def do_hp(self):
        self.done(UP)
        a3 = self.A3[self.c].reshape(2 * self.tokens, self.width)
        for j in range(2):
            hidden = mm(a3, self.weight(UP + j))
            square = hidden * hidden
            tanh = jnp.tanh(GELU_A * hidden * (1.0 + GELU_B * square))
            act = (0.5 * hidden * (1.0 + tanh)).astype(LOW)
            self.SLOPE[j] = 0.5 * (1.0 + tanh) + 0.5 * hidden * (1.0 - tanh * tanh) * (
                GELU_A * (1.0 + 3.0 * GELU_B * square)
            )
            self.U[j, self.c] = act.reshape(2, self.tokens, self.width)
            self.start([self.hidden_copy(self.U, j, self.s_u)])

    def do_dg(self):
        self.wide_arrived(self.G4, self.s_g4)
        for j in range(2):
            self.hidden_copy(self.U, j, self.s_u).wait_recv()
        self.down_grad()

    def do_e3(self):
        self.done(DOWN)
        self.done(DOWN + 1)
        grad = self.G4[self.c].reshape(2 * self.tokens, self.width)
        e3 = 0.0
        for j in range(2):
            down = [self.HD[i, 2 * j : 2 * j + 2].reshape(self.width, 384) for i in range(2)]
            back = mm_bt(grad[:, :384], down[0]) + mm_bt(grad[:, 384:], down[1])
            dhp = (back * self.SLOPE[j]).astype(LOW)
            self.DH[j, self.c] = dhp.reshape(2, self.tokens, self.width)
            self.start([self.hidden_copy(self.DH, j, self.s_dh)])
            e3 = e3 + mm_bt(dhp, self.weight(UP + j))
        self.e3, other = self.both_halves(e3)
        self.FS[0] = other.astype(LOW)
        self.start([self.fold_copy(0)])

    def do_out(self):
        out = [0.0, 0.0]
        for j in range(2):
            act = self.U[j, self.c].reshape(2 * self.tokens, self.width)
            for i in range(2):
                down = self.HD[i, 2 * j : 2 * j + 2].reshape(self.width, 384)
                out[i] = out[i] + mm(act, down)
        own, other = self.both_halves(jnp.concatenate(out, axis=1))
        self.out = self.r2 + own
        self.FS[1] = other.astype(LOW)
        self.start([self.fold_copy(1)])

    def do_lo(self):
        self.fold_copy(1).wait_recv()
        self.layer_out[...] = (self.out + self.FR[1].astype(F32)).astype(LOW)

    def do_ug(self):
        self.wide_arrived(self.A3, self.s_a3)
        for j in range(2):
            self.hidden_copy(self.DH, j, self.s_dh).wait_recv()
        self.up_grad()

    def do_dr2(self):
        self.fold_copy(0).wait_recv()
        back, *self.vec3 = self.pulled(2, self.e3 + self.FR[0].astype(F32))
        self.dr2 = self.out_grad[...].astype(F32) + back
        dcat = self.dr2.astype(LOW)
        self.keep_right(5, dcat)
        self.spread_grad(mm_bt(dcat, self.weight(CO)))
        self.share_start(self.grads)

    def do_p1(self):
        self.share_pass(self.grads)

    def do_cb(self, far):
        far = far * self.N // 2
        self.share_wait(self.grads, far)
        self.sent("numbers")
        self.captions_loop(far, self.cross_backward)
        self.merge_start(self.back, "back", far)

    def do_n1(self):
        self.merge_far(self.back, self.join_sum, "back")

    def do_n2(self):
        self.merge_own(self.back, self.join_sum, "back", (1,))

    def do_dq(self):
        steps = [2**i for i in range(1, self.N.bit_length() - 1)]
        self.merge_own(self.back, self.join_sum, "back", steps)
        dqc = self.NUM[self.captions_of(self.nar)].reshape(self.tokens, self.width)
        self.keep_right(4, dqc)
        back, *self.vec2 = self.pulled(1, mm_bt(dqc, self.weight(CQ)))
        self.dr1 = self.dr2 + back
        dattn = self.dr1.astype(LOW)
        self.keep_right(3, dattn)
        self.dos = mm_bt(dattn, self.weight(SO)).astype(LOW)

    def do_mo(self, which):
        self.memory_grad_other(which)

    def do_mw(self, which):
        self.memory_grad_own(which)

    def do_wg(self, unit):
        self.weight_grad(unit)

    def do_sb(self):
        e1 = 0.0
        for j, item in enumerate(self.self_attention_back(self.dos)):
            self.keep_right(j, item)
            e1 = e1 + mm_bt(item, self.weight(j))
        back, *vec = self.pulled(0, e1)
        self.input_grad[...] = (self.dr1 + back).astype(LOW)
        vec = vec + self.vec2 + self.vec3 + [jnp.zeros((2, self.width), F32)]
        self.sum_start(1, 0, jnp.concatenate(vec, axis=0))

    def do_sum(self, stage):
        self.sum_start(1, stage, self.sum_end(1, stage - 1))

    def do_img(self):
        @pl.loop(0, 3)
        def _(t):
            size = self.images.shape[0] // 3
            rows = pl.ds(pl.multiple_of(size * t, 16), size)
            part = mm_bt(self.KV[0, rows], self.weight(CK))
            part = part + mm_bt(self.KV[1, rows], self.weight(CV))
            self.IMG[rows] = part.astype(LOW)

        self.image_copy(True).start()

    def do_end(self):
        self.vec_grad[...] = lax.dot_general(
            self.sum_end(1, 3),
            self.placement(F32, 128),
            (((1,), (1,)), ((), ())),
            precision=lax.Precision.HIGHEST,
            preferred_element_type=F32,
        )
        for unit in range(UNITS):
            self.rs_done(unit)
        self.image_copy(True).wait()
        for group in list(self.started):
            self.sent(group)

    def run(self):
        steps = {
            Step.begin: self.do_begin,
            Step.up0: self.do_up0,
            Step.vec: self.do_vec,
            Step.g0: self.do_g0,
            Step.g1: self.do_g1,
            Step.mem: self.do_mem,
            Step.a1: self.do_a1,
            Step.qkv: self.do_qkv,
            Step.sa: self.do_sa,
            Step.r1: self.do_r1,
            Step.cq: self.do_cq,
            Step.q1: self.do_q1,
            Step.cf: self.do_cf,
            Step.m1: self.do_m1,
            Step.m2: self.do_m2,
            Step.a3: self.do_a3,
            Step.x1: self.do_x1,
            Step.hp: self.do_hp,
            Step.dg: self.do_dg,
            Step.e3: self.do_e3,
            Step.out: self.do_out,
            Step.lo: self.do_lo,
            Step.ug: self.do_ug,
            Step.dr2: self.do_dr2,
            Step.p1: self.do_p1,
            Step.cb: self.do_cb,
            Step.n1: self.do_n1,
            Step.n2: self.do_n2,
            Step.dq: self.do_dq,
            Step.mo: self.do_mo,
            Step.mw: self.do_mw,
            Step.wg: self.do_wg,
            Step.sb: self.do_sb,
            Step.sum: self.do_sum,
            Step.img: self.do_img,
            Step.end: self.do_end,
            Step.F: self.first,
            Step.S: self.second,
            Step.TA: lambda unit: self.third(unit, 0),
            Step.TB: lambda unit: self.third(unit, 1),
            Step.H: self.hand,
            Step.R1: self.rs_one,
            Step.RA: self.rs_two,
            Step.RB: lambda unit: self.rs_two(unit, 1),
            Step.R3: self.rs_three,
            Step.R4: self.rs_four,
            Step.RU: lambda unit: self.rs_up(),
        }
        for step, *place in ORDER:
            steps[step](*place)


def layer_call(lanes, narrow, captions, images, lengths, out_grad, *params):
    tokens, width = captions.shape
    count = tokens // 64
    groups = narrow * count
    image_rows = images.shape[0]
    pairs = width // 128
    ins = ["captions", "images", "lengths", "out_grad", "self_proj", "self_output"]
    ins += ["cross_query", "cross_memory", "cross_output", "hidden_up", "hidden_down", *VECTORS]
    outs = {
        "layer_out": ((tokens, width), LOW),
        "input_grad": ((tokens, width), LOW),
        "image_grad": ((image_rows, width), LOW),
        "block_grad": ((24, 12 * width), F32),
        "down_out": ((96, width), F32),
        "vec_grad": ((8, 128), F32),
    }
    memory = {
        "W": ((10, 4, 2, 2, 48, width), LOW),
        "HD": ((2, 4, 2, 192, 384), LOW),
        "HG": ((4, 2, 192, 384), LOW),
        "UPS": ((48, width), LOW),
        "UPR": ((48, width), LOW),
        "PA": ((2, 24 * UP, 384), LOW),
        "PB": ((2, 48, width), LOW),
        "IMG": ((image_rows, width), LOW),
        "KV": ((2, image_rows, width), LOW),
        "E": ((groups, pairs // 2, image_rows // groups, 256), LOW),
        "LHS": ((4, 2, tokens, width), LOW),
        "RHS": ((6, 2, tokens, width), LOW),
        "A3": ((2, 2, tokens, width), LOW),
        "G4": ((2, 2, tokens, width), LOW),
        "U": ((2, 2, 2, tokens, width), LOW),
        "DH": ((2, 2, 2, tokens, width), LOW),
        "FS": ((2, tokens, width), LOW),
        "FR": ((2, tokens, width), LOW),
        "R1": ((UP, 4, 2, 48, 384), LOW),
        "R2": ((UP, 4, 48, 384), LOW),
        "R3": ((UP, 3, 48, 384), LOW),
        "RU1": ((4, 2, 48, width), LOW),
        "RU3": ((3, 2, 48, width), LOW),
        "RH1": ((4, 96, 384), LOW),
        "RH3": ((3, 96, 384), LOW),
        "RL1": ((96, 384), LOW),
        "RL3": ((3, 2, 96, 384), LOW),
        "CM": ((2, 4, 2, 2, 48, 384), LOW),
        "CS": ((2, 4, 2, 2, 48, 384), LOW),
        "CP": ((2, 4, 2, 2, 48, 384), LOW),
        "SF": ((UP, 24, 384), F32),
        "SFU": ((2, 24, width), F32),
        "UPG": ((2, 24, 2 * width), F32),
        "SFH": ((96, 384), F32),
        "V": ((2, 4, 8, width), F32),
        "VR": ((2, 6, 8, width), F32),
        "QKV": ((3, tokens, width), LOW),
        "PS": ((HEADS // 2, 128, 256), F32),
        "HAT": ((3, tokens, width), F32),
        "SLOPE": ((2, 2 * tokens, width), F32),
        "OCF": ((tokens, width), F32),
        "QA": ((groups, 64, width), LOW),
        "NUM": ((groups, 64, width), LOW),
        "ST": ((groups, 16, 128), F32),
        "TOP": ((groups, 8, 128), F32),
        "NUMR": ((narrow - 1, count, 64, width), LOW),
        "STR": ((narrow - 1, count, 16, 128), F32),
        "SCT": ((count, 128, 128), F32),
        "GA": ((groups, 64, width), LOW),
        "DL": ((groups, 16, 128), F32),
    }
    signals = {
        "s_pair": (3,),
        "s_up": (2,),
        "s_z": (UNITS, 3),
        "s_two": (UP, 2),
        "s_three": (UNITS, 2),
        "s_hand": (UNITS,),
        "s_rs1": (UNITS, 2),
        "s_rs2": (UP, 2),
        "s_rs3": (UNITS, 3),
        "s_rs4": (UNITS,),
        "s_rs5": (2,),
        "s_vec": (2, 6),
        "s_left": (4,),
        "s_right": (6,),
        "s_a3": (3,),
        "s_g4": (3,),
        "s_u": (2,),
        "s_dh": (2,),
        "s_fold": (2,),
        "s_memory": (2,),
        "s_query": (narrow - 1,),
        "s_num": (narrow - 1,),
        "s_st": (narrow - 1,),
        "s_g": (narrow - 1,),
        "s_dl": (narrow - 1,),
        "s_dq": (narrow - 1,),
        "s_image": (1,),
    }
    scratch = [pltpu.VMEM(shape, kind) for shape, kind in memory.values()]
    for shape in signals.values():
        scratch += [pltpu.SemaphoreType.DMA(shape)] * 2

    def body(*refs):
        named = dict(zip(ins + list(outs) + list(memory), refs))
        rest = refs[len(named) :]
        for i, name in enumerate(signals):
            named[name] = (rest[2 * i], rest[2 * i + 1])
        Layer(named, lanes, narrow).run()

    vmem = pl.BlockSpec(memory_space=pltpu.VMEM)
    in_specs = [vmem] * len(ins)
    in_specs[1] = pl.BlockSpec(memory_space=pl.ANY)
    in_specs[2] = pl.BlockSpec(memory_space=pltpu.SMEM)
    out_specs = [vmem] * len(outs)
    out_specs[2] = pl.BlockSpec(memory_space=pl.ANY)
    return pl.pallas_call(
        body,
        out_shape=[jax.ShapeDtypeStruct(shape, kind) for shape, kind in outs.values()],
        in_specs=in_specs,
        out_specs=out_specs,
        scratch_shapes=scratch,
        compiler_params=pltpu.CompilerParams(
            collective_id=0, has_side_effects=True, vmem_limit_bytes=VMEM_LIMIT
        ),
        cost_estimate=pl.CostEstimate(
            flops=17 * 10**9, bytes_accessed=8 * 10**6, transcendentals=2 * 10**6
        ),
        name="layer",
    )(captions, images, lengths, out_grad, *params)


def deliver(ranges, arrays, block_grad, vec_grad, own):
    count = len(arrays)
    outs = [jax.ShapeDtypeStruct(item.shape, item.dtype) for item in arrays]
    outs += [jax.ShapeDtypeStruct((block_grad.shape[0], b - a), F32) for a, b in ranges]
    rows = [jax.ShapeDtypeStruct((1, own), F32)] * len(VECTORS)

    def body(*refs):
        ins, vec, rest = refs[: count + 1], refs[count + 1], refs[count + 2 :]
        found, rest = rest[: len(outs)], rest[len(outs) :]
        vectors, held, sems = rest[: len(rows)], rest[len(rows) : -1], rest[-1]
        into = [pltpu.make_async_copy(a, b, sems.at[i]) for i, (a, b) in enumerate(zip(ins, held))]
        views = [*held[:count], *[held[count].at[:, pl.ds(a, b - a)] for a, b in ranges]]
        back = [
            pltpu.make_async_copy(a, b, sems.at[count + 1 + i])
            for i, (a, b) in enumerate(zip(views, found))
        ]
        for item in into:
            item.start()
        for i, ref in enumerate(vectors):
            ref[...] = vec[i : i + 1, :own]
        for i, item in enumerate(into):
            item.wait()
            for out in back[i : i + 1] if i < count else back[count:]:
                out.start()
        for out in back:
            out.wait()

    vmem = pl.BlockSpec(memory_space=pltpu.VMEM)
    hold = [pltpu.VMEM(item.shape, item.dtype) for item in (*arrays, block_grad)]
    return pl.pallas_call(
        body,
        out_shape=outs + rows,
        in_specs=[pl.BlockSpec(memory_space=pl.ANY)] * (count + 1) + [vmem],
        out_specs=[pl.BlockSpec(memory_space=pl.ANY)] * len(outs) + [vmem] * len(rows),
        scratch_shapes=hold + [pltpu.SemaphoreType.DMA((count + 1 + len(outs),))],
        compiler_params=pltpu.CompilerParams(vmem_limit_bytes=VMEM_LIMIT),
        name="deliver",
    )(*arrays, block_grad, vec_grad)


def lane_gather(value, lanes, narrow, axis):
    if lanes == 1:
        return value
    assert lanes % narrow == 0
    value = lax.all_gather(value, "narrow", axis=axis, tiled=True)
    step = 1
    wide_count = lax.axis_size("wide")
    while step * narrow < lanes:
        swap = [(i, i ^ step) for i in range(wide_count)]
        other = lax.ppermute(value, "wide", swap)
        low = (lax.axis_index("wide") // step) % 2 == 0
        first = jnp.where(low, value, other)
        second = jnp.where(low, other, value)
        value = jnp.concatenate([first, second], axis=axis)
        step *= 2
    return value


def lane_scatter(value, lanes, narrow, axis):
    if lanes == 1:
        return value
    wide_count = lax.axis_size("wide")
    step = lanes // narrow
    while step > 1:
        step //= 2
        swap = [(i, i ^ step) for i in range(wide_count)]
        first, second = jnp.split(value, 2, axis=axis)
        low = (lax.axis_index("wide") // step) % 2 == 0
        other = lax.ppermute(jnp.where(low, second, first), "wide", swap)
        value = jnp.where(low, first, second) + other
    return lax.psum_scatter(value, "narrow", scatter_dimension=axis, tiled=True)


def per_device(captions, images, lengths, out_grad, *params):
    narrow = lax.axis_size("narrow")
    devices = lax.axis_size("wide") * narrow
    lanes = devices // NODES
    count, seq_len, width = captions.shape
    tokens = count * seq_len
    params = [lane_gather(item, lanes, narrow, 0) for item in params]
    out, input_grad, image_grad, block_grad, down_grad, vec_grad = layer_call(
        lanes,
        narrow,
        captions.reshape(tokens, width),
        images.reshape(-1, width),
        lengths,
        out_grad.reshape(tokens, width),
        *params[:7],
        *[item.reshape(1, -1) for item in params[7:]],
    )
    block_grad = lane_scatter(block_grad, lanes, narrow, 0)
    down_grad = lane_scatter(down_grad, lanes, narrow, 0)
    if lanes > 1:
        vec_grad = lane_scatter(vec_grad[:, : width // NODES], lanes, narrow, 1)

    ends = (QS, SO, CK, CQ, CO, UP, UP + 4)
    ranges = [(width * a, width * b) for a, b in zip(ends, ends[1:])]
    arrays = [out, input_grad, image_grad, down_grad]
    own = width // devices
    found = deliver(ranges, arrays, block_grad, vec_grad, own)
    out, input_grad, image_grad, down_grad = found[:4]
    joint, self_out, memory, query, cross, up = found[4:10]
    return (
        out.reshape(captions.shape),
        input_grad.reshape(captions.shape),
        image_grad.reshape(images.shape),
        joint,
        self_out,
        query,
        memory,
        cross,
        up,
        down_grad,
        *[item.reshape(-1) for item in found[10:]],
    )


def solution(mesh):
    both = ("wide", "narrow")
    rows = P(both, None)
    text = P(both, None, None)
    vector = P(both)
    image = P("wide", "narrow", None)
    in_specs = (text, image, vector, text) + (rows,) * 7 + (vector,) * 6
    out_specs = (text, text, image) + (rows,) * 7 + (vector,) * 6
    return jax.shard_map(
        per_device, mesh=mesh, in_specs=in_specs, out_specs=out_specs, check_vma=False
    )
```

```python
import functools

import jax
import jax.numpy as jnp
from jax import lax
from jax.experimental import pallas as pl
from jax.experimental.pallas import tpu as pltpu
from jax.sharding import PartitionSpec as P

HEADS = 12
NODES = 32
UNITS = 11
VMEM_LIMIT = 64 * 1024 * 1024 - 65536
MESH = pl.DeviceIdType.MESH
F32 = jnp.float32
LOW = jnp.bfloat16
EPSILON = 1e-05
GELU_A = 0.7978845608028654
GELU_B = 0.044715

QS, KS, VS, SO, CK, CV, CQ, CO, UP = 0, 1, 2, 3, 4, 5, 6, 7, 8
DOWN = UP + 1
LATE = DOWN + 1
GATHER = (128, 256) * 4
SCATTER = (256, 128) * 4


VECTORS = ["first_gain", "first_shift", "second_gain", "second_shift"]
VECTORS += ["third_gain", "third_shift"]


class Step:
    (
        begin,
        up0,
        vec,
        g0,
        g1,
        mem,
        a1,
        qkv,
        sa,
        r1,
        cq,
        q1,
        cf,
        m1,
        m2,
        a3,
        x1,
        hp,
        dg,
        e3,
        out,
        lo,
        ug,
        dr2,
        p1,
        cb,
        n1,
        n2,
        dq,
        mo,
        mw,
        wg,
        sb,
        sum,
        img,
        end,
        F,
        S,
        TA,
        TB,
        H,
        R1,
        RA,
        RB,
        R3,
        R4,
        RU,
    ) = range(47)


ORDER = [
    (Step.begin,), (Step.F, 1), (Step.up0,), (Step.vec, 1), (Step.g0,), (Step.F, 0), (Step.vec, 2),
    (Step.F, 3), (Step.S, 1), (Step.F, 2), (Step.S, 0), (Step.F, 5), (Step.TA, 1), (Step.vec, 3),
    (Step.S, 3), (Step.TA, 0), (Step.F, 6), (Step.TB, 0), (Step.S, 2), (Step.F, 4), (Step.TA, 3),
    (Step.S, 5), (Step.TB, 1), (Step.F, 7), (Step.F, 8), (Step.S, 6), (Step.TB, 2), (Step.TA, 2),
    (Step.S, 4), (Step.TA, 6), (Step.TB, 3), (Step.H, 1), (Step.a1,), (Step.qkv, 1), (Step.H, 0),
    (Step.TB, 5), (Step.TA, 5), (Step.TA, 4), (Step.qkv, 0), (Step.F, 10), (Step.H, 2),
    (Step.TB, 6), (Step.qkv, 2), (Step.sa,), (Step.TB, 4), (Step.H, 3), (Step.r1,), (Step.F, 9),
    (Step.H, 6), (Step.S, 8), (Step.g1,), (Step.S, 7), (Step.H, 5), (Step.S, 10), (Step.cq,),
    (Step.H, 4), (Step.mem, 1), (Step.mem, 0), (Step.cf, 0), (Step.q1, 0), (Step.cf, 3),
    (Step.cf, 6), (Step.q1, 1), (Step.TA, 7), (Step.TB, 7), (Step.cf, 4), (Step.cf, 2),
    (Step.cf, 7), (Step.m1, 0), (Step.cf, 5), (Step.H, 8), (Step.m2, 0), (Step.m1, 1), (Step.H, 7),
    (Step.S, 9), (Step.cf, 1), (Step.a3, 0), (Step.m2, 1), (Step.a3, 1), (Step.H, 10),
    (Step.x1, 0), (Step.H, 9), (Step.x1, 1), (Step.hp,), (Step.e3,), (Step.dg,), (Step.R1, 10),
    (Step.R1, 9), (Step.ug,), (Step.dr2, 0), (Step.R1, 8), (Step.dr2, 1), (Step.cb, 0),
    (Step.RA, 9), (Step.out,), (Step.cb, 3), (Step.p1, 0), (Step.wg, 7), (Step.cb, 1),
    (Step.cb, 2), (Step.p1, 1), (Step.R1, 7), (Step.cb, 6), (Step.cb, 5), (Step.cb, 7),
    (Step.n1, 1), (Step.cb, 4), (Step.n2, 1), (Step.mo, 0), (Step.n2, 0), (Step.n1, 0),
    (Step.RB, 7), (Step.mo, 1), (Step.mw, 0), (Step.R1, 4), (Step.RA, 7), (Step.mw, 1),
    (Step.R1, 5), (Step.RA, 8), (Step.dq,), (Step.sb,), (Step.wg, 3), (Step.R1, 3), (Step.wg, 1),
    (Step.RB, 4), (Step.R3, 7), (Step.wg, 2), (Step.R1, 2), (Step.sum, 1), (Step.RA, 3),
    (Step.RB, 5), (Step.wg, 0), (Step.RA, 5), (Step.R1, 0), (Step.RA, 4), (Step.RB, 2),
    (Step.RA, 2), (Step.sum, 2), (Step.R3, 5), (Step.R1, 1), (Step.R4, 8), (Step.R3, 4),
    (Step.RB, 0), (Step.RA, 10), (Step.wg, 6), (Step.RB, 3), (Step.sum, 3), (Step.R1, 6),
    (Step.R4, 5), (Step.R3, 2), (Step.RA, 1), (Step.RA, 0), (Step.R4, 9), (Step.RB, 1),
    (Step.R3, 3), (Step.R4, 2), (Step.R3, 0), (Step.RA, 6), (Step.RB, 6), (Step.R3, 1),
    (Step.R4, 4), (Step.img,), (Step.R3, 6), (Step.R4, 3), (Step.R4, 1), (Step.R4, 7),
    (Step.R4, 0), (Step.lo,), (Step.RU, 8), (Step.R4, 6), (Step.end,),
]


def mm(left, right):
    return jnp.dot(left, right, preferred_element_type=F32)


def mm_bt(left, right):
    return lax.dot_general(left, right, (((1,), (1,)), ((), ())), preferred_element_type=F32)


def mm_at(left, right):
    return lax.dot_general(left, right, (((0,), (0,)), ((), ())), preferred_element_type=F32)


def norm(value, gain, shift):
    centred = value - jnp.mean(value, axis=-1, keepdims=True)
    rstd = lax.rsqrt(jnp.mean(centred * centred, axis=-1, keepdims=True) + EPSILON)
    hat = centred * rstd
    return hat, rstd, hat * gain + shift


def norm_pull(grad, hat, rstd, gain):
    scaled = grad * gain
    inner = jnp.mean(scaled * hat, axis=-1, keepdims=True)
    back = rstd * (scaled - jnp.mean(scaled, axis=-1, keepdims=True) - hat * inner)
    gain_grad = jnp.sum(grad * hat, axis=0, keepdims=True)
    shift_grad = jnp.sum(grad, axis=0, keepdims=True)
    return back, gain_grad, shift_grad


class Layer:
    def __init__(self, refs, lanes, narrow):
        self.__dict__.update(refs)
        self.N = narrow
        self.lanes = lanes
        wide, nar = lax.axis_index("wide"), lax.axis_index("narrow")
        flat = wide * narrow + nar
        self.wide, self.nar = wide, nar
        self.node = lax.div(flat, lanes)
        self.lane = lax.rem(flat, lanes)
        node = self.node
        self.c = lax.rem(node, 2)
        self.x = lax.rem(lax.div(node, 2), 2)
        self.y = lax.rem(lax.div(node, 4), 2)
        self.z = lax.div(node, 8)
        self.started = {}
        self.here = set()
        self.count, self.seq = self.captions.shape[0] // 64, 64
        self.tokens, self.width = self.captions.shape
        self.groups = self.QA.shape[0]
        self.image_rows = self.IMG.shape[0] // self.groups
        self.pairs = self.width // 128
        lane = lax.broadcasted_iota(jnp.int32, (1, 128), 1)
        self.low_lanes = (lane < 64).astype(F32).astype(LOW)
        self.high_lanes = (lane >= 64).astype(F32).astype(LOW)
        self.is_first = lane < 64

    def device(self, z, y, x, c):
        flat = (z * 8 + y * 4 + x * 2 + c) * self.lanes + self.lane
        return (lax.div(flat, self.N), lax.rem(flat, self.N))

    def sibling(self):
        return self.device(self.z, self.y, self.x, 1 - self.c)

    def x_peer(self):
        return self.device(self.z, self.y, 1 - self.x, self.c)

    def y_peer(self):
        return self.device(self.z, 1 - self.y, self.x, self.c)

    def z_index(self, k):
        return lax.rem(self.z + k, 4)

    def z_peer(self, k):
        return self.device(self.z_index(k), self.y, self.x, self.c)

    def n_index(self, k):
        return lax.rem(self.nar + k, self.N)

    def n_peer(self, k):
        return (self.wide, self.n_index(k))

    def enter(self):
        barrier = pltpu.get_barrier_semaphore()
        peers = [self.sibling(), self.x_peer(), self.y_peer()]
        peers += [self.z_peer(k) for k in (1, 2, 3)]
        peers += [self.n_peer(k) for k in range(1, self.N)]
        for peer in peers:
            pl.semaphore_signal(barrier, inc=1, device_id=peer, device_id_type=MESH)
        pl.semaphore_wait(barrier, len(peers))

    def copy(self, src, dst, sems, where, peer):
        send, recv = sems
        return pltpu.make_async_remote_copy(
            src_ref=src,
            dst_ref=dst,
            send_sem=send.at[where],
            recv_sem=recv.at[where],
            device_id=peer,
            device_id_type=MESH,
        )

    def start(self, copies, group=None):
        for item in copies:
            item.start()
        self.started.setdefault(group, []).extend(copies)

    def sent(self, group):
        for item in self.started.pop(group, []):
            item.wait_send()

    def part(self, unit, half, z, y, x, grad=False):
        every = slice(None)
        if unit < UP:
            first = (SCATTER if grad else GATHER)[unit]
            low, size = ((0, 384), (0, first), (first, 384 - first))[0 if half is None else half + 1]
            if grad and unit in (CK, CV):
                return self.CP.at[unit - CK, z, y, x, every, pl.ds(low, size)]
            columns = pl.ds(pl.multiple_of(384 * self.c + low, 128), size)
            return self.W.at[unit, z, y, x, every, columns]
        if unit == UP:
            return self.W.at[UP + self.c, z, y, x]
        ref = self.HG if grad else self.HD.at[self.c]
        return ref.at[z, y, pl.ds(96 * (unit - DOWN), 96)]

    def half_columns(self, c):
        return pl.ds(pl.multiple_of(384 * c, 128), 384)

    def shards(self):
        found = [(self.self_proj, self.width * j) for j in range(3)] + [(self.self_output, 0)]
        found += [(self.cross_memory, self.width * j) for j in range(2)]
        return found + [(self.cross_query, 0), (self.cross_output, 0)]

    def half_block(self, block, c):
        ref, start = self.shards()[block]
        return ref[:, pl.ds(pl.multiple_of(start + 384 * c, 128), 384)].astype(F32)

    def swapped(self, value):
        return pltpu.roll(value, 64, 1)

    def split_runs(self, whole):
        n = [whole[:, 128 * i : 128 * i + 128] for i in range(6)]
        r = [self.swapped(item) for item in n]
        low = self.is_first
        a = [n[0], jnp.where(low, n[1], r[3]), jnp.where(low, r[3], r[4])]
        b = [jnp.where(low, r[1], r[2]), jnp.where(low, r[2], n[4]), n[5]]
        return jnp.concatenate(a, axis=1), jnp.concatenate(b, axis=1)

    def join_runs(self, left, right):
        a = [left[:, 128 * i : 128 * i + 128] for i in range(3)]
        b = [right[:, 128 * i : 128 * i + 128] for i in range(3)]
        ra, rb = [self.swapped(item) for item in a], [self.swapped(item) for item in b]
        low = self.is_first
        out = [a[0], jnp.where(low, a[1], rb[0]), jnp.where(low, rb[0], rb[1])]
        out += [jnp.where(low, ra[1], ra[2]), jnp.where(low, ra[2], b[1]), b[2]]
        return jnp.concatenate(out, axis=1)

    def up_blocks(self, c):
        found = []
        for j in range(2):
            start = pl.multiple_of(self.width * (2 * c + j), 128)
            found.append(self.split_runs(self.hidden_up[:, pl.ds(start, self.width)].astype(F32)))
        return [jnp.concatenate(item, axis=1) for item in zip(*found)]

    def pair_copies(self):
        c = self.c
        rows = pl.ds(pl.multiple_of(96 * c, 32), 96)
        there = self.HD.at[1 - c, self.z, self.y, rows]
        down = self.hidden_down.at[:, self.half_columns(1 - c)]
        return [
            self.copy(self.PA.at[0], self.PA.at[1], self.s_pair, 0, self.sibling()),
            self.copy(self.PB.at[0], self.PB.at[1], self.s_pair, 1, self.sibling()),
            self.copy(down, there, self.s_pair, 2, self.sibling()),
        ]

    def pair_pack(self):
        c = 1 - self.c
        blocks = [self.half_block(block, c) for block in range(UP)]
        self.PA[0] = jnp.concatenate(blocks, axis=0).astype(LOW)
        self.PB[0] = jnp.concatenate(self.up_blocks(c), axis=0).astype(LOW)

    def in_order(self, mine, theirs):
        even = self.c == 0
        low, high = jnp.where(even, mine, theirs), jnp.where(even, theirs, mine)
        return jnp.concatenate([low, high], axis=0)

    def pair_merge(self):
        c = self.c
        copies = self.pair_copies()
        rows = pl.ds(pl.multiple_of(96 * c, 32), 96)
        self.HD[c, self.z, self.y, rows] = self.hidden_down[:, self.half_columns(c)]
        columns = pl.ds(pl.multiple_of(384 * c, 128), 384)
        copies[0].wait_recv()
        theirs = self.PA[1].astype(F32)
        for block in range(UP):
            both = self.in_order(self.half_block(block, c), theirs[24 * block : 24 * block + 24])
            self.W[block, self.z, self.y, self.x, :, columns] = both.astype(LOW)
        copies[1].wait_recv()
        theirs = self.PB[1].astype(F32)
        both = [
            self.in_order(mine, theirs[24 * i : 24 * i + 24])
            for i, mine in enumerate(self.up_blocks(c))
        ]
        west = self.x == 0
        self.W[UP + c, self.z, self.y, self.x] = jnp.where(west, both[0], both[1]).astype(LOW)
        self.UPS[...] = jnp.where(west, both[1], both[0]).astype(LOW)
        copies[2].wait_recv()

    def up_copies(self):
        there = self.W.at[UP + self.c, self.z, self.y, self.x]
        return [self.copy(self.UPS, there, self.s_up, 0, self.x_peer())]

    def z_copies(self, unit):
        x = slice(None) if unit == UP else self.x
        y = slice(None) if unit == LATE else self.y
        here = self.part(unit, None, self.z, y, x)
        return [
            self.copy(here, here, self.s_z, (unit, k - 1), self.z_peer(k)) for k in (1, 2, 3)
        ]

    def halves(self, unit, table):
        return range(1 if table[unit] == 384 else 2)

    def two_copy(self, unit, half):
        here = self.part(unit, half, slice(None), self.y, self.x)
        peer = (self.x_peer, self.y_peer)[half]()
        return self.copy(here, here, self.s_two, (unit, half), peer)

    def three_copy(self, unit, half):
        every = slice(None)
        if unit >= UP:
            z = self.z if unit == LATE else every
            here = self.part(unit, None, z, self.y, every)
            return self.copy(here, here, self.s_three, (unit, 0), self.y_peer())
        y, x = ((self.y, every), (every, self.x))[half]
        here = self.part(unit, half, every, y, x)
        peer = (self.y_peer, self.x_peer)[half]()
        return self.copy(here, here, self.s_three, (unit, half), peer)

    def three_copies(self, unit):
        halves = (0,) if unit >= UP else self.halves(unit, GATHER)
        return [self.three_copy(unit, half) for half in halves]

    def hand_copies(self, unit):
        every = slice(None)
        whole = self.part(unit, None, every, every, every)
        return [self.copy(whole, whole, self.s_hand, unit, self.sibling())]

    def arrived(self, copies):
        for item in copies:
            item.wait_recv()

    def first(self, unit):
        if unit == UP:
            self.arrived(self.up_copies())
        self.start(self.three_copies(unit) if unit == LATE else self.z_copies(unit), unit)

    def second(self, unit):
        if unit == LATE:
            self.arrived(self.three_copies(unit))
            self.start(self.z_copies(unit), unit)
            return
        self.arrived(self.z_copies(unit))
        if unit < UP:
            copies = [self.two_copy(unit, half) for half in self.halves(unit, GATHER)]
        else:
            copies = self.three_copies(unit)
        self.start(copies, unit)

    def third(self, unit, half):
        if half in self.halves(unit, GATHER):
            self.arrived([self.two_copy(unit, half)])
            self.start([self.three_copy(unit, half)], unit)

    def hand(self, unit):
        self.arrived(self.z_copies(unit) if unit == LATE else self.three_copies(unit))
        self.start(self.hand_copies(unit), unit)

    def done(self, unit):
        self.arrived(self.hand_copies(unit))

    def term(self, unit, half, z=slice(None)):
        first = SCATTER[unit]
        return (unit, z, ..., pl.ds(*((0, first), (first, 384 - first))[half]))

    def rs_one_copy(self, unit, half):
        every = slice(None)
        if unit == LATE:
            here = self.part(unit, None, self.z, 1 - self.y, every, grad=True)
            return self.copy(here, self.RL1, self.s_rs1, (unit, 0), self.y_peer())
        if unit >= UP:
            here = self.part(unit, None, every, 1 - self.y, every, grad=True)
            there = self.RU1 if unit == UP else self.RH1
            return self.copy(here, there, self.s_rs1, (unit, 0), self.y_peer())
        y, x = ((1 - self.y, every), (every, 1 - self.x))[half]
        here = self.part(unit, half, every, y, x, grad=True)
        there = self.R1.at[self.term(unit, half)]
        peer = (self.y_peer, self.x_peer)[half]()
        return self.copy(here, there, self.s_rs1, (unit, half), peer)

    def rs_two_copy(self, unit, half):
        y, x = ((self.y, 1 - self.x), (1 - self.y, self.x))[half]
        here = self.part(unit, half, slice(None), y, x, grad=True)
        there = self.R2.at[self.term(unit, half)]
        peer = (self.x_peer, self.y_peer)[half]()
        return self.copy(here, there, self.s_rs2, (unit, half), peer)

    def rs_three_copies(self, unit):
        out = []
        x = slice(None) if unit == UP else self.x
        y = slice(None) if unit == LATE else self.y
        for k in (1, 2, 3):
            here = self.part(unit, None, self.z_index(k), y, x, grad=True)
            if unit < UP:
                there = self.R3.at[unit, k - 1]
            elif unit == UP:
                there = self.RU3.at[k - 1]
            else:
                there = (self.RL3 if unit == LATE else self.RH3).at[k - 1]
            out.append(self.copy(here, there, self.s_rs3, (unit, k - 1), self.z_peer(k)))
        return out

    def up_back_copies(self):
        return [self.copy(self.UPS, self.UPR, self.s_up, 1, self.x_peer())]

    def grad_columns(self, block):
        return pl.ds(pl.multiple_of(self.width * block + 384 * self.c, 128), 384)

    def rs_four_copies(self, unit):
        c = self.c
        if unit < UP:
            there = self.block_grad.at[:, self.grad_columns(unit)]
            return [self.copy(self.SF.at[unit], there, self.s_rs4, unit, self.sibling())]
        if unit == UP:
            columns = self.half_columns_up()
            return [
                self.copy(
                    self.SFU.at[i],
                    self.UPG.at[self.up_side(i), :, columns],
                    self.s_rs5,
                    i,
                    self.sibling(),
                )
                for i in range(2)
            ]
        there = self.down_out.at[:, self.half_columns(c)]
        return [self.copy(self.SFH, there, self.s_rs4, unit, self.sibling())]

    def up_side(self, i):
        return self.x if i == 0 else 1 - self.x

    def half_columns_up(self):
        return pl.ds(pl.multiple_of(self.width * self.c, 128), self.width)

    def add_into(self, ref, term):
        ref[...] = (ref[...].astype(F32) + term.astype(F32)).astype(LOW)

    def rs_one(self, unit):
        halves = (0,) if unit >= UP else self.halves(unit, SCATTER)
        if unit == LATE:
            self.start(self.rs_three_copies(unit))
        else:
            self.start([self.rs_one_copy(unit, half) for half in halves])

    def rs_two(self, unit, half=0):
        every = slice(None)
        if unit < UP and half not in self.halves(unit, SCATTER):
            return
        if unit == LATE:
            self.arrived(self.rs_three_copies(unit))
            here = self.part(unit, None, self.z, every, self.x, grad=True)
            here[...] = self.sum_of(here[...], [self.RL3[k] for k in range(3)]).astype(LOW)
            self.start([self.rs_one_copy(unit, 0)])
            return
        self.arrived([self.rs_one_copy(unit, half)])

        @pl.loop(0, 4)
        def _(z):
            if unit < UP:
                y, x = ((self.y, every), (every, self.x))[half]
                more = self.R1[self.term(unit, half, z)]
                self.add_into(self.part(unit, half, z, y, x, grad=True), more)
            else:
                more = self.RU1[z] if unit == UP else self.RH1[z]
                self.add_into(self.part(unit, None, z, self.y, every, grad=True), more)

        if unit < UP:
            self.start([self.rs_two_copy(unit, half)])
        else:
            self.start(self.rs_three_copies(unit))

    def rs_three(self, unit):
        halves = self.halves(unit, SCATTER)
        self.arrived([self.rs_two_copy(unit, half) for half in halves])

        @pl.loop(0, 4)
        def _(z):
            for half in halves:
                more = self.R2[self.term(unit, half, z)]
                self.add_into(self.part(unit, half, z, self.y, self.x, grad=True), more)

        self.start(self.rs_three_copies(unit))

    def sum_of(self, value, terms):
        return sum((item.astype(F32) for item in terms), value.astype(F32))

    def rs_total(self, unit):
        x = slice(None) if unit == UP else self.x
        own = self.part(unit, None, self.z, self.y, x, grad=True)
        if unit == LATE:
            self.arrived([self.rs_one_copy(unit, 0)])
            return self.sum_of(own[...], [self.RL1[...]])
        self.arrived(self.rs_three_copies(unit))
        if unit < UP:
            return self.sum_of(own[...], [self.R3[unit, k] for k in range(3)])
        ref = self.RU3 if unit == UP else self.RH3
        return self.sum_of(own[...], [ref[k] for k in range(3)])

    def rs_four(self, unit):
        even = self.c == 0
        if unit < UP:
            total = self.rs_total(unit)
            low, high = total[:24], total[24:]
            self.block_grad[:, self.grad_columns(unit)] = jnp.where(even, low, high)
            self.SF[unit] = jnp.where(even, high, low)
            self.start(self.rs_four_copies(unit))
        if unit == UP:
            total = self.rs_total(unit)
            west = self.x == 0
            self.sent("up")
            self.UPS[...] = jnp.where(west, total[1], total[0]).astype(LOW)
            self.start(self.up_back_copies())
            self.up_rows(0, jnp.where(west, total[0], total[1]))
        if unit == DOWN:
            low, high = self.rs_total(DOWN), self.rs_total(DOWN + 1)
            self.down_out[:, self.half_columns(self.c)] = jnp.where(even, low, high)
            self.SFH[...] = jnp.where(even, high, low)
            self.start(self.rs_four_copies(DOWN))

    def up_rows(self, i, total):
        even = self.c == 0
        low, high = total[:24], total[24:]
        self.UPG[self.up_side(i), :, self.half_columns_up()] = jnp.where(even, low, high)
        self.SFU[i] = jnp.where(even, high, low)

    def rs_up(self):
        self.arrived(self.up_back_copies())
        self.up_rows(1, self.UPR[...].astype(F32))
        self.start(self.rs_four_copies(UP))

    def rs_done(self, unit):
        if unit != DOWN + 1:
            self.arrived(self.rs_four_copies(unit))
        if unit == UP:
            for z in range(4):
                at = slice(384 * z, 384 * z + 384)
                start = self.width * (UP + z)
                both = self.join_runs(self.UPG[0, :, at], self.UPG[1, :, at])
                self.block_grad[:, start : start + self.width] = both

    def sum_copies(self, which, stage):
        peers = [[self.sibling()], [self.x_peer()], [self.y_peer()]]
        peers += [[self.z_peer(k) for k in (1, 2, 3)]]
        return [
            self.copy(
                self.V.at[which, stage],
                self.VR.at[which, stage + i],
                self.s_vec,
                (which, stage + i),
                peer,
            )
            for i, peer in enumerate(peers[stage])
        ]

    def placement(self, dtype, rows):
        own = self.width // NODES
        at = lax.broadcasted_iota(jnp.int32, (rows, self.width), 0)
        feature = lax.broadcasted_iota(jnp.int32, (rows, self.width), 1)
        return ((at < own) & (feature == at + own * self.node)).astype(F32).astype(dtype)

    def sum_start(self, which, stage, value):
        self.V[which, stage] = value
        self.start(self.sum_copies(which, stage))

    def sum_end(self, which, stage):
        now = self.sum_copies(which, stage)
        self.arrived(now)
        value = self.V[which, stage]
        for i in range(len(now)):
            value = value + self.VR[which, stage + i]
        return value

    def keep_left(self, place, value):
        self.LHS[place, self.c] = value
        self.send_left(place)

    def send_left(self, place):
        here = self.LHS.at[place, self.c]
        self.start([self.copy(here, here, self.s_left, place, self.sibling())])

    def keep_right(self, place, value):
        self.RHS[place, self.c] = value
        self.send_right(place)

    def send_right(self, place):
        here = self.RHS.at[place, self.c]
        self.start([self.copy(here, here, self.s_right, place, self.sibling())])

    def left_arrived(self, place):
        if ("left", place) not in self.here:
            self.here.add(("left", place))
            here = self.LHS.at[place, self.c]
            self.copy(here, here, self.s_left, place, self.sibling()).wait_recv()

    def right_arrived(self, place):
        if ("right", place) not in self.here:
            self.here.add(("right", place))
            here = self.RHS.at[place, self.c]
            self.copy(here, here, self.s_right, place, self.sibling()).wait_recv()

    def weight(self, block):
        return self.W[block].reshape(self.width, self.width)

    def weight_grad(self, unit):
        left, right = {QS: (0, 0), KS: (0, 1), VS: (0, 2), SO: (1, 3), CQ: (2, 4), CO: (3, 5)}[unit]
        self.sent(unit)
        self.left_arrived(left)
        self.right_arrived(right)
        columns = self.half_columns(self.c)
        right_all = self.RHS[right, :, :, columns].reshape(2 * self.tokens, 384)
        for t in range(2):
            left_all = self.LHS[left, :, :, pl.ds(384 * t, 384)].reshape(2 * self.tokens, 384)
            part = mm_at(left_all, right_all).astype(LOW)
            self.W[unit, pl.ds(2 * t, 2), :, :, :, columns] = part.reshape(2, 2, 2, 48, 384)

    def up_grad(self):
        c = self.c
        self.sent(UP)
        right_all = self.DH[c].reshape(4 * self.tokens, self.width)
        for t in range(2):
            left_all = self.A3[:, :, :, pl.ds(384 * t, 384)].reshape(4 * self.tokens, 384)
            part = mm_at(left_all, right_all).astype(LOW)
            self.W[UP + c, pl.ds(2 * t, 2)] = part.reshape(2, 2, 2, 48, self.width)

    def down_grad(self):
        right_all = self.G4[:, :, :, self.half_columns(self.c)].reshape(4 * self.tokens, 384)
        for z in range(4):
            j, t = z // 2, z % 2
            left_all = self.U[j, :, :, :, pl.ds(384 * t, 384)].reshape(4 * self.tokens, 384)
            part = mm_at(left_all, right_all).astype(LOW)
            self.HG[z] = part.reshape(2, 192, 384)

    def memory_copy(self, which):
        return self.copy(
            self.CS.at[which], self.CM.at[which], self.s_memory, which, self.sibling()
        )

    def memory_term(self, which, c, t):
        left = self.IMG[:, pl.ds(384 * t, 384)]
        part = mm_at(left, self.KV[which, :, self.half_columns(c)])
        return part.reshape(2, 2, 2, 48, 384)

    def memory_grad_other(self, which):
        for t in range(2):
            part = self.memory_term(which, 1 - self.c, t)
            self.CS[which, pl.ds(2 * t, 2)] = part.astype(LOW)
        self.start([self.memory_copy(which)])

    def memory_grad_own(self, which):
        self.memory_copy(which).wait_recv()
        for t in range(2):
            part = self.memory_term(which, self.c, t)
            part = part + self.CM[which, pl.ds(2 * t, 2)].astype(F32)
            self.CP[which, pl.ds(2 * t, 2)] = part.astype(LOW)

    def masked(self, value):
        return value * self.low_lanes, value * self.high_lanes

    def self_attention(self):
        rows = lax.broadcasted_iota(jnp.int32, (128, 128), 0)
        cols = lax.broadcasted_iota(jnp.int32, (128, 128), 1)
        length = jnp.where(cols < 64, self.lengths[0], self.lengths[1])
        allowed = (lax.div(rows, 64) == lax.div(cols, 64)) & (cols <= rows)
        allowed = allowed & (lax.rem(cols, 64) < length)
        parts = []
        for p in range(self.pairs):
            at = slice(128 * p, 128 * p + 128)
            q, k, v = self.QKV[0, :, at], self.QKV[1, :, at], self.QKV[2, :, at]
            both = mm_bt(q, self.stacked(k)) * 0.125
            probs = []
            for h in range(2):
                s = jnp.where(allowed, both[:, 128 * h : 128 * h + 128], -1000000000.0)
                e = jnp.exp(s - jnp.max(s, axis=-1, keepdims=True))
                probs.append(e / jnp.sum(e, axis=-1, keepdims=True))
            prob = jnp.concatenate(probs, axis=1)
            self.PS[p] = prob
            parts.append(mm(prob.astype(LOW), self.stacked(v)).astype(LOW))
        return jnp.concatenate(parts, axis=1)

    def self_attention_back(self, grad):
        parts = ([], [], [])
        for p in range(self.pairs):
            at = slice(128 * p, 128 * p + 128)
            q, k, v = self.QKV[0, :, at], self.QKV[1, :, at], self.QKV[2, :, at]
            g = grad[:, at]
            prob = self.PS[p]
            dp = mm_bt(g, self.stacked(v))
            prod = prob * dp
            parts_ds = []
            for h in range(2):
                lanes = slice(128 * h, 128 * h + 128)
                inner = jnp.sum(prod[:, lanes], axis=-1, keepdims=True)
                parts_ds.append(prob[:, lanes] * (dp[:, lanes] - inner))
            ds = jnp.concatenate(parts_ds, axis=1).astype(LOW)
            dq = mm(ds, self.stacked(k))
            dk = self.diagonal(mm_at(ds, q), 128)
            dv = self.diagonal(mm_at(prob.astype(LOW), g), 128)
            for out, item in zip(parts, (dq * 0.125, dk * 0.125, dv)):
                out.append(item.astype(LOW))
        return [jnp.concatenate(item, axis=1) for item in parts]

    def stacked(self, value):
        a, b = self.masked(value)
        return jnp.concatenate([a, b], axis=0)

    def diagonal(self, value, rows):
        return jnp.where(self.is_first, value[:rows], value[rows:])

    def stacked_four(self, value):
        zero = jnp.zeros((value.shape[0], 128), LOW)
        left = [jnp.concatenate([item, zero], axis=1) for item in self.masked(value[:, :128])]
        right = [jnp.concatenate([zero, item], axis=1) for item in self.masked(value[:, 128:])]
        return jnp.concatenate(left + right, axis=0)

    def diagonal_four(self, value):
        left = jnp.where(self.is_first, value[:64, :128], value[64:128, :128])
        right = jnp.where(self.is_first, value[128:192, 128:], value[192:, 128:])
        return jnp.concatenate([left, right], axis=1)

    def row_pair(self, ref, place, row):
        return jnp.concatenate([ref[place, row : row + 1], ref[place, row + 1 : row + 2]], axis=1)

    def put_pair(self, ref, place, row, value):
        ref[place, row : row + 1] = value[:, :128]
        ref[place, row + 1 : row + 2] = value[:, 128:]

    def memory_forward(self, which):
        w = self.weight(CK + which)

        @pl.loop(0, 3)
        def _(t):
            size = self.IMG.shape[0] // 3
            rows = pl.ds(pl.multiple_of(size * t, 16), size)
            self.KV[which, rows] = mm(self.IMG[rows], w).astype(LOW)

    def cross_forward(self, place):
        rows = pl.ds(pl.multiple_of(place * self.image_rows, 16), self.image_rows)
        for f in range(self.pairs // 2):
            at = slice(256 * f, 256 * f + 256)
            k, v = self.KV[0, rows, at], self.KV[1, rows, at]
            q = self.stacked_four(self.QA[place, :, at])
            s = mm_bt(k, q) * 0.125
            top = jnp.max(s, axis=0, keepdims=True)
            e = jnp.exp(s - top)
            low = e.astype(LOW)
            self.E[place, f] = low
            self.put_pair(self.ST, place, 2 * f, jnp.sum(e, axis=0, keepdims=True))
            self.put_pair(self.ST, place, 8 + 2 * f, top)
            self.put_pair(self.TOP, place, 2 * f, top)
            num = mm_at(low, v)
            self.NUM[place, :, at] = self.diagonal_four(num).astype(LOW)
        self.ST[place, 6:8] = jnp.ones((2, 128), F32)
        self.ST[place, 14:16] = jnp.zeros((2, 128), F32)

    def cross_backward(self, place):
        rows = pl.ds(pl.multiple_of(place * self.image_rows, 16), self.image_rows)
        for f in range(self.pairs // 2):
            at = slice(256 * f, 256 * f + 256)
            k, v = self.KV[0, rows, at], self.KV[1, rows, at]
            q = self.stacked_four(self.QA[place, :, at])
            g = self.stacked_four(self.GA[place, :, at])
            top = self.row_pair(self.TOP, place, 2 * f)
            share = jnp.exp(top - self.row_pair(self.DL, place, 8 + 2 * f))
            e = self.E[place, f].astype(F32) * share
            ds = e * (mm_bt(v, g) + self.row_pair(self.DL, place, 2 * f))
            ds = ds.astype(LOW)
            dq = mm_at(ds, k)
            self.NUM[place, :, at] = (self.diagonal_four(dq) * 0.125).astype(LOW)
            self.KV[0, rows, at] = (mm(ds, q) * 0.125).astype(LOW)
            self.KV[1, rows, at] = mm(e.astype(LOW), g).astype(LOW)

    def captions_of(self, owner):
        return pl.ds(owner * self.count, self.count)

    def caption(self, bits, j):
        return self.owner(bits) * self.count + j

    def partner(self, bit):
        return (self.wide, jnp.bitwise_xor(self.nar, bit))

    def owner(self, bits):
        return jnp.bitwise_xor(self.nar, bits)

    def once(self, key, copies):
        if key not in self.here:
            self.here.add(key)
            self.arrived(copies())

    def share_copies(self, refs, bit, bits, j):
        where = ((self.N + bits) // (2 * bit) - 1) * self.count + j
        place = self.caption(bits, j)
        peer = self.partner(bit)
        return [self.copy(ref.at[place], ref.at[place], sems, where, peer) for ref, sems in refs]

    def share_start(self, refs, j):
        bit = self.N // 2
        while bit:
            self.start(self.share_copies(refs, bit, 0, j))
            bit //= 2

    def share_wait(self, refs, bits, j):
        if bits:
            bit = bits & -bits
            key = (refs is self.queries, bits, j)
            self.once(key, lambda: self.share_copies(refs, bit, bits - bit, j))

    def share_pass(self, refs, j):
        bit = self.N // 2
        while bit:
            for bits in range(2 * bit, self.N, 2 * bit):
                self.share_wait(refs, bits, j)
                self.start(self.share_copies(refs, bit, bits, j))
            bit //= 2

    def merge_slot(self, bit, bits):
        return self.N - self.N // bit + bits // (2 * bit)

    def merge_copies(self, refs, bit, bits, j):
        slot = self.merge_slot(bit, bits)
        place = self.caption(bits + bit, j)
        where = slot * self.count + j
        peer = self.partner(bit)
        return [
            self.copy(ref.at[place], there.at[slot, j], sems, where, peer)
            for ref, there, sems in refs
        ]

    def merge_start(self, refs, bits, j, group):
        if bits % 2:
            self.start(self.merge_copies(refs, 1, bits - 1, j), group)

    def merge_part(self, refs, join, bit, bits, j, group):
        self.arrived(self.merge_copies(refs, bit, bits, j))
        join(self.caption(bits, j), self.merge_slot(bit, bits), j)
        if bits % (4 * bit):
            self.start(self.merge_copies(refs, 2 * bit, bits - 2 * bit, j), group)

    def merge_far(self, refs, join, j, group):
        bit = 1
        while bit < self.N:
            for bits in reversed(range(2 * bit, self.N, 2 * bit)):
                self.merge_part(refs, join, bit, bits, j, group)
            bit *= 2

    def merge_own(self, refs, join, j, group, low, high):
        bit = low
        while bit < high:
            self.merge_part(refs, join, bit, 0, j, group)
            bit *= 2

    def column(self, turned, p):
        return jnp.where(self.is_first, turned[:64, p : p + 1], turned[64:, p : p + 1])

    def turn(self, *rows):
        have = 8 * len(rows)
        return jnp.concatenate([*rows, jnp.zeros((128 - have, 128), F32)], axis=0).T

    def join_softmax(self, place, slot, j):
        total_a, top_a = self.ST[place, :8], self.ST[place, 8:]
        total_b, top_b = self.STR[slot, j, :8], self.STR[slot, j, 8:]
        top = jnp.maximum(top_a, top_b)
        share_a, share_b = jnp.exp(top_a - top), jnp.exp(top_b - top)
        self.ST[place, :8] = share_a * total_a + share_b * total_b
        self.ST[place, 8:] = top
        turned = self.turn(share_a, share_b)
        for p in range(self.pairs):
            at = slice(128 * p, 128 * p + 128)
            a = self.NUM[place, :, at].astype(F32) * self.column(turned, p)
            b = self.NUMR[slot, j, :, at].astype(F32) * self.column(turned, 8 + p)
            self.NUM[place, :, at] = (a + b).astype(LOW)

    def join_sum(self, place, slot, j):
        self.add_into(self.NUM.at[place], self.NUMR[slot, j])

    def attended(self, j):
        place = self.nar * self.count + j
        turned = self.turn(1.0 / self.ST[place, :8])
        self.SCT[j] = turned
        parts = []
        for p in range(self.pairs):
            at = slice(128 * p, 128 * p + 128)
            parts.append(self.NUM[place, :, at].astype(F32) * self.column(turned, p))
        return jnp.concatenate(parts, axis=1)

    def spread_grad(self, j, doc):
        lane = lax.broadcasted_iota(jnp.int32, (128, 128), 1)
        place = self.nar * self.count + j
        rows = self.rows_of(j)
        turned = self.SCT[j]
        inner = jnp.zeros((128, 128), F32)
        for p in range(self.pairs):
            at = slice(128 * p, 128 * p + 128)
            part = doc[:, at] * self.column(turned, p)
            self.GA[place, :, at] = part.astype(LOW)
            prod = part * self.OCF[rows, at]
            a = jnp.sum(jnp.where(self.is_first, prod, 0.0), axis=1, keepdims=True)
            b = jnp.sum(jnp.where(self.is_first, 0.0, prod), axis=1, keepdims=True)
            inner = jnp.where(lane == p, jnp.concatenate([a, b], axis=0), inner)
        self.DL[place, :8] = -inner.T[:8]
        self.DL[place, 8:] = self.ST[place, 8:]

    def rows_of(self, j):
        return slice(self.seq * j, self.seq * j + self.seq)

    def wide_copy(self, ref, sems, i, j):
        here = ref.at[self.c, 1 - self.x if i == 2 else self.x, self.rows_of(j)]
        peer = self.x_peer() if i == 0 else self.sibling()
        return self.copy(here, here, sems, i * self.count + j, peer)

    def keep_wide(self, ref, value, sems, j):
        ref[self.c, self.x, self.rows_of(j)] = value
        self.start([self.wide_copy(ref, sems, i, j) for i in range(2)])

    def wide_across(self, ref, sems, j):
        self.arrived([self.wide_copy(ref, sems, 0, j)])
        self.start([self.wide_copy(ref, sems, 2, j)])

    def wide_arrived(self, ref, sems):
        for j in range(self.count):
            self.arrived([self.wide_copy(ref, sems, i, j) for i in (1, 2)])

    def hidden_copy(self, ref, j, sems):
        here = ref.at[j, self.c]
        return self.copy(here, here, sems, j, self.sibling())

    def fold_copy(self, which, j):
        at = (which, self.rows_of(j))
        where = which * self.count + j
        return self.copy(self.FS.at[at], self.FR.at[at], self.s_fold, where, self.x_peer())

    def fold_start(self, which):
        self.start([self.fold_copy(which, j) for j in range(self.count)])

    def inward(self, name):
        sem = self.s_in[0].at[self.ins.index(name)]
        return pltpu.make_async_copy(self.outer[name], getattr(self, name), sem)

    def outward(self, name):
        sem = self.s_out[0].at[self.outs.index(name)]
        return pltpu.make_async_copy(getattr(self, name), self.outer[name], sem)

    def image_copy(self, back):
        src, dst = (self.IMG, self.outer["image_grad"]) if back else (self.outer["images"], self.IMG)
        return pltpu.make_async_copy(src, dst, self.s_image[0].at[0])

    def both_halves(self, value):
        low, high = value[: self.tokens], value[self.tokens :]
        west = self.x == 0
        return jnp.where(west, low, high), jnp.where(west, high, low)

    def do_begin(self):
        ins = [self.inward(name) for name in self.ins]
        for item in ins:
            item.start()
        self.image_copy(False).start()
        self.enter()
        for item in ins:
            item.wait()
        self.pair_pack()
        self.start(self.pair_copies())
        rows = [getattr(self, name)[...].astype(F32) for name in VECTORS]
        rows = jnp.concatenate(rows + [jnp.zeros((2, rows[0].shape[1]), F32)], axis=0)
        self.sum_start(0, 0, mm(rows.astype(LOW), self.placement(LOW, rows.shape[1])))
        self.pair_merge()
        self.inputs = self.captions[...].astype(F32)
        self.queries = [(self.QA, self.s_query)]
        self.numbers = [(self.NUM, self.NUMR, self.s_num), (self.ST, self.STR, self.s_st)]
        self.grads = [(self.GA, self.s_g), (self.DL, self.s_dl)]
        self.back = [(self.NUM, self.NUMR, self.s_dq)]

    def do_up0(self):
        self.start(self.up_copies(), "up")

    def do_vec(self, stage):
        self.sum_start(0, stage, self.sum_end(0, stage - 1))

    def do_g0(self):
        for j in range(self.count):
            self.keep_wide(self.G4, self.out_grad[self.rows_of(j)], self.s_g4, j)

    def do_g1(self):
        for j in range(self.count):
            self.wide_across(self.G4, self.s_g4, j)

    def do_mem(self, which):
        if "images" not in self.here:
            self.here.add("images")
            self.image_copy(False).wait()
        self.done(CK + which)
        self.memory_forward(which)

    def do_a1(self):
        vectors = self.sum_end(0, 3)
        self.gains = [vectors[i : i + 1] for i in (0, 2, 4)]
        self.shifts = [vectors[i : i + 1] for i in (1, 3, 5)]
        self.rstds = [None, None, []]
        self.r2 = []
        self.a1 = self.normed(0, self.inputs)
        self.keep_left(0, self.a1)

    def normed(self, which, value):
        hat, self.rstds[which], out = norm(value, self.gains[which], self.shifts[which])
        self.HAT[which] = hat
        return out.astype(LOW)

    def pulled(self, which, grad):
        return norm_pull(grad, self.HAT[which], self.rstds[which], self.gains[which])

    def do_qkv(self, which):
        self.done(which)
        self.QKV[which] = mm(self.a1, self.weight(which)).astype(LOW)

    def do_sa(self):
        self.mixed = self.self_attention()
        self.keep_left(1, self.mixed)

    def do_r1(self):
        self.done(SO)
        self.r1 = self.inputs + mm(self.mixed, self.weight(SO))
        self.a2 = self.normed(1, self.r1)
        self.keep_left(2, self.a2)

    def do_cq(self):
        self.done(CQ)
        query = mm(self.a2, self.weight(CQ)).astype(LOW)
        self.QA[self.captions_of(self.nar)] = query.reshape(self.count, 64, self.width)
        for j in range(self.count):
            self.share_start(self.queries, j)

    def do_q1(self, j):
        self.share_pass(self.queries, j)

    def do_cf(self, item):
        bits, j = divmod(item, self.count)
        self.share_wait(self.queries, bits, j)
        self.cross_forward(self.caption(bits, j))
        self.merge_start(self.numbers, bits, j, "numbers")

    def do_m1(self, j):
        self.merge_far(self.numbers, self.join_softmax, j, "numbers")

    def do_m2(self, j):
        self.merge_own(self.numbers, self.join_softmax, j, "numbers", 1, 2)

    def do_a3(self, j):
        self.merge_own(self.numbers, self.join_softmax, j, "numbers", 2, self.N)
        rows = self.rows_of(j)
        full = self.attended(j)
        self.OCF[rows] = full
        oc = full.astype(LOW)
        self.LHS[3, self.c, rows] = oc
        self.once("co", lambda: self.hand_copies(CO))
        r2 = self.r1[rows] + mm(oc, self.weight(CO))
        hat, rstd, out = norm(r2, self.gains[2], self.shifts[2])
        self.HAT[2, rows] = hat
        self.keep_wide(self.A3, out.astype(LOW), self.s_a3, j)
        self.r2.append(r2)
        self.rstds[2].append(rstd)
        if j == self.count - 1:
            self.send_left(3)

    def do_x1(self, j):
        self.wide_across(self.A3, self.s_a3, j)

    def do_hp(self):
        self.done(UP)
        a3 = self.A3[self.c].reshape(2 * self.tokens, self.width)
        for j in range(2):
            hidden = mm(a3, self.weight(UP + j))
            square = hidden * hidden
            tanh = jnp.tanh(GELU_A * hidden * (1.0 + GELU_B * square))
            act = (0.5 * hidden * (1.0 + tanh)).astype(LOW)
            self.SLOPE[j] = 0.5 * (1.0 + tanh) + 0.5 * hidden * (1.0 - tanh * tanh) * (
                GELU_A * (1.0 + 3.0 * GELU_B * square)
            )
            self.U[j, self.c] = act.reshape(2, self.tokens, self.width)
            self.start([self.hidden_copy(self.U, j, self.s_u)])

    def do_dg(self):
        self.wide_arrived(self.G4, self.s_g4)
        for j in range(2):
            self.hidden_copy(self.U, j, self.s_u).wait_recv()
        self.down_grad()

    def do_e3(self):
        self.done(DOWN)
        self.done(DOWN + 1)
        grad = self.G4[self.c].reshape(2 * self.tokens, self.width)
        e3 = 0.0
        for j in range(2):
            down = [self.HD[i, 2 * j : 2 * j + 2].reshape(self.width, 384) for i in range(2)]
            back = mm_bt(grad[:, :384], down[0]) + mm_bt(grad[:, 384:], down[1])
            dhp = (back * self.SLOPE[j]).astype(LOW)
            self.DH[j, self.c] = dhp.reshape(2, self.tokens, self.width)
            self.start([self.hidden_copy(self.DH, j, self.s_dh)])
            e3 = e3 + mm_bt(dhp, self.weight(UP + j))
        self.dr2 = []
        self.e3, other = self.both_halves(e3)
        self.FS[0] = other.astype(LOW)
        self.fold_start(0)

    def do_out(self):
        out = [0.0, 0.0]
        for j in range(2):
            act = self.U[j, self.c].reshape(2 * self.tokens, self.width)
            for i in range(2):
                down = self.HD[i, 2 * j : 2 * j + 2].reshape(self.width, 384)
                out[i] = out[i] + mm(act, down)
        own, other = self.both_halves(jnp.concatenate(out, axis=1))
        self.out = jnp.concatenate(self.r2, axis=0) + own
        self.FS[1] = other.astype(LOW)
        self.fold_start(1)

    def do_lo(self):
        self.arrived([self.fold_copy(1, j) for j in range(self.count)])
        self.layer_out[...] = (self.out + self.FR[1].astype(F32)).astype(LOW)
        self.outward("layer_out").start()

    def do_ug(self):
        self.wide_arrived(self.A3, self.s_a3)
        for j in range(2):
            self.hidden_copy(self.DH, j, self.s_dh).wait_recv()
        self.up_grad()

    def do_dr2(self, j):
        self.arrived([self.fold_copy(0, j)])
        rows = self.rows_of(j)
        e3 = self.e3[rows] + self.FR[0, rows].astype(F32)
        back, *vec = norm_pull(e3, self.HAT[2, rows], self.rstds[2][j], self.gains[2])
        self.vec3 = [a + b for a, b in zip(self.vec3, vec)] if j else vec
        dr2 = self.out_grad[rows].astype(F32) + back
        self.dr2.append(dr2)
        dcat = dr2.astype(LOW)
        self.RHS[5, self.c, rows] = dcat
        self.spread_grad(j, mm_bt(dcat, self.weight(CO)))
        self.share_start(self.grads, j)
        if j == self.count - 1:
            self.send_right(5)

    def do_p1(self, j):
        self.share_pass(self.grads, j)

    def do_cb(self, item):
        bits, j = divmod(item, self.count)
        self.share_wait(self.grads, bits, j)
        self.sent("numbers")
        self.cross_backward(self.caption(bits, j))
        self.merge_start(self.back, bits, j, "back")

    def do_n1(self, j):
        self.merge_far(self.back, self.join_sum, j, "back")

    def do_n2(self, j):
        self.merge_own(self.back, self.join_sum, j, "back", 1, 2)

    def do_dq(self):
        for j in range(self.count):
            self.merge_own(self.back, self.join_sum, j, "back", 2, self.N)
        dqc = self.NUM[self.captions_of(self.nar)].reshape(self.tokens, self.width)
        self.keep_right(4, dqc)
        back, *self.vec2 = self.pulled(1, mm_bt(dqc, self.weight(CQ)))
        self.dr1 = jnp.concatenate(self.dr2, axis=0) + back
        dattn = self.dr1.astype(LOW)
        self.keep_right(3, dattn)
        self.dos = mm_bt(dattn, self.weight(SO)).astype(LOW)

    def do_mo(self, which):
        self.memory_grad_other(which)

    def do_mw(self, which):
        self.memory_grad_own(which)

    def do_wg(self, unit):
        self.weight_grad(unit)

    def do_sb(self):
        e1 = 0.0
        for j, item in enumerate(self.self_attention_back(self.dos)):
            self.keep_right(j, item)
            e1 = e1 + mm_bt(item, self.weight(j))
        back, *vec = self.pulled(0, e1)
        self.input_grad[...] = (self.dr1 + back).astype(LOW)
        self.outward("input_grad").start()
        vec = vec + self.vec2 + self.vec3 + [jnp.zeros((2, self.width), F32)]
        self.sum_start(1, 0, jnp.concatenate(vec, axis=0))

    def do_sum(self, stage):
        self.sum_start(1, stage, self.sum_end(1, stage - 1))

    def do_img(self):
        @pl.loop(0, 3)
        def _(t):
            size = self.IMG.shape[0] // 3
            rows = pl.ds(pl.multiple_of(size * t, 16), size)
            part = mm_bt(self.KV[0, rows], self.weight(CK))
            part = part + mm_bt(self.KV[1, rows], self.weight(CV))
            self.IMG[rows] = part.astype(LOW)

        self.image_copy(True).start()

    def do_end(self):
        self.vec_grad[...] = lax.dot_general(
            self.sum_end(1, 3),
            self.placement(F32, 128),
            (((1,), (1,)), ((), ())),
            precision=lax.Precision.HIGHEST,
            preferred_element_type=F32,
        )
        self.outward("vec_grad").start()
        for unit in range(UNITS):
            self.rs_done(unit)
        self.outward("block_grad").start()
        self.outward("down_out").start()
        self.image_copy(True).wait()
        for name in self.outs:
            self.outward(name).wait()
        for group in list(self.started):
            self.sent(group)

    def run(self):
        steps = {
            Step.begin: self.do_begin,
            Step.up0: self.do_up0,
            Step.vec: self.do_vec,
            Step.g0: self.do_g0,
            Step.g1: self.do_g1,
            Step.mem: self.do_mem,
            Step.a1: self.do_a1,
            Step.qkv: self.do_qkv,
            Step.sa: self.do_sa,
            Step.r1: self.do_r1,
            Step.cq: self.do_cq,
            Step.q1: self.do_q1,
            Step.cf: self.do_cf,
            Step.m1: self.do_m1,
            Step.m2: self.do_m2,
            Step.a3: self.do_a3,
            Step.x1: self.do_x1,
            Step.hp: self.do_hp,
            Step.dg: self.do_dg,
            Step.e3: self.do_e3,
            Step.out: self.do_out,
            Step.lo: self.do_lo,
            Step.ug: self.do_ug,
            Step.dr2: self.do_dr2,
            Step.p1: self.do_p1,
            Step.cb: self.do_cb,
            Step.n1: self.do_n1,
            Step.n2: self.do_n2,
            Step.dq: self.do_dq,
            Step.mo: self.do_mo,
            Step.mw: self.do_mw,
            Step.wg: self.do_wg,
            Step.sb: self.do_sb,
            Step.sum: self.do_sum,
            Step.img: self.do_img,
            Step.end: self.do_end,
            Step.F: self.first,
            Step.S: self.second,
            Step.TA: lambda unit: self.third(unit, 0),
            Step.TB: lambda unit: self.third(unit, 1),
            Step.H: self.hand,
            Step.R1: self.rs_one,
            Step.RA: self.rs_two,
            Step.RB: lambda unit: self.rs_two(unit, 1),
            Step.R3: self.rs_three,
            Step.R4: self.rs_four,
            Step.RU: lambda unit: self.rs_up(),
        }
        for step, *place in ORDER:
            steps[step](*place)


def layer_call(lanes, narrow, captions, images, lengths, out_grad, *params):
    tokens, width = captions.shape
    count = tokens // 64
    groups = narrow * count
    image_rows = images.shape[0]
    pairs = width // 128
    ins = ["captions", "out_grad", "self_proj", "self_output"]
    ins += ["cross_query", "cross_memory", "cross_output", "hidden_up", "hidden_down", *VECTORS]
    given = dict(zip(ins, (captions, out_grad, *params)))
    outs = {
        "layer_out": ((tokens, width), LOW),
        "input_grad": ((tokens, width), LOW),
        "image_grad": ((image_rows, width), LOW),
        "block_grad": ((24, 12 * width), F32),
        "down_out": ((96, width), F32),
        "vec_grad": ((8, 128), F32),
    }
    results = [name for name in outs if name != "image_grad"]
    memory = {name: (item.shape, item.dtype) for name, item in given.items()}
    memory |= {name: outs[name] for name in results}
    memory |= {
        "W": ((10, 4, 2, 2, 48, width), LOW),
        "HD": ((2, 4, 2, 192, 384), LOW),
        "HG": ((4, 2, 192, 384), LOW),
        "UPS": ((48, width), LOW),
        "UPR": ((48, width), LOW),
        "PA": ((2, 24 * UP, 384), LOW),
        "PB": ((2, 48, width), LOW),
        "IMG": ((image_rows, width), LOW),
        "KV": ((2, image_rows, width), LOW),
        "E": ((groups, pairs // 2, image_rows // groups, 256), LOW),
        "LHS": ((4, 2, tokens, width), LOW),
        "RHS": ((6, 2, tokens, width), LOW),
        "A3": ((2, 2, tokens, width), LOW),
        "G4": ((2, 2, tokens, width), LOW),
        "U": ((2, 2, 2, tokens, width), LOW),
        "DH": ((2, 2, 2, tokens, width), LOW),
        "FS": ((2, tokens, width), LOW),
        "FR": ((2, tokens, width), LOW),
        "R1": ((UP, 4, 2, 48, 384), LOW),
        "R2": ((UP, 4, 48, 384), LOW),
        "R3": ((UP, 3, 48, 384), LOW),
        "RU1": ((4, 2, 48, width), LOW),
        "RU3": ((3, 2, 48, width), LOW),
        "RH1": ((4, 96, 384), LOW),
        "RH3": ((3, 96, 384), LOW),
        "RL1": ((96, 384), LOW),
        "RL3": ((3, 2, 96, 384), LOW),
        "CM": ((2, 4, 2, 2, 48, 384), LOW),
        "CS": ((2, 4, 2, 2, 48, 384), LOW),
        "CP": ((2, 4, 2, 2, 48, 384), LOW),
        "SF": ((UP, 24, 384), F32),
        "SFU": ((2, 24, width), F32),
        "UPG": ((2, 24, 2 * width), F32),
        "SFH": ((96, 384), F32),
        "V": ((2, 4, 8, width), F32),
        "VR": ((2, 6, 8, width), F32),
        "QKV": ((3, tokens, width), LOW),
        "PS": ((HEADS // 2, 128, 256), F32),
        "HAT": ((3, tokens, width), F32),
        "SLOPE": ((2, 2 * tokens, width), F32),
        "OCF": ((tokens, width), F32),
        "QA": ((groups, 64, width), LOW),
        "NUM": ((groups, 64, width), LOW),
        "ST": ((groups, 16, 128), F32),
        "TOP": ((groups, 8, 128), F32),
        "NUMR": ((narrow - 1, count, 64, width), LOW),
        "STR": ((narrow - 1, count, 16, 128), F32),
        "SCT": ((count, 128, 128), F32),
        "GA": ((groups, 64, width), LOW),
        "DL": ((groups, 16, 128), F32),
    }
    signals = {
        "s_pair": (3,),
        "s_up": (2,),
        "s_z": (UNITS, 3),
        "s_two": (UP, 2),
        "s_three": (UNITS, 2),
        "s_hand": (UNITS,),
        "s_rs1": (UNITS, 2),
        "s_rs2": (UP, 2),
        "s_rs3": (UNITS, 3),
        "s_rs4": (UNITS,),
        "s_rs5": (2,),
        "s_vec": (2, 6),
        "s_left": (4,),
        "s_right": (6,),
        "s_a3": (3 * count,),
        "s_g4": (3 * count,),
        "s_u": (2,),
        "s_dh": (2,),
        "s_fold": (2 * count,),
        "s_memory": (2,),
        "s_query": ((narrow - 1) * count,),
        "s_num": ((narrow - 1) * count,),
        "s_st": ((narrow - 1) * count,),
        "s_g": ((narrow - 1) * count,),
        "s_dl": ((narrow - 1) * count,),
        "s_dq": ((narrow - 1) * count,),
        "s_image": (1,),
        "s_in": (len(ins),),
        "s_out": (len(results),),
    }
    scratch = [pltpu.VMEM(shape, kind) for shape, kind in memory.values()]
    for shape in signals.values():
        scratch += [pltpu.SemaphoreType.DMA(shape)] * 2

    def body(*refs):
        names = ["lengths", "images", *ins, *outs]
        outer = dict(zip(names, refs))
        named = dict(zip(memory, refs[len(names) :]))
        rest = refs[len(names) + len(memory) :]
        for i, name in enumerate(signals):
            named[name] = (rest[2 * i], rest[2 * i + 1])
        named |= {"outer": outer, "lengths": outer["lengths"], "ins": ins, "outs": results}
        Layer(named, lanes, narrow).run()

    anywhere = pl.BlockSpec(memory_space=pl.ANY)
    return pl.pallas_call(
        body,
        out_shape=[jax.ShapeDtypeStruct(shape, kind) for shape, kind in outs.values()],
        in_specs=[pl.BlockSpec(memory_space=pltpu.SMEM)] + [anywhere] * (len(ins) + 1),
        out_specs=[anywhere] * len(outs),
        scratch_shapes=scratch,
        compiler_params=pltpu.CompilerParams(
            collective_id=0, has_side_effects=True, vmem_limit_bytes=VMEM_LIMIT
        ),
        cost_estimate=pl.CostEstimate(
            flops=17 * 10**9, bytes_accessed=8 * 10**6, transcendentals=2 * 10**6
        ),
        name="layer",
    )(lengths, images, *given.values())


def deliver(ranges, arrays, block_grad, vec_grad, own):
    count = len(arrays)
    ins = [vec_grad, block_grad, *arrays]
    outs = [jax.ShapeDtypeStruct((1, own), F32)] * len(VECTORS)
    outs += [jax.ShapeDtypeStruct((block_grad.shape[0], b - a), F32) for a, b in ranges]
    outs += [jax.ShapeDtypeStruct(item.shape, item.dtype) for item in arrays]

    def body(*refs):
        given, found = refs[: len(ins)], refs[len(ins) : len(ins) + len(outs)]
        rest = refs[len(ins) + len(outs) :]
        held, rows, sems = rest[: len(ins)], rest[len(ins) : -1], rest[-1]
        copies = zip(given, held)
        into = [pltpu.make_async_copy(a, b, sems.at[i]) for i, (a, b) in enumerate(copies)]
        for item in into:
            item.start()
        views = [*rows, *[held[1].at[:, pl.ds(a, b - a)] for a, b in ranges], *held[2:]]
        back = [
            pltpu.make_async_copy(a, b, sems.at[len(ins) + i])
            for i, (a, b) in enumerate(zip(views, found))
        ]
        into[0].wait()
        for i, ref in enumerate(rows):
            ref[...] = held[0][i : i + 1, :own]
            back[i].start()
        into[1].wait()
        for item in back[len(rows) : len(rows) + len(ranges)]:
            item.start()
        for item, last in zip(into[2:], back[len(rows) + len(ranges) :]):
            item.wait()
            last.start()
        for item in back:
            item.wait()

    hold = [pltpu.VMEM(item.shape, item.dtype) for item in ins]
    hold += [pltpu.VMEM((1, own), F32)] * len(VECTORS)
    anywhere = pl.BlockSpec(memory_space=pl.ANY)
    return pl.pallas_call(
        body,
        out_shape=outs,
        in_specs=[anywhere] * len(ins),
        out_specs=[anywhere] * len(outs),
        scratch_shapes=hold + [pltpu.SemaphoreType.DMA((len(ins) + len(outs),))],
        compiler_params=pltpu.CompilerParams(vmem_limit_bytes=VMEM_LIMIT),
        name="deliver",
    )(*ins)


def lane_gather(value, lanes, narrow, axis):
    if lanes == 1:
        return value
    assert lanes % narrow == 0
    value = lax.all_gather(value, "narrow", axis=axis, tiled=True)
    step = 1
    wide_count = lax.axis_size("wide")
    while step * narrow < lanes:
        swap = [(i, i ^ step) for i in range(wide_count)]
        other = lax.ppermute(value, "wide", swap)
        low = (lax.axis_index("wide") // step) % 2 == 0
        first = jnp.where(low, value, other)
        second = jnp.where(low, other, value)
        value = jnp.concatenate([first, second], axis=axis)
        step *= 2
    return value


def lane_scatter(value, lanes, narrow, axis):
    if lanes == 1:
        return value
    wide_count = lax.axis_size("wide")
    step = lanes // narrow
    while step > 1:
        step //= 2
        swap = [(i, i ^ step) for i in range(wide_count)]
        first, second = jnp.split(value, 2, axis=axis)
        low = (lax.axis_index("wide") // step) % 2 == 0
        other = lax.ppermute(jnp.where(low, second, first), "wide", swap)
        value = jnp.where(low, first, second) + other
    return lax.psum_scatter(value, "narrow", scatter_dimension=axis, tiled=True)


def per_device(captions, images, lengths, out_grad, *params):
    narrow = lax.axis_size("narrow")
    devices = lax.axis_size("wide") * narrow
    lanes = devices // NODES
    count, seq_len, width = captions.shape
    tokens = count * seq_len
    params = [lane_gather(item, lanes, narrow, 0) for item in params]
    out, input_grad, image_grad, block_grad, down_grad, vec_grad = layer_call(
        lanes,
        narrow,
        captions.reshape(tokens, width),
        images.reshape(-1, width),
        lengths,
        out_grad.reshape(tokens, width),
        *params[:7],
        *[item.reshape(1, -1) for item in params[7:]],
    )
    block_grad = lane_scatter(block_grad, lanes, narrow, 0)
    down_grad = lane_scatter(down_grad, lanes, narrow, 0)
    if lanes > 1:
        vec_grad = lane_scatter(vec_grad[:, : width // NODES], lanes, narrow, 1)

    ends = (QS, SO, CK, CQ, CO, UP, UP + 4)
    ranges = [(width * a, width * b) for a, b in zip(ends, ends[1:])]
    arrays = [out, input_grad, image_grad, down_grad]
    own = width // devices
    found = deliver(ranges, arrays, block_grad, vec_grad, own)
    vectors, found = found[: len(VECTORS)], found[len(VECTORS) :]
    joint, self_out, memory, query, cross, up = found[:6]
    out, input_grad, image_grad, down_grad = found[6:]
    return (
        out.reshape(captions.shape),
        input_grad.reshape(captions.shape),
        image_grad.reshape(images.shape),
        joint,
        self_out,
        query,
        memory,
        cross,
        up,
        down_grad,
        *[item.reshape(-1) for item in vectors],
    )


def solution(mesh):
    both = ("wide", "narrow")
    rows = P(both, None)
    text = P(both, None, None)
    vector = P(both)
    image = P("wide", "narrow", None)
    in_specs = (text, image, vector, text) + (rows,) * 7 + (vector,) * 6
    out_specs = (text, text, image) + (rows,) * 7 + (vector,) * 6
    return jax.shard_map(
        per_device, mesh=mesh, in_specs=in_specs, out_specs=out_specs, check_vma=False
    )
```

```python
import functools

import jax
import jax.numpy as jnp
from jax import lax
from jax.experimental import pallas as pl
from jax.experimental.pallas import tpu as pltpu
from jax.sharding import PartitionSpec as P

HEADS = 12
NODES = 32
UNITS = 11
VMEM_LIMIT = 64 * 1024 * 1024 - 65536
MESH = pl.DeviceIdType.MESH
F32 = jnp.float32
LOW = jnp.bfloat16
EPSILON = 1e-05
GELU_A = 0.7978845608028654
GELU_B = 0.044715

QS, KS, VS, SO, CK, CV, CQ, CO, UP = 0, 1, 2, 3, 4, 5, 6, 7, 8
DOWN = UP + 1
LATE = DOWN + 1
GATHER = (128, 256) * 4
SCATTER = (256, 128) * 4


VECTORS = ["first_gain", "first_shift", "second_gain", "second_shift"]
VECTORS += ["third_gain", "third_shift"]


class Step:
    (
        begin,
        up0,
        vec,
        g0,
        g1,
        mem,
        a1,
        qkv,
        sa,
        r1,
        cq,
        q1,
        cf,
        m1,
        m2,
        a3,
        x1,
        hp,
        dg,
        e3,
        out,
        lo,
        ug,
        dr2,
        p1,
        cb,
        n1,
        n2,
        dq,
        mo,
        mw,
        wg,
        sb,
        sum,
        img,
        end,
        F,
        S,
        TA,
        TB,
        H,
        R1,
        RA,
        RB,
        R3,
        R4,
        RU,
    ) = range(47)


ORDER = [
    (Step.begin,), (Step.F, 1), (Step.up0,), (Step.vec, 1), (Step.g0,), (Step.F, 0), (Step.vec, 2),
    (Step.F, 3), (Step.S, 1), (Step.F, 2), (Step.S, 0), (Step.F, 5), (Step.TA, 1), (Step.vec, 3),
    (Step.S, 3), (Step.TA, 0), (Step.F, 6), (Step.TB, 0), (Step.S, 2), (Step.F, 4), (Step.TA, 3),
    (Step.S, 5), (Step.TB, 1), (Step.F, 7), (Step.F, 8), (Step.S, 6), (Step.TB, 2), (Step.TA, 2),
    (Step.S, 4), (Step.TA, 6), (Step.TB, 3), (Step.H, 1), (Step.a1,), (Step.qkv, 1), (Step.H, 0),
    (Step.TB, 5), (Step.TA, 5), (Step.TA, 4), (Step.qkv, 0), (Step.F, 10), (Step.H, 2),
    (Step.TB, 6), (Step.qkv, 2), (Step.sa,), (Step.TB, 4), (Step.H, 3), (Step.r1,), (Step.F, 9),
    (Step.H, 6), (Step.S, 8), (Step.g1,), (Step.S, 7), (Step.H, 5), (Step.S, 10), (Step.cq,),
    (Step.H, 4), (Step.mem, 1), (Step.mem, 0), (Step.cf, 0), (Step.q1, 0), (Step.cf, 3),
    (Step.cf, 6), (Step.q1, 1), (Step.TA, 7), (Step.TB, 7), (Step.cf, 4), (Step.cf, 2),
    (Step.cf, 7), (Step.m1, 0), (Step.cf, 5), (Step.H, 8), (Step.m2, 0), (Step.m1, 1), (Step.H, 7),
    (Step.S, 9), (Step.cf, 1), (Step.a3, 0), (Step.m2, 1), (Step.a3, 1), (Step.H, 10),
    (Step.x1, 0), (Step.H, 9), (Step.x1, 1), (Step.hp,), (Step.e3,), (Step.dg,), (Step.R1, 10),
    (Step.R1, 9), (Step.ug,), (Step.dr2, 0), (Step.R1, 8), (Step.dr2, 1), (Step.cb, 0),
    (Step.RA, 9), (Step.out,), (Step.cb, 3), (Step.p1, 0), (Step.wg, 7), (Step.cb, 1),
    (Step.cb, 2), (Step.p1, 1), (Step.R1, 7), (Step.cb, 6), (Step.cb, 5), (Step.cb, 7),
    (Step.n1, 1), (Step.cb, 4), (Step.n2, 1), (Step.mo, 0), (Step.n2, 0), (Step.n1, 0),
    (Step.RB, 7), (Step.mo, 1), (Step.mw, 0), (Step.R1, 4), (Step.RA, 7), (Step.mw, 1),
    (Step.R1, 5), (Step.RA, 8), (Step.dq,), (Step.sb,), (Step.wg, 3), (Step.R1, 3), (Step.wg, 1),
    (Step.RB, 4), (Step.R3, 7), (Step.wg, 2), (Step.R1, 2), (Step.sum, 1), (Step.RA, 3),
    (Step.RB, 5), (Step.wg, 0), (Step.RA, 5), (Step.R1, 0), (Step.RA, 4), (Step.RB, 2),
    (Step.RA, 2), (Step.sum, 2), (Step.R3, 5), (Step.R1, 1), (Step.R4, 8), (Step.R3, 4),
    (Step.RB, 0), (Step.RA, 10), (Step.wg, 6), (Step.RB, 3), (Step.sum, 3), (Step.R1, 6),
    (Step.R4, 5), (Step.R3, 2), (Step.RA, 1), (Step.RA, 0), (Step.R4, 9), (Step.RB, 1),
    (Step.R3, 3), (Step.R4, 2), (Step.R3, 0), (Step.RA, 6), (Step.RB, 6), (Step.R3, 1),
    (Step.R4, 4), (Step.img,), (Step.R3, 6), (Step.R4, 3), (Step.R4, 1), (Step.R4, 7),
    (Step.R4, 0), (Step.lo,), (Step.RU, 8), (Step.R4, 6), (Step.end,),
]


def mm(left, right):
    return jnp.dot(left, right, preferred_element_type=F32)


def mm_bt(left, right):
    return lax.dot_general(left, right, (((1,), (1,)), ((), ())), preferred_element_type=F32)


def mm_at(left, right):
    return lax.dot_general(left, right, (((0,), (0,)), ((), ())), preferred_element_type=F32)


def norm(value, gain, shift):
    centred = value - jnp.mean(value, axis=-1, keepdims=True)
    rstd = lax.rsqrt(jnp.mean(centred * centred, axis=-1, keepdims=True) + EPSILON)
    hat = centred * rstd
    return hat, rstd, hat * gain + shift


def norm_pull(grad, hat, rstd, gain):
    scaled = grad * gain
    inner = jnp.mean(scaled * hat, axis=-1, keepdims=True)
    back = rstd * (scaled - jnp.mean(scaled, axis=-1, keepdims=True) - hat * inner)
    gain_grad = jnp.sum(grad * hat, axis=0, keepdims=True)
    shift_grad = jnp.sum(grad, axis=0, keepdims=True)
    return back, gain_grad, shift_grad


class Layer:
    def __init__(self, refs, lanes, narrow):
        self.__dict__.update(refs)
        self.N = narrow
        self.lanes = lanes
        wide, nar = lax.axis_index("wide"), lax.axis_index("narrow")
        flat = wide * narrow + nar
        self.wide, self.nar = wide, nar
        self.node = lax.div(flat, lanes)
        self.lane = lax.rem(flat, lanes)
        node = self.node
        self.c = lax.rem(node, 2)
        self.x = lax.rem(lax.div(node, 2), 2)
        self.y = lax.rem(lax.div(node, 4), 2)
        self.z = lax.div(node, 8)
        self.started = {}
        self.here = set()
        self.count, self.seq = self.captions.shape[0] // 64, 64
        self.tokens, self.width = self.captions.shape
        self.groups = self.QA.shape[0]
        self.image_rows = self.IMG.shape[0] // self.groups
        self.pairs = self.width // 128
        lane = lax.broadcasted_iota(jnp.int32, (1, 128), 1)
        self.low_lanes = (lane < 64).astype(F32).astype(LOW)
        self.high_lanes = (lane >= 64).astype(F32).astype(LOW)
        self.is_first = lane < 64

    def device(self, z, y, x, c):
        flat = (z * 8 + y * 4 + x * 2 + c) * self.lanes + self.lane
        return (lax.div(flat, self.N), lax.rem(flat, self.N))

    def sibling(self):
        return self.device(self.z, self.y, self.x, 1 - self.c)

    def x_peer(self):
        return self.device(self.z, self.y, 1 - self.x, self.c)

    def y_peer(self):
        return self.device(self.z, 1 - self.y, self.x, self.c)

    def z_index(self, k):
        return lax.rem(self.z + k, 4)

    def z_peer(self, k):
        return self.device(self.z_index(k), self.y, self.x, self.c)

    def n_index(self, k):
        return lax.rem(self.nar + k, self.N)

    def n_peer(self, k):
        return (self.wide, self.n_index(k))

    def enter(self):
        barrier = pltpu.get_barrier_semaphore()
        peers = [self.sibling(), self.x_peer(), self.y_peer()]
        peers += [self.z_peer(k) for k in (1, 2, 3)]
        peers += [self.n_peer(k) for k in range(1, self.N)]
        for peer in peers:
            pl.semaphore_signal(barrier, inc=1, device_id=peer, device_id_type=MESH)
        pl.semaphore_wait(barrier, len(peers))

    def copy(self, src, dst, sems, where, peer):
        send, recv = sems
        return pltpu.make_async_remote_copy(
            src_ref=src,
            dst_ref=dst,
            send_sem=send.at[where],
            recv_sem=recv.at[where],
            device_id=peer,
            device_id_type=MESH,
        )

    def start(self, copies, group=None):
        for item in copies:
            item.start()
        self.started.setdefault(group, []).extend(copies)

    def sent(self, group):
        for item in self.started.pop(group, []):
            item.wait_send()

    def part(self, unit, half, z, y, x, grad=False):
        every = slice(None)
        if unit < UP:
            first = (SCATTER if grad else GATHER)[unit]
            low, size = ((0, 384), (0, first), (first, 384 - first))[0 if half is None else half + 1]
            if grad and unit in (CK, CV):
                return self.CP.at[unit - CK, z, y, x, every, pl.ds(low, size)]
            columns = pl.ds(pl.multiple_of(384 * self.c + low, 128), size)
            return self.W.at[unit, z, y, x, every, columns]
        if unit == UP:
            return self.W.at[UP + self.c, z, y, x]
        ref = self.HG if grad else self.HD.at[self.c]
        return ref.at[z, y, pl.ds(96 * (unit - DOWN), 96)]

    def half_columns(self, c):
        return pl.ds(pl.multiple_of(384 * c, 128), 384)

    def shards(self):
        found = [(self.self_proj, self.width * j) for j in range(3)] + [(self.self_output, 0)]
        found += [(self.cross_memory, self.width * j) for j in range(2)]
        return found + [(self.cross_query, 0), (self.cross_output, 0)]

    def half_block(self, block, c):
        ref, start = self.shards()[block]
        return ref[:, pl.ds(pl.multiple_of(start + 384 * c, 128), 384)].astype(F32)

    def swapped(self, value):
        return pltpu.roll(value, 64, 1)

    def split_runs(self, whole):
        n = [whole[:, 128 * i : 128 * i + 128] for i in range(6)]
        r = [self.swapped(item) for item in n]
        low = self.is_first
        a = [n[0], jnp.where(low, n[1], r[3]), jnp.where(low, r[3], r[4])]
        b = [jnp.where(low, r[1], r[2]), jnp.where(low, r[2], n[4]), n[5]]
        return jnp.concatenate(a, axis=1), jnp.concatenate(b, axis=1)

    def join_runs(self, left, right):
        a = [left[:, 128 * i : 128 * i + 128] for i in range(3)]
        b = [right[:, 128 * i : 128 * i + 128] for i in range(3)]
        ra, rb = [self.swapped(item) for item in a], [self.swapped(item) for item in b]
        low = self.is_first
        out = [a[0], jnp.where(low, a[1], rb[0]), jnp.where(low, rb[0], rb[1])]
        out += [jnp.where(low, ra[1], ra[2]), jnp.where(low, ra[2], b[1]), b[2]]
        return jnp.concatenate(out, axis=1)

    def up_blocks(self, c):
        found = []
        for j in range(2):
            start = pl.multiple_of(self.width * (2 * c + j), 128)
            found.append(self.split_runs(self.hidden_up[:, pl.ds(start, self.width)].astype(F32)))
        return [jnp.concatenate(item, axis=1) for item in zip(*found)]

    def pair_copies(self):
        c = self.c
        rows = pl.ds(pl.multiple_of(96 * c, 32), 96)
        there = self.HD.at[1 - c, self.z, self.y, rows]
        down = self.hidden_down.at[:, self.half_columns(1 - c)]
        return [
            self.copy(self.PA.at[0], self.PA.at[1], self.s_pair, 0, self.sibling()),
            self.copy(self.PB.at[0], self.PB.at[1], self.s_pair, 1, self.sibling()),
            self.copy(down, there, self.s_pair, 2, self.sibling()),
        ]

    def pair_pack(self):
        c = 1 - self.c
        blocks = [self.half_block(block, c) for block in range(UP)]
        self.PA[0] = jnp.concatenate(blocks, axis=0).astype(LOW)
        self.PB[0] = jnp.concatenate(self.up_blocks(c), axis=0).astype(LOW)

    def in_order(self, mine, theirs):
        even = self.c == 0
        low, high = jnp.where(even, mine, theirs), jnp.where(even, theirs, mine)
        return jnp.concatenate([low, high], axis=0)

    def pair_merge(self):
        c = self.c
        copies = self.pair_copies()
        rows = pl.ds(pl.multiple_of(96 * c, 32), 96)
        self.HD[c, self.z, self.y, rows] = self.hidden_down[:, self.half_columns(c)]
        columns = pl.ds(pl.multiple_of(384 * c, 128), 384)
        copies[0].wait_recv()
        theirs = self.PA[1].astype(F32)
        for block in range(UP):
            both = self.in_order(self.half_block(block, c), theirs[24 * block : 24 * block + 24])
            self.W[block, self.z, self.y, self.x, :, columns] = both.astype(LOW)
        copies[1].wait_recv()
        theirs = self.PB[1].astype(F32)
        both = [
            self.in_order(mine, theirs[24 * i : 24 * i + 24])
            for i, mine in enumerate(self.up_blocks(c))
        ]
        west = self.x == 0
        self.W[UP + c, self.z, self.y, self.x] = jnp.where(west, both[0], both[1]).astype(LOW)
        self.UPS[...] = jnp.where(west, both[1], both[0]).astype(LOW)
        copies[2].wait_recv()

    def up_copies(self):
        there = self.W.at[UP + self.c, self.z, self.y, self.x]
        return [self.copy(self.UPS, there, self.s_up, 0, self.x_peer())]

    def z_copies(self, unit):
        x = slice(None) if unit == UP else self.x
        y = slice(None) if unit == LATE else self.y
        here = self.part(unit, None, self.z, y, x)
        return [
            self.copy(here, here, self.s_z, (unit, k - 1), self.z_peer(k)) for k in (1, 2, 3)
        ]

    def halves(self, unit, table):
        return range(1 if table[unit] == 384 else 2)

    def two_copy(self, unit, half):
        here = self.part(unit, half, slice(None), self.y, self.x)
        peer = (self.x_peer, self.y_peer)[half]()
        return self.copy(here, here, self.s_two, (unit, half), peer)

    def three_copy(self, unit, half):
        every = slice(None)
        if unit >= UP:
            z = self.z if unit == LATE else every
            here = self.part(unit, None, z, self.y, every)
            return self.copy(here, here, self.s_three, (unit, 0), self.y_peer())
        y, x = ((self.y, every), (every, self.x))[half]
        here = self.part(unit, half, every, y, x)
        peer = (self.y_peer, self.x_peer)[half]()
        return self.copy(here, here, self.s_three, (unit, half), peer)

    def three_copies(self, unit):
        halves = (0,) if unit >= UP else self.halves(unit, GATHER)
        return [self.three_copy(unit, half) for half in halves]

    def hand_copies(self, unit):
        every = slice(None)
        whole = self.part(unit, None, every, every, every)
        return [self.copy(whole, whole, self.s_hand, unit, self.sibling())]

    def arrived(self, copies):
        for item in copies:
            item.wait_recv()

    def first(self, unit):
        if unit == UP:
            self.arrived(self.up_copies())
        self.start(self.three_copies(unit) if unit == LATE else self.z_copies(unit), unit)

    def second(self, unit):
        if unit == LATE:
            self.arrived(self.three_copies(unit))
            self.start(self.z_copies(unit), unit)
            return
        self.arrived(self.z_copies(unit))
        if unit < UP:
            copies = [self.two_copy(unit, half) for half in self.halves(unit, GATHER)]
        else:
            copies = self.three_copies(unit)
        self.start(copies, unit)

    def third(self, unit, half):
        if half in self.halves(unit, GATHER):
            self.arrived([self.two_copy(unit, half)])
            self.start([self.three_copy(unit, half)], unit)

    def hand(self, unit):
        self.arrived(self.z_copies(unit) if unit == LATE else self.three_copies(unit))
        self.start(self.hand_copies(unit), unit)

    def done(self, unit):
        self.arrived(self.hand_copies(unit))

    def term(self, unit, half, z=slice(None)):
        first = SCATTER[unit]
        return (unit, z, ..., pl.ds(*((0, first), (first, 384 - first))[half]))

    def rs_one_copy(self, unit, half):
        every = slice(None)
        if unit == LATE:
            here = self.part(unit, None, self.z, 1 - self.y, every, grad=True)
            return self.copy(here, self.RL1, self.s_rs1, (unit, 0), self.y_peer())
        if unit >= UP:
            here = self.part(unit, None, every, 1 - self.y, every, grad=True)
            there = self.RU1 if unit == UP else self.RH1
            return self.copy(here, there, self.s_rs1, (unit, 0), self.y_peer())
        y, x = ((1 - self.y, every), (every, 1 - self.x))[half]
        here = self.part(unit, half, every, y, x, grad=True)
        there = self.R1.at[self.term(unit, half)]
        peer = (self.y_peer, self.x_peer)[half]()
        return self.copy(here, there, self.s_rs1, (unit, half), peer)

    def rs_two_copy(self, unit, half):
        y, x = ((self.y, 1 - self.x), (1 - self.y, self.x))[half]
        here = self.part(unit, half, slice(None), y, x, grad=True)
        there = self.R2.at[self.term(unit, half)]
        peer = (self.x_peer, self.y_peer)[half]()
        return self.copy(here, there, self.s_rs2, (unit, half), peer)

    def rs_three_copies(self, unit):
        out = []
        x = slice(None) if unit == UP else self.x
        y = slice(None) if unit == LATE else self.y
        for k in (1, 2, 3):
            here = self.part(unit, None, self.z_index(k), y, x, grad=True)
            if unit < UP:
                there = self.R3.at[unit, k - 1]
            elif unit == UP:
                there = self.RU3.at[k - 1]
            else:
                there = (self.RL3 if unit == LATE else self.RH3).at[k - 1]
            out.append(self.copy(here, there, self.s_rs3, (unit, k - 1), self.z_peer(k)))
        return out

    def up_back_copies(self):
        return [self.copy(self.UPS, self.UPR, self.s_up, 1, self.x_peer())]

    def grad_columns(self, block):
        return pl.ds(pl.multiple_of(self.width * block + 384 * self.c, 128), 384)

    def rs_four_copies(self, unit):
        c = self.c
        if unit < UP:
            there = self.block_grad.at[:, self.grad_columns(unit)]
            return [self.copy(self.SF.at[unit], there, self.s_rs4, unit, self.sibling())]
        if unit == UP:
            columns = self.half_columns_up()
            return [
                self.copy(
                    self.SFU.at[i],
                    self.UPG.at[self.up_side(i), :, columns],
                    self.s_rs5,
                    i,
                    self.sibling(),
                )
                for i in range(2)
            ]
        there = self.down_out.at[:, self.half_columns(c)]
        return [self.copy(self.SFH, there, self.s_rs4, unit, self.sibling())]

    def up_side(self, i):
        return self.x if i == 0 else 1 - self.x

    def half_columns_up(self):
        return pl.ds(pl.multiple_of(self.width * self.c, 128), self.width)

    def add_into(self, ref, term):
        ref[...] = (ref[...].astype(F32) + term.astype(F32)).astype(LOW)

    def rs_one(self, unit):
        halves = (0,) if unit >= UP else self.halves(unit, SCATTER)
        if unit == LATE:
            self.start(self.rs_three_copies(unit))
        else:
            self.start([self.rs_one_copy(unit, half) for half in halves])

    def rs_two(self, unit, half=0):
        every = slice(None)
        if unit < UP and half not in self.halves(unit, SCATTER):
            return
        if unit == LATE:
            self.arrived(self.rs_three_copies(unit))
            here = self.part(unit, None, self.z, every, self.x, grad=True)
            here[...] = self.sum_of(here[...], [self.RL3[k] for k in range(3)]).astype(LOW)
            self.start([self.rs_one_copy(unit, 0)])
            return
        self.arrived([self.rs_one_copy(unit, half)])

        @pl.loop(0, 4)
        def _(z):
            if unit < UP:
                y, x = ((self.y, every), (every, self.x))[half]
                more = self.R1[self.term(unit, half, z)]
                self.add_into(self.part(unit, half, z, y, x, grad=True), more)
            else:
                more = self.RU1[z] if unit == UP else self.RH1[z]
                self.add_into(self.part(unit, None, z, self.y, every, grad=True), more)

        if unit < UP:
            self.start([self.rs_two_copy(unit, half)])
        else:
            self.start(self.rs_three_copies(unit))

    def rs_three(self, unit):
        halves = self.halves(unit, SCATTER)
        self.arrived([self.rs_two_copy(unit, half) for half in halves])

        @pl.loop(0, 4)
        def _(z):
            for half in halves:
                more = self.R2[self.term(unit, half, z)]
                self.add_into(self.part(unit, half, z, self.y, self.x, grad=True), more)

        self.start(self.rs_three_copies(unit))

    def sum_of(self, value, terms):
        return sum((item.astype(F32) for item in terms), value.astype(F32))

    def rs_total(self, unit):
        x = slice(None) if unit == UP else self.x
        own = self.part(unit, None, self.z, self.y, x, grad=True)
        if unit == LATE:
            self.arrived([self.rs_one_copy(unit, 0)])
            return self.sum_of(own[...], [self.RL1[...]])
        self.arrived(self.rs_three_copies(unit))
        if unit < UP:
            return self.sum_of(own[...], [self.R3[unit, k] for k in range(3)])
        ref = self.RU3 if unit == UP else self.RH3
        return self.sum_of(own[...], [ref[k] for k in range(3)])

    def rs_four(self, unit):
        even = self.c == 0
        if unit < UP:
            total = self.rs_total(unit)
            low, high = total[:24], total[24:]
            self.block_grad[:, self.grad_columns(unit)] = jnp.where(even, low, high)
            self.SF[unit] = jnp.where(even, high, low)
            self.start(self.rs_four_copies(unit))
        if unit == UP:
            total = self.rs_total(unit)
            west = self.x == 0
            self.sent("up")
            self.UPS[...] = jnp.where(west, total[1], total[0]).astype(LOW)
            self.start(self.up_back_copies())
            self.up_rows(0, jnp.where(west, total[0], total[1]))
        if unit == DOWN:
            low, high = self.rs_total(DOWN), self.rs_total(DOWN + 1)
            self.down_out[:, self.half_columns(self.c)] = jnp.where(even, low, high)
            self.SFH[...] = jnp.where(even, high, low)
            self.start(self.rs_four_copies(DOWN))

    def up_rows(self, i, total):
        even = self.c == 0
        low, high = total[:24], total[24:]
        self.UPG[self.up_side(i), :, self.half_columns_up()] = jnp.where(even, low, high)
        self.SFU[i] = jnp.where(even, high, low)

    def rs_up(self):
        self.arrived(self.up_back_copies())
        self.up_rows(1, self.UPR[...].astype(F32))
        self.start(self.rs_four_copies(UP))

    def rs_done(self, unit):
        if unit != DOWN + 1:
            self.arrived(self.rs_four_copies(unit))
        if unit == UP:
            for z in range(4):
                at = slice(384 * z, 384 * z + 384)
                start = self.width * (UP + z)
                both = self.join_runs(self.UPG[0, :, at], self.UPG[1, :, at])
                self.block_grad[:, start : start + self.width] = both

    def sum_copies(self, which, stage):
        peers = [[self.sibling()], [self.x_peer()], [self.y_peer()]]
        peers += [[self.z_peer(k) for k in (1, 2, 3)]]
        return [
            self.copy(
                self.V.at[which, stage],
                self.VR.at[which, stage + i],
                self.s_vec,
                (which, stage + i),
                peer,
            )
            for i, peer in enumerate(peers[stage])
        ]

    def placement(self, dtype, rows):
        own = self.width // NODES
        at = lax.broadcasted_iota(jnp.int32, (rows, self.width), 0)
        feature = lax.broadcasted_iota(jnp.int32, (rows, self.width), 1)
        return ((at < own) & (feature == at + own * self.node)).astype(F32).astype(dtype)

    def sum_start(self, which, stage, value):
        self.V[which, stage] = value
        self.start(self.sum_copies(which, stage))

    def sum_end(self, which, stage):
        now = self.sum_copies(which, stage)
        self.arrived(now)
        value = self.V[which, stage]
        for i in range(len(now)):
            value = value + self.VR[which, stage + i]
        return value

    def keep_left(self, place, value):
        self.LHS[place, self.c] = value
        self.send_left(place)

    def send_left(self, place):
        here = self.LHS.at[place, self.c]
        self.start([self.copy(here, here, self.s_left, place, self.sibling())])

    def keep_right(self, place, value):
        self.RHS[place, self.c] = value
        self.send_right(place)

    def send_right(self, place):
        here = self.RHS.at[place, self.c]
        self.start([self.copy(here, here, self.s_right, place, self.sibling())])

    def left_arrived(self, place):
        if ("left", place) not in self.here:
            self.here.add(("left", place))
            here = self.LHS.at[place, self.c]
            self.copy(here, here, self.s_left, place, self.sibling()).wait_recv()

    def right_arrived(self, place):
        if ("right", place) not in self.here:
            self.here.add(("right", place))
            here = self.RHS.at[place, self.c]
            self.copy(here, here, self.s_right, place, self.sibling()).wait_recv()

    def weight(self, block):
        return self.W[block].reshape(self.width, self.width)

    def weight_grad(self, unit):
        left, right = {QS: (0, 0), KS: (0, 1), VS: (0, 2), SO: (1, 3), CQ: (2, 4), CO: (3, 5)}[unit]
        self.sent(unit)
        self.left_arrived(left)
        self.right_arrived(right)
        columns = self.half_columns(self.c)
        right_all = self.RHS[right, :, :, columns].reshape(2 * self.tokens, 384)
        for t in range(2):
            left_all = self.LHS[left, :, :, pl.ds(384 * t, 384)].reshape(2 * self.tokens, 384)
            part = mm_at(left_all, right_all).astype(LOW)
            self.W[unit, pl.ds(2 * t, 2), :, :, :, columns] = part.reshape(2, 2, 2, 48, 384)

    def up_grad(self):
        c = self.c
        self.sent(UP)
        right_all = self.DH[c].reshape(4 * self.tokens, self.width)
        for t in range(2):
            left_all = self.A3[:, :, :, pl.ds(384 * t, 384)].reshape(4 * self.tokens, 384)
            part = mm_at(left_all, right_all).astype(LOW)
            self.W[UP + c, pl.ds(2 * t, 2)] = part.reshape(2, 2, 2, 48, self.width)

    def down_grad(self):
        right_all = self.G4[:, :, :, self.half_columns(self.c)].reshape(4 * self.tokens, 384)
        for z in range(4):
            j, t = z // 2, z % 2
            left_all = self.U[j, :, :, :, pl.ds(384 * t, 384)].reshape(4 * self.tokens, 384)
            part = mm_at(left_all, right_all).astype(LOW)
            self.HG[z] = part.reshape(2, 192, 384)

    def memory_copy(self, which):
        return self.copy(
            self.CS.at[which], self.CM.at[which], self.s_memory, which, self.sibling()
        )

    def memory_term(self, which, c, t):
        left = self.IMG[:, pl.ds(384 * t, 384)]
        part = mm_at(left, self.KV[which, :, self.half_columns(c)])
        return part.reshape(2, 2, 2, 48, 384)

    def memory_grad_other(self, which):
        for t in range(2):
            part = self.memory_term(which, 1 - self.c, t)
            self.CS[which, pl.ds(2 * t, 2)] = part.astype(LOW)
        self.start([self.memory_copy(which)])

    def memory_grad_own(self, which):
        self.memory_copy(which).wait_recv()
        for t in range(2):
            part = self.memory_term(which, self.c, t)
            part = part + self.CM[which, pl.ds(2 * t, 2)].astype(F32)
            self.CP[which, pl.ds(2 * t, 2)] = part.astype(LOW)

    def masked(self, value):
        return value * self.low_lanes, value * self.high_lanes

    def self_attention(self):
        rows = lax.broadcasted_iota(jnp.int32, (128, 128), 0)
        cols = lax.broadcasted_iota(jnp.int32, (128, 128), 1)
        length = jnp.where(cols < 64, self.lengths[0], self.lengths[1])
        allowed = (lax.div(rows, 64) == lax.div(cols, 64)) & (cols <= rows)
        allowed = allowed & (lax.rem(cols, 64) < length)
        parts = []
        for p in range(self.pairs):
            at = slice(128 * p, 128 * p + 128)
            q, k, v = self.QKV[0, :, at], self.QKV[1, :, at], self.QKV[2, :, at]
            both = mm_bt(q, self.stacked(k)) * 0.125
            probs = []
            for h in range(2):
                s = jnp.where(allowed, both[:, 128 * h : 128 * h + 128], -1000000000.0)
                e = jnp.exp(s - jnp.max(s, axis=-1, keepdims=True))
                probs.append(e / jnp.sum(e, axis=-1, keepdims=True))
            prob = jnp.concatenate(probs, axis=1)
            self.PS[p] = prob
            parts.append(mm(prob.astype(LOW), self.stacked(v)).astype(LOW))
        return jnp.concatenate(parts, axis=1)

    def self_attention_back(self, grad):
        parts = ([], [], [])
        for p in range(self.pairs):
            at = slice(128 * p, 128 * p + 128)
            q, k, v = self.QKV[0, :, at], self.QKV[1, :, at], self.QKV[2, :, at]
            g = grad[:, at]
            prob = self.PS[p]
            dp = mm_bt(g, self.stacked(v))
            prod = prob * dp
            parts_ds = []
            for h in range(2):
                lanes = slice(128 * h, 128 * h + 128)
                inner = jnp.sum(prod[:, lanes], axis=-1, keepdims=True)
                parts_ds.append(prob[:, lanes] * (dp[:, lanes] - inner))
            ds = jnp.concatenate(parts_ds, axis=1).astype(LOW)
            dq = mm(ds, self.stacked(k))
            dk = self.diagonal(mm_at(ds, q), 128)
            dv = self.diagonal(mm_at(prob.astype(LOW), g), 128)
            for out, item in zip(parts, (dq * 0.125, dk * 0.125, dv)):
                out.append(item.astype(LOW))
        return [jnp.concatenate(item, axis=1) for item in parts]

    def stacked(self, value):
        a, b = self.masked(value)
        return jnp.concatenate([a, b], axis=0)

    def diagonal(self, value, rows):
        return jnp.where(self.is_first, value[:rows], value[rows:])

    def stacked_four(self, value):
        zero = jnp.zeros((value.shape[0], 128), LOW)
        left = [jnp.concatenate([item, zero], axis=1) for item in self.masked(value[:, :128])]
        right = [jnp.concatenate([zero, item], axis=1) for item in self.masked(value[:, 128:])]
        return jnp.concatenate(left + right, axis=0)

    def diagonal_four(self, value):
        left = jnp.where(self.is_first, value[:64, :128], value[64:128, :128])
        right = jnp.where(self.is_first, value[128:192, 128:], value[192:, 128:])
        return jnp.concatenate([left, right], axis=1)

    def row_pair(self, ref, place, row):
        return jnp.concatenate([ref[place, row : row + 1], ref[place, row + 1 : row + 2]], axis=1)

    def put_pair(self, ref, place, row, value):
        ref[place, row : row + 1] = value[:, :128]
        ref[place, row + 1 : row + 2] = value[:, 128:]

    def memory_forward(self, which):
        w = self.weight(CK + which)

        @pl.loop(0, 3)
        def _(t):
            size = self.IMG.shape[0] // 3
            rows = pl.ds(pl.multiple_of(size * t, 16), size)
            self.KV[which, rows] = mm(self.IMG[rows], w).astype(LOW)

    def cross_forward(self, place):
        rows = pl.ds(pl.multiple_of(place * self.image_rows, 16), self.image_rows)
        for f in range(self.pairs // 2):
            at = slice(256 * f, 256 * f + 256)
            k, v = self.KV[0, rows, at], self.KV[1, rows, at]
            q = self.stacked_four(self.QA[place, :, at])
            s = mm_bt(k, q) * 0.125
            top = jnp.max(s, axis=0, keepdims=True)
            e = jnp.exp(s - top)
            low = e.astype(LOW)
            self.E[place, f] = low
            self.put_pair(self.ST, place, 2 * f, jnp.sum(e, axis=0, keepdims=True))
            self.put_pair(self.ST, place, 8 + 2 * f, top)
            self.put_pair(self.TOP, place, 2 * f, top)
            num = mm_at(low, v)
            self.NUM[place, :, at] = self.diagonal_four(num).astype(LOW)
        self.ST[place, 6:8] = jnp.ones((2, 128), F32)
        self.ST[place, 14:16] = jnp.zeros((2, 128), F32)

    def cross_backward(self, place):
        rows = pl.ds(pl.multiple_of(place * self.image_rows, 16), self.image_rows)
        for f in range(self.pairs // 2):
            at = slice(256 * f, 256 * f + 256)
            k, v = self.KV[0, rows, at], self.KV[1, rows, at]
            q = self.stacked_four(self.QA[place, :, at])
            g = self.stacked_four(self.GA[place, :, at])
            top = self.row_pair(self.TOP, place, 2 * f)
            share = jnp.exp(top - self.row_pair(self.DL, place, 8 + 2 * f))
            e = self.E[place, f].astype(F32) * share
            ds = e * (mm_bt(v, g) + self.row_pair(self.DL, place, 2 * f))
            ds = ds.astype(LOW)
            dq = mm_at(ds, k)
            self.NUM[place, :, at] = (self.diagonal_four(dq) * 0.125).astype(LOW)
            self.KV[0, rows, at] = (mm(ds, q) * 0.125).astype(LOW)
            self.KV[1, rows, at] = mm(e.astype(LOW), g).astype(LOW)

    def captions_of(self, owner):
        return pl.ds(owner * self.count, self.count)

    def caption(self, bits, j):
        return self.owner(bits) * self.count + j

    def partner(self, bit):
        return (self.wide, jnp.bitwise_xor(self.nar, bit))

    def owner(self, bits):
        return jnp.bitwise_xor(self.nar, bits)

    def once(self, key, copies):
        if key not in self.here:
            self.here.add(key)
            self.arrived(copies())

    def share_copies(self, refs, bit, bits, j):
        where = ((self.N + bits) // (2 * bit) - 1) * self.count + j
        place = self.caption(bits, j)
        peer = self.partner(bit)
        return [self.copy(ref.at[place], ref.at[place], sems, where, peer) for ref, sems in refs]

    def share_start(self, refs, j):
        bit = self.N // 2
        while bit:
            self.start(self.share_copies(refs, bit, 0, j))
            bit //= 2

    def share_wait(self, refs, bits, j):
        if bits:
            bit = bits & -bits
            key = (refs is self.queries, bits, j)
            self.once(key, lambda: self.share_copies(refs, bit, bits - bit, j))

    def share_pass(self, refs, j):
        bit = self.N // 2
        while bit:
            for bits in range(2 * bit, self.N, 2 * bit):
                self.share_wait(refs, bits, j)
                self.start(self.share_copies(refs, bit, bits, j))
            bit //= 2

    def merge_slot(self, bit, bits):
        return self.N - self.N // bit + bits // (2 * bit)

    def merge_copies(self, refs, bit, bits, j):
        slot = self.merge_slot(bit, bits)
        place = self.caption(bits + bit, j)
        where = slot * self.count + j
        peer = self.partner(bit)
        return [
            self.copy(ref.at[place], there.at[slot, j], sems, where, peer)
            for ref, there, sems in refs
        ]

    def merge_start(self, refs, bits, j, group):
        if bits % 2:
            self.start(self.merge_copies(refs, 1, bits - 1, j), group)

    def merge_part(self, refs, join, bit, bits, j, group):
        self.arrived(self.merge_copies(refs, bit, bits, j))
        join(self.caption(bits, j), self.merge_slot(bit, bits), j)
        if bits % (4 * bit):
            self.start(self.merge_copies(refs, 2 * bit, bits - 2 * bit, j), group)

    def merge_far(self, refs, join, j, group):
        bit = 1
        while bit < self.N:
            for bits in reversed(range(2 * bit, self.N, 2 * bit)):
                self.merge_part(refs, join, bit, bits, j, group)
            bit *= 2

    def merge_own(self, refs, join, j, group, low, high):
        bit = low
        while bit < high:
            self.merge_part(refs, join, bit, 0, j, group)
            bit *= 2

    def column(self, turned, p):
        return jnp.where(self.is_first, turned[:64, p : p + 1], turned[64:, p : p + 1])

    def turn(self, *rows):
        have = 8 * len(rows)
        return jnp.concatenate([*rows, jnp.zeros((128 - have, 128), F32)], axis=0).T

    def join_softmax(self, place, slot, j):
        total_a, top_a = self.ST[place, :8], self.ST[place, 8:]
        total_b, top_b = self.STR[slot, j, :8], self.STR[slot, j, 8:]
        top = jnp.maximum(top_a, top_b)
        share_a, share_b = jnp.exp(top_a - top), jnp.exp(top_b - top)
        self.ST[place, :8] = share_a * total_a + share_b * total_b
        self.ST[place, 8:] = top
        turned = self.turn(share_a, share_b)
        for p in range(self.pairs):
            at = slice(128 * p, 128 * p + 128)
            a = self.NUM[place, :, at].astype(F32) * self.column(turned, p)
            b = self.NUMR[slot, j, :, at].astype(F32) * self.column(turned, 8 + p)
            self.NUM[place, :, at] = (a + b).astype(LOW)

    def join_sum(self, place, slot, j):
        self.add_into(self.NUM.at[place], self.NUMR[slot, j])

    def attended(self, j):
        place = self.nar * self.count + j
        turned = self.turn(1.0 / self.ST[place, :8])
        self.SCT[j] = turned
        parts = []
        for p in range(self.pairs):
            at = slice(128 * p, 128 * p + 128)
            parts.append(self.NUM[place, :, at].astype(F32) * self.column(turned, p))
        return jnp.concatenate(parts, axis=1)

    def spread_grad(self, j, doc):
        lane = lax.broadcasted_iota(jnp.int32, (128, 128), 1)
        place = self.nar * self.count + j
        rows = self.rows_of(j)
        turned = self.SCT[j]
        inner = jnp.zeros((128, 128), F32)
        for p in range(self.pairs):
            at = slice(128 * p, 128 * p + 128)
            part = doc[:, at] * self.column(turned, p)
            self.GA[place, :, at] = part.astype(LOW)
            prod = part * self.OCF[rows, at]
            a = jnp.sum(jnp.where(self.is_first, prod, 0.0), axis=1, keepdims=True)
            b = jnp.sum(jnp.where(self.is_first, 0.0, prod), axis=1, keepdims=True)
            inner = jnp.where(lane == p, jnp.concatenate([a, b], axis=0), inner)
        self.DL[place, :8] = -inner.T[:8]
        self.DL[place, 8:] = self.ST[place, 8:]

    def rows_of(self, j):
        return slice(self.seq * j, self.seq * j + self.seq)

    def wide_copy(self, ref, sems, i, j):
        here = ref.at[self.c, 1 - self.x if i == 2 else self.x, self.rows_of(j)]
        peer = self.x_peer() if i == 0 else self.sibling()
        return self.copy(here, here, sems, i * self.count + j, peer)

    def keep_wide(self, ref, value, sems, j):
        ref[self.c, self.x, self.rows_of(j)] = value
        self.start([self.wide_copy(ref, sems, i, j) for i in range(2)])

    def wide_across(self, ref, sems, j):
        self.arrived([self.wide_copy(ref, sems, 0, j)])
        self.start([self.wide_copy(ref, sems, 2, j)])

    def wide_arrived(self, ref, sems):
        for j in range(self.count):
            self.arrived([self.wide_copy(ref, sems, i, j) for i in (1, 2)])

    def hidden_copy(self, ref, j, sems):
        here = ref.at[j, self.c]
        return self.copy(here, here, sems, j, self.sibling())

    def fold_copy(self, which, j):
        at = (which, self.rows_of(j))
        where = which * self.count + j
        return self.copy(self.FS.at[at], self.FR.at[at], self.s_fold, where, self.x_peer())

    def fold_start(self, which):
        self.start([self.fold_copy(which, j) for j in range(self.count)])

    def outward(self, name):
        sem = self.s_out[0].at[self.outs.index(name)]
        return pltpu.make_async_copy(getattr(self, name), self.outer[name], sem)

    def image_copy(self, back):
        src, dst = (self.IMG, self.outer["image_grad"]) if back else (self.outer["images"], self.IMG)
        return pltpu.make_async_copy(src, dst, self.s_image[0].at[0])

    def both_halves(self, value):
        low, high = value[: self.tokens], value[self.tokens :]
        west = self.x == 0
        return jnp.where(west, low, high), jnp.where(west, high, low)

    def do_begin(self):
        self.image_copy(False).start()
        self.pair_pack()
        self.enter()
        self.start(self.pair_copies())
        rows = [getattr(self, name)[...].astype(F32) for name in VECTORS]
        rows = jnp.concatenate(rows + [jnp.zeros((2, rows[0].shape[1]), F32)], axis=0)
        self.sum_start(0, 0, mm(rows.astype(LOW), self.placement(LOW, rows.shape[1])))
        self.pair_merge()
        self.inputs = self.captions[...].astype(F32)
        self.queries = [(self.QA, self.s_query)]
        self.numbers = [(self.NUM, self.NUMR, self.s_num), (self.ST, self.STR, self.s_st)]
        self.grads = [(self.GA, self.s_g), (self.DL, self.s_dl)]
        self.back = [(self.NUM, self.NUMR, self.s_dq)]

    def do_up0(self):
        self.start(self.up_copies(), "up")

    def do_vec(self, stage):
        self.sum_start(0, stage, self.sum_end(0, stage - 1))

    def do_g0(self):
        for j in range(self.count):
            self.keep_wide(self.G4, self.out_grad[self.rows_of(j)], self.s_g4, j)

    def do_g1(self):
        for j in range(self.count):
            self.wide_across(self.G4, self.s_g4, j)

    def do_mem(self, which):
        if "images" not in self.here:
            self.here.add("images")
            self.image_copy(False).wait()
        self.done(CK + which)
        self.memory_forward(which)

    def do_a1(self):
        vectors = self.sum_end(0, 3)
        self.gains = [vectors[i : i + 1] for i in (0, 2, 4)]
        self.shifts = [vectors[i : i + 1] for i in (1, 3, 5)]
        self.rstds = [None, None, []]
        self.r2 = []
        self.a1 = self.normed(0, self.inputs)
        self.keep_left(0, self.a1)

    def normed(self, which, value):
        hat, self.rstds[which], out = norm(value, self.gains[which], self.shifts[which])
        self.HAT[which] = hat
        return out.astype(LOW)

    def pulled(self, which, grad):
        return norm_pull(grad, self.HAT[which], self.rstds[which], self.gains[which])

    def do_qkv(self, which):
        self.done(which)
        self.QKV[which] = mm(self.a1, self.weight(which)).astype(LOW)

    def do_sa(self):
        self.mixed = self.self_attention()
        self.keep_left(1, self.mixed)

    def do_r1(self):
        self.done(SO)
        self.r1 = self.inputs + mm(self.mixed, self.weight(SO))
        self.a2 = self.normed(1, self.r1)
        self.keep_left(2, self.a2)

    def do_cq(self):
        self.done(CQ)
        query = mm(self.a2, self.weight(CQ)).astype(LOW)
        self.QA[self.captions_of(self.nar)] = query.reshape(self.count, 64, self.width)
        for j in range(self.count):
            self.share_start(self.queries, j)

    def do_q1(self, j):
        self.share_pass(self.queries, j)

    def do_cf(self, item):
        bits, j = divmod(item, self.count)
        self.share_wait(self.queries, bits, j)
        self.cross_forward(self.caption(bits, j))
        self.merge_start(self.numbers, bits, j, "numbers")

    def do_m1(self, j):
        self.merge_far(self.numbers, self.join_softmax, j, "numbers")

    def do_m2(self, j):
        self.merge_own(self.numbers, self.join_softmax, j, "numbers", 1, 2)

    def do_a3(self, j):
        self.merge_own(self.numbers, self.join_softmax, j, "numbers", 2, self.N)
        rows = self.rows_of(j)
        full = self.attended(j)
        self.OCF[rows] = full
        oc = full.astype(LOW)
        self.LHS[3, self.c, rows] = oc
        self.once("co", lambda: self.hand_copies(CO))
        r2 = self.r1[rows] + mm(oc, self.weight(CO))
        hat, rstd, out = norm(r2, self.gains[2], self.shifts[2])
        self.HAT[2, rows] = hat
        self.keep_wide(self.A3, out.astype(LOW), self.s_a3, j)
        self.r2.append(r2)
        self.rstds[2].append(rstd)
        if j == self.count - 1:
            self.send_left(3)

    def do_x1(self, j):
        self.wide_across(self.A3, self.s_a3, j)

    def do_hp(self):
        self.done(UP)
        a3 = self.A3[self.c].reshape(2 * self.tokens, self.width)
        for j in range(2):
            hidden = mm(a3, self.weight(UP + j))
            square = hidden * hidden
            tanh = jnp.tanh(GELU_A * hidden * (1.0 + GELU_B * square))
            act = (0.5 * hidden * (1.0 + tanh)).astype(LOW)
            self.SLOPE[j] = 0.5 * (1.0 + tanh) + 0.5 * hidden * (1.0 - tanh * tanh) * (
                GELU_A * (1.0 + 3.0 * GELU_B * square)
            )
            self.U[j, self.c] = act.reshape(2, self.tokens, self.width)
            self.start([self.hidden_copy(self.U, j, self.s_u)])

    def do_dg(self):
        self.wide_arrived(self.G4, self.s_g4)
        for j in range(2):
            self.hidden_copy(self.U, j, self.s_u).wait_recv()
        self.down_grad()

    def do_e3(self):
        self.done(DOWN)
        self.done(DOWN + 1)
        grad = self.G4[self.c].reshape(2 * self.tokens, self.width)
        e3 = 0.0
        for j in range(2):
            down = [self.HD[i, 2 * j : 2 * j + 2].reshape(self.width, 384) for i in range(2)]
            back = mm_bt(grad[:, :384], down[0]) + mm_bt(grad[:, 384:], down[1])
            dhp = (back * self.SLOPE[j]).astype(LOW)
            self.DH[j, self.c] = dhp.reshape(2, self.tokens, self.width)
            self.start([self.hidden_copy(self.DH, j, self.s_dh)])
            e3 = e3 + mm_bt(dhp, self.weight(UP + j))
        self.dr2 = []
        self.e3, other = self.both_halves(e3)
        self.FS[0] = other.astype(LOW)
        self.fold_start(0)

    def do_out(self):
        out = [0.0, 0.0]
        for j in range(2):
            act = self.U[j, self.c].reshape(2 * self.tokens, self.width)
            for i in range(2):
                down = self.HD[i, 2 * j : 2 * j + 2].reshape(self.width, 384)
                out[i] = out[i] + mm(act, down)
        own, other = self.both_halves(jnp.concatenate(out, axis=1))
        self.out = jnp.concatenate(self.r2, axis=0) + own
        self.FS[1] = other.astype(LOW)
        self.fold_start(1)

    def do_lo(self):
        self.arrived([self.fold_copy(1, j) for j in range(self.count)])
        self.layer_out[...] = (self.out + self.FR[1].astype(F32)).astype(LOW)
        self.outward("layer_out").start()

    def do_ug(self):
        self.wide_arrived(self.A3, self.s_a3)
        for j in range(2):
            self.hidden_copy(self.DH, j, self.s_dh).wait_recv()
        self.up_grad()

    def do_dr2(self, j):
        self.arrived([self.fold_copy(0, j)])
        rows = self.rows_of(j)
        e3 = self.e3[rows] + self.FR[0, rows].astype(F32)
        back, *vec = norm_pull(e3, self.HAT[2, rows], self.rstds[2][j], self.gains[2])
        self.vec3 = [a + b for a, b in zip(self.vec3, vec)] if j else vec
        dr2 = self.out_grad[rows].astype(F32) + back
        self.dr2.append(dr2)
        dcat = dr2.astype(LOW)
        self.RHS[5, self.c, rows] = dcat
        self.spread_grad(j, mm_bt(dcat, self.weight(CO)))
        self.share_start(self.grads, j)
        if j == self.count - 1:
            self.send_right(5)

    def do_p1(self, j):
        self.share_pass(self.grads, j)

    def do_cb(self, item):
        bits, j = divmod(item, self.count)
        self.share_wait(self.grads, bits, j)
        self.sent("numbers")
        self.cross_backward(self.caption(bits, j))
        self.merge_start(self.back, bits, j, "back")

    def do_n1(self, j):
        self.merge_far(self.back, self.join_sum, j, "back")

    def do_n2(self, j):
        self.merge_own(self.back, self.join_sum, j, "back", 1, 2)

    def do_dq(self):
        for j in range(self.count):
            self.merge_own(self.back, self.join_sum, j, "back", 2, self.N)
        dqc = self.NUM[self.captions_of(self.nar)].reshape(self.tokens, self.width)
        self.keep_right(4, dqc)
        back, *self.vec2 = self.pulled(1, mm_bt(dqc, self.weight(CQ)))
        self.dr1 = jnp.concatenate(self.dr2, axis=0) + back
        dattn = self.dr1.astype(LOW)
        self.keep_right(3, dattn)
        self.dos = mm_bt(dattn, self.weight(SO)).astype(LOW)

    def do_mo(self, which):
        self.memory_grad_other(which)

    def do_mw(self, which):
        self.memory_grad_own(which)

    def do_wg(self, unit):
        self.weight_grad(unit)

    def do_sb(self):
        e1 = 0.0
        for j, item in enumerate(self.self_attention_back(self.dos)):
            self.keep_right(j, item)
            e1 = e1 + mm_bt(item, self.weight(j))
        back, *vec = self.pulled(0, e1)
        self.input_grad[...] = (self.dr1 + back).astype(LOW)
        self.outward("input_grad").start()
        vec = vec + self.vec2 + self.vec3 + [jnp.zeros((2, self.width), F32)]
        self.sum_start(1, 0, jnp.concatenate(vec, axis=0))

    def do_sum(self, stage):
        self.sum_start(1, stage, self.sum_end(1, stage - 1))

    def do_img(self):
        @pl.loop(0, 3)
        def _(t):
            size = self.IMG.shape[0] // 3
            rows = pl.ds(pl.multiple_of(size * t, 16), size)
            part = mm_bt(self.KV[0, rows], self.weight(CK))
            part = part + mm_bt(self.KV[1, rows], self.weight(CV))
            self.IMG[rows] = part.astype(LOW)

        self.image_copy(True).start()

    def do_end(self):
        self.vec_grad[...] = lax.dot_general(
            self.sum_end(1, 3),
            self.placement(F32, 128),
            (((1,), (1,)), ((), ())),
            precision=lax.Precision.HIGHEST,
            preferred_element_type=F32,
        )
        self.outward("vec_grad").start()
        for unit in range(UNITS):
            self.rs_done(unit)
        self.outward("block_grad").start()
        self.outward("down_out").start()
        self.image_copy(True).wait()
        for name in self.outs:
            self.outward(name).wait()
        for group in list(self.started):
            self.sent(group)

    def run(self):
        steps = {
            Step.begin: self.do_begin,
            Step.up0: self.do_up0,
            Step.vec: self.do_vec,
            Step.g0: self.do_g0,
            Step.g1: self.do_g1,
            Step.mem: self.do_mem,
            Step.a1: self.do_a1,
            Step.qkv: self.do_qkv,
            Step.sa: self.do_sa,
            Step.r1: self.do_r1,
            Step.cq: self.do_cq,
            Step.q1: self.do_q1,
            Step.cf: self.do_cf,
            Step.m1: self.do_m1,
            Step.m2: self.do_m2,
            Step.a3: self.do_a3,
            Step.x1: self.do_x1,
            Step.hp: self.do_hp,
            Step.dg: self.do_dg,
            Step.e3: self.do_e3,
            Step.out: self.do_out,
            Step.lo: self.do_lo,
            Step.ug: self.do_ug,
            Step.dr2: self.do_dr2,
            Step.p1: self.do_p1,
            Step.cb: self.do_cb,
            Step.n1: self.do_n1,
            Step.n2: self.do_n2,
            Step.dq: self.do_dq,
            Step.mo: self.do_mo,
            Step.mw: self.do_mw,
            Step.wg: self.do_wg,
            Step.sb: self.do_sb,
            Step.sum: self.do_sum,
            Step.img: self.do_img,
            Step.end: self.do_end,
            Step.F: self.first,
            Step.S: self.second,
            Step.TA: lambda unit: self.third(unit, 0),
            Step.TB: lambda unit: self.third(unit, 1),
            Step.H: self.hand,
            Step.R1: self.rs_one,
            Step.RA: self.rs_two,
            Step.RB: lambda unit: self.rs_two(unit, 1),
            Step.R3: self.rs_three,
            Step.R4: self.rs_four,
            Step.RU: lambda unit: self.rs_up(),
        }
        for step, *place in ORDER:
            steps[step](*place)


def layer_call(lanes, narrow, captions, images, lengths, out_grad, *params):
    tokens, width = captions.shape
    count = tokens // 64
    groups = narrow * count
    image_rows = images.shape[0]
    pairs = width // 128
    ins = ["captions", "out_grad", "self_proj", "self_output"]
    ins += ["cross_query", "cross_memory", "cross_output", "hidden_up", "hidden_down", *VECTORS]
    given = dict(zip(ins, (captions, out_grad, *params)))
    outs = {
        "layer_out": ((tokens, width), LOW),
        "input_grad": ((tokens, width), LOW),
        "image_grad": ((image_rows, width), LOW),
        "block_grad": ((24, 12 * width), F32),
        "down_out": ((96, width), F32),
        "vec_grad": ((8, 128), F32),
    }
    results = [name for name in outs if name != "image_grad"]
    memory = {name: outs[name] for name in results}
    memory |= {
        "W": ((10, 4, 2, 2, 48, width), LOW),
        "HD": ((2, 4, 2, 192, 384), LOW),
        "HG": ((4, 2, 192, 384), LOW),
        "UPS": ((48, width), LOW),
        "UPR": ((48, width), LOW),
        "PA": ((2, 24 * UP, 384), LOW),
        "PB": ((2, 48, width), LOW),
        "IMG": ((image_rows, width), LOW),
        "KV": ((2, image_rows, width), LOW),
        "E": ((groups, pairs // 2, image_rows // groups, 256), LOW),
        "LHS": ((4, 2, tokens, width), LOW),
        "RHS": ((6, 2, tokens, width), LOW),
        "A3": ((2, 2, tokens, width), LOW),
        "G4": ((2, 2, tokens, width), LOW),
        "U": ((2, 2, 2, tokens, width), LOW),
        "DH": ((2, 2, 2, tokens, width), LOW),
        "FS": ((2, tokens, width), LOW),
        "FR": ((2, tokens, width), LOW),
        "R1": ((UP, 4, 2, 48, 384), LOW),
        "R2": ((UP, 4, 48, 384), LOW),
        "R3": ((UP, 3, 48, 384), LOW),
        "RU1": ((4, 2, 48, width), LOW),
        "RU3": ((3, 2, 48, width), LOW),
        "RH1": ((4, 96, 384), LOW),
        "RH3": ((3, 96, 384), LOW),
        "RL1": ((96, 384), LOW),
        "RL3": ((3, 2, 96, 384), LOW),
        "CM": ((2, 4, 2, 2, 48, 384), LOW),
        "CS": ((2, 4, 2, 2, 48, 384), LOW),
        "CP": ((2, 4, 2, 2, 48, 384), LOW),
        "SF": ((UP, 24, 384), F32),
        "SFU": ((2, 24, width), F32),
        "UPG": ((2, 24, 2 * width), F32),
        "SFH": ((96, 384), F32),
        "V": ((2, 4, 8, width), F32),
        "VR": ((2, 6, 8, width), F32),
        "QKV": ((3, tokens, width), LOW),
        "PS": ((HEADS // 2, 128, 256), F32),
        "HAT": ((3, tokens, width), F32),
        "SLOPE": ((2, 2 * tokens, width), F32),
        "OCF": ((tokens, width), F32),
        "QA": ((groups, 64, width), LOW),
        "NUM": ((groups, 64, width), LOW),
        "ST": ((groups, 16, 128), F32),
        "TOP": ((groups, 8, 128), F32),
        "NUMR": ((narrow - 1, count, 64, width), LOW),
        "STR": ((narrow - 1, count, 16, 128), F32),
        "SCT": ((count, 128, 128), F32),
        "GA": ((groups, 64, width), LOW),
        "DL": ((groups, 16, 128), F32),
    }
    signals = {
        "s_pair": (3,),
        "s_up": (2,),
        "s_z": (UNITS, 3),
        "s_two": (UP, 2),
        "s_three": (UNITS, 2),
        "s_hand": (UNITS,),
        "s_rs1": (UNITS, 2),
        "s_rs2": (UP, 2),
        "s_rs3": (UNITS, 3),
        "s_rs4": (UNITS,),
        "s_rs5": (2,),
        "s_vec": (2, 6),
        "s_left": (4,),
        "s_right": (6,),
        "s_a3": (3 * count,),
        "s_g4": (3 * count,),
        "s_u": (2,),
        "s_dh": (2,),
        "s_fold": (2 * count,),
        "s_memory": (2,),
        "s_query": ((narrow - 1) * count,),
        "s_num": ((narrow - 1) * count,),
        "s_st": ((narrow - 1) * count,),
        "s_g": ((narrow - 1) * count,),
        "s_dl": ((narrow - 1) * count,),
        "s_dq": ((narrow - 1) * count,),
        "s_image": (1,),
        "s_out": (len(results),),
    }
    scratch = [pltpu.VMEM(shape, kind) for shape, kind in memory.values()]
    for shape in signals.values():
        scratch += [pltpu.SemaphoreType.DMA(shape)] * 2

    def body(*refs):
        names = ["lengths", "images", *ins, *outs]
        outer = dict(zip(names, refs))
        named = dict(zip(memory, refs[len(names) :]))
        rest = refs[len(names) + len(memory) :]
        for i, name in enumerate(signals):
            named[name] = (rest[2 * i], rest[2 * i + 1])
        named |= {name: outer[name] for name in ["lengths", *ins]}
        named |= {"outer": outer, "outs": results}
        Layer(named, lanes, narrow).run()

    anywhere = pl.BlockSpec(memory_space=pl.ANY)
    vmem = pl.BlockSpec(memory_space=pltpu.VMEM)
    return pl.pallas_call(
        body,
        out_shape=[jax.ShapeDtypeStruct(shape, kind) for shape, kind in outs.values()],
        in_specs=[pl.BlockSpec(memory_space=pltpu.SMEM), anywhere] + [vmem] * len(ins),
        out_specs=[anywhere] * len(outs),
        scratch_shapes=scratch,
        compiler_params=pltpu.CompilerParams(
            collective_id=0, has_side_effects=True, vmem_limit_bytes=VMEM_LIMIT
        ),
        cost_estimate=pl.CostEstimate(
            flops=17 * 10**9, bytes_accessed=8 * 10**6, transcendentals=2 * 10**6
        ),
        name="layer",
    )(lengths, images, *given.values())


def deliver(ranges, arrays, block_grad, vec_grad, own):
    count = len(arrays)
    ins = [vec_grad, block_grad, *arrays]
    outs = [jax.ShapeDtypeStruct((1, own), F32)] * len(VECTORS)
    outs += [jax.ShapeDtypeStruct((block_grad.shape[0], b - a), F32) for a, b in ranges]
    outs += [jax.ShapeDtypeStruct(item.shape, item.dtype) for item in arrays]

    def body(*refs):
        given, found = refs[: len(ins)], refs[len(ins) : len(ins) + len(outs)]
        rest = refs[len(ins) + len(outs) :]
        held, rows, sems = rest[: len(ins)], rest[len(ins) : -1], rest[-1]
        copies = zip(given, held)
        into = [pltpu.make_async_copy(a, b, sems.at[i]) for i, (a, b) in enumerate(copies)]
        for item in into:
            item.start()
        views = [*rows, *[held[1].at[:, pl.ds(a, b - a)] for a, b in ranges], *held[2:]]
        back = [
            pltpu.make_async_copy(a, b, sems.at[len(ins) + i])
            for i, (a, b) in enumerate(zip(views, found))
        ]
        into[0].wait()
        for i, ref in enumerate(rows):
            ref[...] = held[0][i : i + 1, :own]
            back[i].start()
        into[1].wait()
        for item in back[len(rows) : len(rows) + len(ranges)]:
            item.start()
        for item, last in zip(into[2:], back[len(rows) + len(ranges) :]):
            item.wait()
            last.start()
        for item in back:
            item.wait()

    hold = [pltpu.VMEM(item.shape, item.dtype) for item in ins]
    hold += [pltpu.VMEM((1, own), F32)] * len(VECTORS)
    anywhere = pl.BlockSpec(memory_space=pl.ANY)
    return pl.pallas_call(
        body,
        out_shape=outs,
        in_specs=[anywhere] * len(ins),
        out_specs=[anywhere] * len(outs),
        scratch_shapes=hold + [pltpu.SemaphoreType.DMA((len(ins) + len(outs),))],
        compiler_params=pltpu.CompilerParams(vmem_limit_bytes=VMEM_LIMIT),
        name="deliver",
    )(*ins)


def lane_gather(value, lanes, narrow, axis):
    if lanes == 1:
        return value
    assert lanes % narrow == 0
    value = lax.all_gather(value, "narrow", axis=axis, tiled=True)
    step = 1
    wide_count = lax.axis_size("wide")
    while step * narrow < lanes:
        swap = [(i, i ^ step) for i in range(wide_count)]
        other = lax.ppermute(value, "wide", swap)
        low = (lax.axis_index("wide") // step) % 2 == 0
        first = jnp.where(low, value, other)
        second = jnp.where(low, other, value)
        value = jnp.concatenate([first, second], axis=axis)
        step *= 2
    return value


def lane_scatter(value, lanes, narrow, axis):
    if lanes == 1:
        return value
    wide_count = lax.axis_size("wide")
    step = lanes // narrow
    while step > 1:
        step //= 2
        swap = [(i, i ^ step) for i in range(wide_count)]
        first, second = jnp.split(value, 2, axis=axis)
        low = (lax.axis_index("wide") // step) % 2 == 0
        other = lax.ppermute(jnp.where(low, second, first), "wide", swap)
        value = jnp.where(low, first, second) + other
    return lax.psum_scatter(value, "narrow", scatter_dimension=axis, tiled=True)


def per_device(captions, images, lengths, out_grad, *params):
    narrow = lax.axis_size("narrow")
    devices = lax.axis_size("wide") * narrow
    lanes = devices // NODES
    count, seq_len, width = captions.shape
    tokens = count * seq_len
    params = [lane_gather(item, lanes, narrow, 0) for item in params]
    out, input_grad, image_grad, block_grad, down_grad, vec_grad = layer_call(
        lanes,
        narrow,
        captions.reshape(tokens, width),
        images.reshape(-1, width),
        lengths,
        out_grad.reshape(tokens, width),
        *params[:7],
        *[item.reshape(1, -1) for item in params[7:]],
    )
    block_grad = lane_scatter(block_grad, lanes, narrow, 0)
    down_grad = lane_scatter(down_grad, lanes, narrow, 0)
    if lanes > 1:
        vec_grad = lane_scatter(vec_grad[:, : width // NODES], lanes, narrow, 1)

    ends = (QS, SO, CK, CQ, CO, UP, UP + 4)
    ranges = [(width * a, width * b) for a, b in zip(ends, ends[1:])]
    arrays = [out, input_grad, image_grad, down_grad]
    own = width // devices
    found = deliver(ranges, arrays, block_grad, vec_grad, own)
    vectors, found = found[: len(VECTORS)], found[len(VECTORS) :]
    joint, self_out, memory, query, cross, up = found[:6]
    out, input_grad, image_grad, down_grad = found[6:]
    return (
        out.reshape(captions.shape),
        input_grad.reshape(captions.shape),
        image_grad.reshape(images.shape),
        joint,
        self_out,
        query,
        memory,
        cross,
        up,
        down_grad,
        *[item.reshape(-1) for item in vectors],
    )


def solution(mesh):
    both = ("wide", "narrow")
    rows = P(both, None)
    text = P(both, None, None)
    vector = P(both)
    image = P("wide", "narrow", None)
    in_specs = (text, image, vector, text) + (rows,) * 7 + (vector,) * 6
    out_specs = (text, text, image) + (rows,) * 7 + (vector,) * 6
    return jax.shard_map(
        per_device, mesh=mesh, in_specs=in_specs, out_specs=out_specs, check_vma=False
    )
```

```python
import functools

import jax
import jax.numpy as jnp
from jax import lax
from jax.experimental import pallas as pl
from jax.experimental.pallas import tpu as pltpu
from jax.sharding import PartitionSpec as P

HEADS = 12
NODES = 32
UNITS = 11
VMEM_LIMIT = 64 * 1024 * 1024 - 65536
MESH = pl.DeviceIdType.MESH
F32 = jnp.float32
LOW = jnp.bfloat16
EPSILON = 1e-05
GELU_A = 0.7978845608028654
GELU_B = 0.044715

QS, KS, VS, SO, CK, CV, CQ, CO, UP = 0, 1, 2, 3, 4, 5, 6, 7, 8
DOWN = UP + 1
LATE = DOWN + 1
GATHER = (128, 256) * 4
SCATTER = (256, 128) * 4


VECTORS = ["first_gain", "first_shift", "second_gain", "second_shift"]
VECTORS += ["third_gain", "third_shift"]


class Step:
    (
        begin,
        up0,
        vec,
        g0,
        g1,
        mem,
        a1,
        qkv,
        sa,
        r1,
        cq,
        q1,
        cf,
        m1,
        m2,
        a3,
        x1,
        hp,
        dg,
        e3,
        out,
        lo,
        ug,
        dr2,
        p1,
        cb,
        n1,
        n2,
        dq,
        mo,
        mw,
        wg,
        sb,
        sum,
        img,
        end,
        F,
        S,
        TA,
        TB,
        H,
        R1,
        RA,
        RB,
        R3,
        R4,
        RU,
    ) = range(47)


ORDER = [
    (Step.begin,), (Step.F, 1), (Step.up0,), (Step.vec, 1), (Step.g0,), (Step.F, 0), (Step.vec, 2),
    (Step.F, 3), (Step.S, 1), (Step.F, 2), (Step.S, 0), (Step.F, 5), (Step.TA, 1), (Step.vec, 3),
    (Step.S, 3), (Step.TA, 0), (Step.F, 6), (Step.TB, 0), (Step.S, 2), (Step.F, 4), (Step.TA, 3),
    (Step.S, 5), (Step.TB, 1), (Step.F, 7), (Step.F, 8), (Step.S, 6), (Step.TB, 2), (Step.TA, 2),
    (Step.S, 4), (Step.TA, 6), (Step.TB, 3), (Step.H, 1), (Step.a1,), (Step.qkv, 1), (Step.H, 0),
    (Step.TB, 5), (Step.TA, 5), (Step.TA, 4), (Step.qkv, 0), (Step.F, 10), (Step.H, 2),
    (Step.TB, 6), (Step.qkv, 2), (Step.sa,), (Step.TB, 4), (Step.H, 3), (Step.r1,), (Step.F, 9),
    (Step.H, 6), (Step.S, 8), (Step.g1,), (Step.S, 7), (Step.H, 5), (Step.S, 10), (Step.cq,),
    (Step.H, 4), (Step.mem, 1), (Step.mem, 0), (Step.cf, 0), (Step.q1, 0), (Step.cf, 3),
    (Step.cf, 6), (Step.q1, 1), (Step.TA, 7), (Step.TB, 7), (Step.cf, 4), (Step.cf, 2),
    (Step.cf, 7), (Step.m1, 0), (Step.cf, 5), (Step.H, 8), (Step.m2, 0), (Step.m1, 1), (Step.H, 7),
    (Step.S, 9), (Step.cf, 1), (Step.a3, 0), (Step.m2, 1), (Step.a3, 1), (Step.H, 10),
    (Step.x1, 0), (Step.H, 9), (Step.x1, 1), (Step.hp,), (Step.e3,), (Step.dg,), (Step.R1, 10),
    (Step.R1, 9), (Step.ug,), (Step.dr2, 0), (Step.R1, 8), (Step.dr2, 1), (Step.cb, 0),
    (Step.RA, 9), (Step.out,), (Step.cb, 3), (Step.p1, 0), (Step.wg, 7), (Step.cb, 1),
    (Step.cb, 2), (Step.p1, 1), (Step.R1, 7), (Step.cb, 6), (Step.cb, 5), (Step.cb, 7),
    (Step.n1, 1), (Step.cb, 4), (Step.n2, 1), (Step.mo, 0), (Step.n2, 0), (Step.n1, 0),
    (Step.RB, 7), (Step.mo, 1), (Step.mw, 0), (Step.R1, 4), (Step.RA, 7), (Step.mw, 1),
    (Step.R1, 5), (Step.RA, 8), (Step.dq,), (Step.sb,), (Step.wg, 3), (Step.R1, 3), (Step.wg, 1),
    (Step.RB, 4), (Step.R3, 7), (Step.wg, 2), (Step.R1, 2), (Step.sum, 1), (Step.RA, 3),
    (Step.RB, 5), (Step.wg, 0), (Step.RA, 5), (Step.R1, 0), (Step.RA, 4), (Step.RB, 2),
    (Step.RA, 2), (Step.sum, 2), (Step.R3, 5), (Step.R1, 1), (Step.R4, 8), (Step.R3, 4),
    (Step.RB, 0), (Step.RA, 10), (Step.wg, 6), (Step.RB, 3), (Step.sum, 3), (Step.R1, 6),
    (Step.R4, 5), (Step.R3, 2), (Step.RA, 1), (Step.RA, 0), (Step.R4, 9), (Step.RB, 1),
    (Step.R3, 3), (Step.R4, 2), (Step.img,), (Step.R3, 0), (Step.RA, 6), (Step.RB, 6),
    (Step.R3, 1), (Step.R4, 4), (Step.R3, 6), (Step.R4, 3), (Step.R4, 1), (Step.R4, 7),
    (Step.R4, 0), (Step.lo,), (Step.RU, 8), (Step.R4, 6), (Step.end,),
]


def mm(left, right):
    return jnp.dot(left, right, preferred_element_type=F32)


def mm_bt(left, right):
    return lax.dot_general(left, right, (((1,), (1,)), ((), ())), preferred_element_type=F32)


def mm_at(left, right):
    return lax.dot_general(left, right, (((0,), (0,)), ((), ())), preferred_element_type=F32)


def norm(value, gain, shift):
    centred = value - jnp.mean(value, axis=-1, keepdims=True)
    rstd = lax.rsqrt(jnp.mean(centred * centred, axis=-1, keepdims=True) + EPSILON)
    hat = centred * rstd
    return hat, rstd, hat * gain + shift


def norm_pull(grad, hat, rstd, gain):
    scaled = grad * gain
    inner = jnp.mean(scaled * hat, axis=-1, keepdims=True)
    back = rstd * (scaled - jnp.mean(scaled, axis=-1, keepdims=True) - hat * inner)
    gain_grad = jnp.sum(grad * hat, axis=0, keepdims=True)
    shift_grad = jnp.sum(grad, axis=0, keepdims=True)
    return back, gain_grad, shift_grad


class Layer:
    def __init__(self, refs, lanes, narrow):
        self.__dict__.update(refs)
        self.N = narrow
        self.lanes = lanes
        wide, nar = lax.axis_index("wide"), lax.axis_index("narrow")
        flat = wide * narrow + nar
        self.wide, self.nar = wide, nar
        self.node = lax.div(flat, lanes)
        self.lane = lax.rem(flat, lanes)
        node = self.node
        self.c = lax.rem(node, 2)
        self.x = lax.rem(lax.div(node, 2), 2)
        self.y = lax.rem(lax.div(node, 4), 2)
        self.z = lax.div(node, 8)
        self.started = {}
        self.here = set()
        self.count, self.seq = self.captions.shape[0] // 64, 64
        self.tokens, self.width = self.captions.shape
        self.groups = self.QA.shape[0]
        self.image_rows = self.IMG.shape[0] // self.groups
        self.pairs = self.width // 128
        lane = lax.broadcasted_iota(jnp.int32, (1, 128), 1)
        self.low_lanes = (lane < 64).astype(F32).astype(LOW)
        self.high_lanes = (lane >= 64).astype(F32).astype(LOW)
        self.is_first = lane < 64

    def device(self, z, y, x, c):
        flat = (z * 8 + y * 4 + x * 2 + c) * self.lanes + self.lane
        return (lax.div(flat, self.N), lax.rem(flat, self.N))

    def sibling(self):
        return self.device(self.z, self.y, self.x, 1 - self.c)

    def x_peer(self):
        return self.device(self.z, self.y, 1 - self.x, self.c)

    def y_peer(self):
        return self.device(self.z, 1 - self.y, self.x, self.c)

    def z_index(self, k):
        return lax.rem(self.z + k, 4)

    def z_peer(self, k):
        return self.device(self.z_index(k), self.y, self.x, self.c)

    def n_index(self, k):
        return lax.rem(self.nar + k, self.N)

    def n_peer(self, k):
        return (self.wide, self.n_index(k))

    def enter(self):
        barrier = pltpu.get_barrier_semaphore()
        peers = [self.sibling(), self.x_peer(), self.y_peer()]
        peers += [self.z_peer(k) for k in (1, 2, 3)]
        peers += [self.n_peer(k) for k in range(1, self.N)]
        for peer in peers:
            pl.semaphore_signal(barrier, inc=1, device_id=peer, device_id_type=MESH)
        pl.semaphore_wait(barrier, len(peers))

    def copy(self, src, dst, sems, where, peer):
        send, recv = sems
        return pltpu.make_async_remote_copy(
            src_ref=src,
            dst_ref=dst,
            send_sem=send.at[where],
            recv_sem=recv.at[where],
            device_id=peer,
            device_id_type=MESH,
        )

    def start(self, copies, group=None):
        for item in copies:
            item.start()
        self.started.setdefault(group, []).extend(copies)

    def sent(self, group):
        for item in self.started.pop(group, []):
            item.wait_send()

    def part(self, unit, half, z, y, x, grad=False):
        every = slice(None)
        if unit < UP:
            first = (SCATTER if grad else GATHER)[unit]
            low, size = ((0, 384), (0, first), (first, 384 - first))[0 if half is None else half + 1]
            if grad and unit in (CK, CV):
                return self.CP.at[unit - CK, z, y, x, every, pl.ds(low, size)]
            columns = pl.ds(pl.multiple_of(384 * self.c + low, 128), size)
            return self.W.at[unit, z, y, x, every, columns]
        if unit == UP:
            return self.W.at[UP + self.c, z, y, x]
        ref = self.HG if grad else self.HD.at[self.c]
        return ref.at[z, y, pl.ds(96 * (unit - DOWN), 96)]

    def half_columns(self, c):
        return pl.ds(pl.multiple_of(384 * c, 128), 384)

    def shards(self):
        found = [(self.self_proj, self.width * j) for j in range(3)] + [(self.self_output, 0)]
        found += [(self.cross_memory, self.width * j) for j in range(2)]
        return found + [(self.cross_query, 0), (self.cross_output, 0)]

    def half_block(self, block, c):
        ref, start = self.shards()[block]
        return ref[:, pl.ds(pl.multiple_of(start + 384 * c, 128), 384)].astype(F32)

    def swapped(self, value):
        return pltpu.roll(value, 64, 1)

    def split_runs(self, whole):
        n = [whole[:, 128 * i : 128 * i + 128] for i in range(6)]
        r = [self.swapped(item) for item in n]
        low = self.is_first
        a = [n[0], jnp.where(low, n[1], r[3]), jnp.where(low, r[3], r[4])]
        b = [jnp.where(low, r[1], r[2]), jnp.where(low, r[2], n[4]), n[5]]
        return jnp.concatenate(a, axis=1), jnp.concatenate(b, axis=1)

    def join_runs(self, left, right):
        a = [left[:, 128 * i : 128 * i + 128] for i in range(3)]
        b = [right[:, 128 * i : 128 * i + 128] for i in range(3)]
        ra, rb = [self.swapped(item) for item in a], [self.swapped(item) for item in b]
        low = self.is_first
        out = [a[0], jnp.where(low, a[1], rb[0]), jnp.where(low, rb[0], rb[1])]
        out += [jnp.where(low, ra[1], ra[2]), jnp.where(low, ra[2], b[1]), b[2]]
        return jnp.concatenate(out, axis=1)

    def up_blocks(self, c):
        found = []
        for j in range(2):
            start = pl.multiple_of(self.width * (2 * c + j), 128)
            found.append(self.split_runs(self.hidden_up[:, pl.ds(start, self.width)].astype(F32)))
        return [jnp.concatenate(item, axis=1) for item in zip(*found)]

    def pair_copies(self):
        c = self.c
        rows = pl.ds(pl.multiple_of(96 * c, 32), 96)
        there = self.HD.at[1 - c, self.z, self.y, rows]
        down = self.hidden_down.at[:, self.half_columns(1 - c)]
        return [
            self.copy(self.PA.at[0], self.PA.at[1], self.s_pair, 0, self.sibling()),
            self.copy(self.PB.at[0], self.PB.at[1], self.s_pair, 1, self.sibling()),
            self.copy(down, there, self.s_pair, 2, self.sibling()),
        ]

    def pair_pack(self):
        c = 1 - self.c
        blocks = [self.half_block(block, c) for block in range(UP)]
        self.PA[0] = jnp.concatenate(blocks, axis=0).astype(LOW)
        self.PB[0] = jnp.concatenate(self.up_blocks(c), axis=0).astype(LOW)

    def in_order(self, mine, theirs):
        even = self.c == 0
        low, high = jnp.where(even, mine, theirs), jnp.where(even, theirs, mine)
        return jnp.concatenate([low, high], axis=0)

    def pair_merge(self):
        c = self.c
        copies = self.pair_copies()
        rows = pl.ds(pl.multiple_of(96 * c, 32), 96)
        self.HD[c, self.z, self.y, rows] = self.hidden_down[:, self.half_columns(c)]
        columns = pl.ds(pl.multiple_of(384 * c, 128), 384)
        copies[0].wait_recv()
        theirs = self.PA[1].astype(F32)
        for block in range(UP):
            both = self.in_order(self.half_block(block, c), theirs[24 * block : 24 * block + 24])
            self.W[block, self.z, self.y, self.x, :, columns] = both.astype(LOW)
        copies[1].wait_recv()
        theirs = self.PB[1].astype(F32)
        both = [
            self.in_order(mine, theirs[24 * i : 24 * i + 24])
            for i, mine in enumerate(self.up_blocks(c))
        ]
        west = self.x == 0
        self.W[UP + c, self.z, self.y, self.x] = jnp.where(west, both[0], both[1]).astype(LOW)
        self.UPS[...] = jnp.where(west, both[1], both[0]).astype(LOW)
        copies[2].wait_recv()

    def up_copies(self):
        there = self.W.at[UP + self.c, self.z, self.y, self.x]
        return [self.copy(self.UPS, there, self.s_up, 0, self.x_peer())]

    def z_copies(self, unit):
        x = slice(None) if unit == UP else self.x
        y = slice(None) if unit == LATE else self.y
        here = self.part(unit, None, self.z, y, x)
        return [
            self.copy(here, here, self.s_z, (unit, k - 1), self.z_peer(k)) for k in (1, 2, 3)
        ]

    def halves(self, unit, table):
        return range(1 if table[unit] == 384 else 2)

    def two_copy(self, unit, half):
        here = self.part(unit, half, slice(None), self.y, self.x)
        peer = (self.x_peer, self.y_peer)[half]()
        return self.copy(here, here, self.s_two, (unit, half), peer)

    def three_copy(self, unit, half):
        every = slice(None)
        if unit >= UP:
            z = self.z if unit == LATE else every
            here = self.part(unit, None, z, self.y, every)
            return self.copy(here, here, self.s_three, (unit, 0), self.y_peer())
        y, x = ((self.y, every), (every, self.x))[half]
        here = self.part(unit, half, every, y, x)
        peer = (self.y_peer, self.x_peer)[half]()
        return self.copy(here, here, self.s_three, (unit, half), peer)

    def three_copies(self, unit):
        halves = (0,) if unit >= UP else self.halves(unit, GATHER)
        return [self.three_copy(unit, half) for half in halves]

    def hand_copies(self, unit):
        every = slice(None)
        whole = self.part(unit, None, every, every, every)
        return [self.copy(whole, whole, self.s_hand, unit, self.sibling())]

    def arrived(self, copies):
        for item in copies:
            item.wait_recv()

    def first(self, unit):
        if unit == UP:
            self.arrived(self.up_copies())
        self.start(self.three_copies(unit) if unit == LATE else self.z_copies(unit), unit)

    def second(self, unit):
        if unit == LATE:
            self.arrived(self.three_copies(unit))
            self.start(self.z_copies(unit), unit)
            return
        self.arrived(self.z_copies(unit))
        if unit < UP:
            copies = [self.two_copy(unit, half) for half in self.halves(unit, GATHER)]
        else:
            copies = self.three_copies(unit)
        self.start(copies, unit)

    def third(self, unit, half):
        if half in self.halves(unit, GATHER):
            self.arrived([self.two_copy(unit, half)])
            self.start([self.three_copy(unit, half)], unit)

    def hand(self, unit):
        self.arrived(self.z_copies(unit) if unit == LATE else self.three_copies(unit))
        self.start(self.hand_copies(unit), unit)

    def done(self, unit):
        self.arrived(self.hand_copies(unit))

    def term(self, unit, half, z=slice(None)):
        first = SCATTER[unit]
        return (unit, z, ..., pl.ds(*((0, first), (first, 384 - first))[half]))

    def rs_one_copy(self, unit, half):
        every = slice(None)
        if unit == LATE:
            here = self.part(unit, None, self.z, 1 - self.y, every, grad=True)
            return self.copy(here, self.RL1, self.s_rs1, (unit, 0), self.y_peer())
        if unit >= UP:
            here = self.part(unit, None, every, 1 - self.y, every, grad=True)
            there = self.RU1 if unit == UP else self.RH1
            return self.copy(here, there, self.s_rs1, (unit, 0), self.y_peer())
        y, x = ((1 - self.y, every), (every, 1 - self.x))[half]
        here = self.part(unit, half, every, y, x, grad=True)
        there = self.R1.at[self.term(unit, half)]
        peer = (self.y_peer, self.x_peer)[half]()
        return self.copy(here, there, self.s_rs1, (unit, half), peer)

    def rs_two_copy(self, unit, half):
        y, x = ((self.y, 1 - self.x), (1 - self.y, self.x))[half]
        here = self.part(unit, half, slice(None), y, x, grad=True)
        there = self.R2.at[self.term(unit, half)]
        peer = (self.x_peer, self.y_peer)[half]()
        return self.copy(here, there, self.s_rs2, (unit, half), peer)

    def rs_three_copies(self, unit):
        out = []
        x = slice(None) if unit == UP else self.x
        y = slice(None) if unit == LATE else self.y
        for k in (1, 2, 3):
            here = self.part(unit, None, self.z_index(k), y, x, grad=True)
            if unit < UP:
                there = self.R3.at[unit, k - 1]
            elif unit == UP:
                there = self.RU3.at[k - 1]
            else:
                there = (self.RL3 if unit == LATE else self.RH3).at[k - 1]
            out.append(self.copy(here, there, self.s_rs3, (unit, k - 1), self.z_peer(k)))
        return out

    def up_back_copies(self):
        return [self.copy(self.UPS, self.UPR, self.s_up, 1, self.x_peer())]

    def grad_columns(self, block):
        return pl.ds(pl.multiple_of(self.width * block + 384 * self.c, 128), 384)

    def rs_four_copies(self, unit):
        c = self.c
        if unit < UP:
            there = self.block_grad.at[:, self.grad_columns(unit)]
            return [self.copy(self.SF.at[unit], there, self.s_rs4, unit, self.sibling())]
        if unit == UP:
            columns = self.half_columns_up()
            return [
                self.copy(
                    self.SFU.at[i],
                    self.UPG.at[self.up_side(i), :, columns],
                    self.s_rs5,
                    i,
                    self.sibling(),
                )
                for i in range(2)
            ]
        there = self.down_out.at[:, self.half_columns(c)]
        return [self.copy(self.SFH, there, self.s_rs4, unit, self.sibling())]

    def up_side(self, i):
        return self.x if i == 0 else 1 - self.x

    def half_columns_up(self):
        return pl.ds(pl.multiple_of(self.width * self.c, 128), self.width)

    def add_into(self, ref, term):
        ref[...] = (ref[...].astype(F32) + term.astype(F32)).astype(LOW)

    def rs_one(self, unit):
        halves = (0,) if unit >= UP else self.halves(unit, SCATTER)
        if unit == LATE:
            self.start(self.rs_three_copies(unit))
        else:
            self.start([self.rs_one_copy(unit, half) for half in halves])

    def rs_two(self, unit, half=0):
        every = slice(None)
        if unit < UP and half not in self.halves(unit, SCATTER):
            return
        if unit == LATE:
            self.arrived(self.rs_three_copies(unit))
            here = self.part(unit, None, self.z, every, self.x, grad=True)
            here[...] = self.sum_of(here[...], [self.RL3[k] for k in range(3)]).astype(LOW)
            self.start([self.rs_one_copy(unit, 0)])
            return
        self.arrived([self.rs_one_copy(unit, half)])

        @pl.loop(0, 4, unroll=2)
        def _(z):
            if unit < UP:
                y, x = ((self.y, every), (every, self.x))[half]
                more = self.R1[self.term(unit, half, z)]
                self.add_into(self.part(unit, half, z, y, x, grad=True), more)
            else:
                more = self.RU1[z] if unit == UP else self.RH1[z]
                self.add_into(self.part(unit, None, z, self.y, every, grad=True), more)

        if unit < UP:
            self.start([self.rs_two_copy(unit, half)])
        else:
            self.start(self.rs_three_copies(unit))

    def rs_three(self, unit):
        halves = self.halves(unit, SCATTER)
        self.arrived([self.rs_two_copy(unit, half) for half in halves])

        @pl.loop(0, 4, unroll=2)
        def _(z):
            for half in halves:
                more = self.R2[self.term(unit, half, z)]
                self.add_into(self.part(unit, half, z, self.y, self.x, grad=True), more)

        self.start(self.rs_three_copies(unit))

    def sum_of(self, value, terms):
        return sum((item.astype(F32) for item in terms), value.astype(F32))

    def rs_total(self, unit):
        x = slice(None) if unit == UP else self.x
        own = self.part(unit, None, self.z, self.y, x, grad=True)
        if unit == LATE:
            self.arrived([self.rs_one_copy(unit, 0)])
            return self.sum_of(own[...], [self.RL1[...]])
        self.arrived(self.rs_three_copies(unit))
        if unit < UP:
            return self.sum_of(own[...], [self.R3[unit, k] for k in range(3)])
        ref = self.RU3 if unit == UP else self.RH3
        return self.sum_of(own[...], [ref[k] for k in range(3)])

    def rs_four(self, unit):
        even = self.c == 0
        if unit < UP:
            total = self.rs_total(unit)
            low, high = total[:24], total[24:]
            self.block_grad[:, self.grad_columns(unit)] = jnp.where(even, low, high)
            self.SF[unit] = jnp.where(even, high, low)
            self.start(self.rs_four_copies(unit))
        if unit == UP:
            total = self.rs_total(unit)
            west = self.x == 0
            self.sent("up")
            self.UPS[...] = jnp.where(west, total[1], total[0]).astype(LOW)
            self.start(self.up_back_copies())
            self.up_rows(0, jnp.where(west, total[0], total[1]))
        if unit == DOWN:
            low, high = self.rs_total(DOWN), self.rs_total(DOWN + 1)
            self.down_out[:, self.half_columns(self.c)] = jnp.where(even, low, high)
            self.SFH[...] = jnp.where(even, high, low)
            self.start(self.rs_four_copies(DOWN))

    def up_rows(self, i, total):
        even = self.c == 0
        low, high = total[:24], total[24:]
        self.UPG[self.up_side(i), :, self.half_columns_up()] = jnp.where(even, low, high)
        self.SFU[i] = jnp.where(even, high, low)

    def rs_up(self):
        self.arrived(self.up_back_copies())
        self.up_rows(1, self.UPR[...].astype(F32))
        self.start(self.rs_four_copies(UP))

    def rs_done(self, unit):
        if unit != DOWN + 1:
            self.arrived(self.rs_four_copies(unit))
        if unit == UP:
            for z in range(4):
                at = slice(384 * z, 384 * z + 384)
                start = self.width * (UP + z)
                both = self.join_runs(self.UPG[0, :, at], self.UPG[1, :, at])
                self.block_grad[:, start : start + self.width] = both

    def sum_copies(self, which, stage):
        peers = [[self.sibling()], [self.x_peer()], [self.y_peer()]]
        peers += [[self.z_peer(k) for k in (1, 2, 3)]]
        return [
            self.copy(
                self.V.at[which, stage],
                self.VR.at[which, stage + i],
                self.s_vec,
                (which, stage + i),
                peer,
            )
            for i, peer in enumerate(peers[stage])
        ]

    def placement(self, dtype, rows):
        own = self.width // NODES
        at = lax.broadcasted_iota(jnp.int32, (rows, self.width), 0)
        feature = lax.broadcasted_iota(jnp.int32, (rows, self.width), 1)
        return ((at < own) & (feature == at + own * self.node)).astype(F32).astype(dtype)

    def sum_start(self, which, stage, value):
        self.V[which, stage] = value
        self.start(self.sum_copies(which, stage))

    def sum_end(self, which, stage):
        now = self.sum_copies(which, stage)
        self.arrived(now)
        value = self.V[which, stage]
        for i in range(len(now)):
            value = value + self.VR[which, stage + i]
        return value

    def keep_left(self, place, value):
        self.LHS[place, self.c] = value
        self.send_left(place)

    def send_left(self, place):
        here = self.LHS.at[place, self.c]
        self.start([self.copy(here, here, self.s_left, place, self.sibling())])

    def keep_right(self, place, value):
        self.RHS[place, self.c] = value
        self.send_right(place)

    def send_right(self, place):
        here = self.RHS.at[place, self.c]
        self.start([self.copy(here, here, self.s_right, place, self.sibling())])

    def left_arrived(self, place):
        if ("left", place) not in self.here:
            self.here.add(("left", place))
            here = self.LHS.at[place, self.c]
            self.copy(here, here, self.s_left, place, self.sibling()).wait_recv()

    def right_arrived(self, place):
        if ("right", place) not in self.here:
            self.here.add(("right", place))
            here = self.RHS.at[place, self.c]
            self.copy(here, here, self.s_right, place, self.sibling()).wait_recv()

    def weight(self, block):
        return self.W[block].reshape(self.width, self.width)

    def weight_grad(self, unit):
        left, right = {QS: (0, 0), KS: (0, 1), VS: (0, 2), SO: (1, 3), CQ: (2, 4), CO: (3, 5)}[unit]
        self.sent(unit)
        self.left_arrived(left)
        self.right_arrived(right)
        columns = self.half_columns(self.c)
        right_all = self.RHS[right, :, :, columns].reshape(2 * self.tokens, 384)
        for t in range(2):
            left_all = self.LHS[left, :, :, pl.ds(384 * t, 384)].reshape(2 * self.tokens, 384)
            part = mm_at(left_all, right_all).astype(LOW)
            self.W[unit, pl.ds(2 * t, 2), :, :, :, columns] = part.reshape(2, 2, 2, 48, 384)

    def up_grad(self):
        c = self.c
        self.sent(UP)
        right_all = self.DH[c].reshape(4 * self.tokens, self.width)
        for t in range(2):
            left_all = self.A3[:, :, :, pl.ds(384 * t, 384)].reshape(4 * self.tokens, 384)
            part = mm_at(left_all, right_all).astype(LOW)
            self.W[UP + c, pl.ds(2 * t, 2)] = part.reshape(2, 2, 2, 48, self.width)

    def down_grad(self):
        right_all = self.G4[:, :, :, self.half_columns(self.c)].reshape(4 * self.tokens, 384)
        for z in range(4):
            j, t = z // 2, z % 2
            left_all = self.U[j, :, :, :, pl.ds(384 * t, 384)].reshape(4 * self.tokens, 384)
            part = mm_at(left_all, right_all).astype(LOW)
            self.HG[z] = part.reshape(2, 192, 384)

    def memory_copy(self, which):
        return self.copy(
            self.CS.at[which], self.CM.at[which], self.s_memory, which, self.sibling()
        )

    def memory_term(self, which, c, t):
        left = self.IMG[:, pl.ds(384 * t, 384)]
        part = mm_at(left, self.KV[which, :, self.half_columns(c)])
        return part.reshape(2, 2, 2, 48, 384)

    def memory_grad_other(self, which):
        for t in range(2):
            part = self.memory_term(which, 1 - self.c, t)
            self.CS[which, pl.ds(2 * t, 2)] = part.astype(LOW)
        self.start([self.memory_copy(which)])

    def memory_grad_own(self, which):
        self.memory_copy(which).wait_recv()
        for t in range(2):
            part = self.memory_term(which, self.c, t)
            part = part + self.CM[which, pl.ds(2 * t, 2)].astype(F32)
            self.CP[which, pl.ds(2 * t, 2)] = part.astype(LOW)

    def masked(self, value):
        return value * self.low_lanes, value * self.high_lanes

    def self_attention(self):
        rows = lax.broadcasted_iota(jnp.int32, (128, 128), 0)
        cols = lax.broadcasted_iota(jnp.int32, (128, 128), 1)
        length = jnp.where(cols < 64, self.lengths[0], self.lengths[1])
        allowed = (lax.div(rows, 64) == lax.div(cols, 64)) & (cols <= rows)
        allowed = allowed & (lax.rem(cols, 64) < length)
        parts = []
        for p in range(self.pairs):
            at = slice(128 * p, 128 * p + 128)
            q, k, v = self.QKV[0, :, at], self.QKV[1, :, at], self.QKV[2, :, at]
            both = mm_bt(q, self.stacked(k)) * 0.125
            probs = []
            for h in range(2):
                s = jnp.where(allowed, both[:, 128 * h : 128 * h + 128], -1000000000.0)
                e = jnp.exp(s - jnp.max(s, axis=-1, keepdims=True))
                probs.append(e / jnp.sum(e, axis=-1, keepdims=True))
            prob = jnp.concatenate(probs, axis=1)
            self.PS[p] = prob
            parts.append(mm(prob.astype(LOW), self.stacked(v)).astype(LOW))
        return jnp.concatenate(parts, axis=1)

    def self_attention_back(self, grad):
        parts = ([], [], [])
        for p in range(self.pairs):
            at = slice(128 * p, 128 * p + 128)
            q, k, v = self.QKV[0, :, at], self.QKV[1, :, at], self.QKV[2, :, at]
            g = grad[:, at]
            prob = self.PS[p]
            dp = mm_bt(g, self.stacked(v))
            prod = prob * dp
            parts_ds = []
            for h in range(2):
                lanes = slice(128 * h, 128 * h + 128)
                inner = jnp.sum(prod[:, lanes], axis=-1, keepdims=True)
                parts_ds.append(prob[:, lanes] * (dp[:, lanes] - inner))
            ds = jnp.concatenate(parts_ds, axis=1).astype(LOW)
            dq = mm(ds, self.stacked(k))
            dk = self.diagonal(mm_at(ds, q), 128)
            dv = self.diagonal(mm_at(prob.astype(LOW), g), 128)
            for out, item in zip(parts, (dq * 0.125, dk * 0.125, dv)):
                out.append(item.astype(LOW))
        return [jnp.concatenate(item, axis=1) for item in parts]

    def stacked(self, value):
        a, b = self.masked(value)
        return jnp.concatenate([a, b], axis=0)

    def diagonal(self, value, rows):
        return jnp.where(self.is_first, value[:rows], value[rows:])

    def stacked_four(self, value):
        zero = jnp.zeros((value.shape[0], 128), LOW)
        left = [jnp.concatenate([item, zero], axis=1) for item in self.masked(value[:, :128])]
        right = [jnp.concatenate([zero, item], axis=1) for item in self.masked(value[:, 128:])]
        return jnp.concatenate(left + right, axis=0)

    def diagonal_four(self, value):
        left = jnp.where(self.is_first, value[:64, :128], value[64:128, :128])
        right = jnp.where(self.is_first, value[128:192, 128:], value[192:, 128:])
        return jnp.concatenate([left, right], axis=1)

    def row_pair(self, ref, place, row):
        return jnp.concatenate([ref[place, row : row + 1], ref[place, row + 1 : row + 2]], axis=1)

    def put_pair(self, ref, place, row, value):
        ref[place, row : row + 1] = value[:, :128]
        ref[place, row + 1 : row + 2] = value[:, 128:]

    def memory_forward(self, which):
        w = self.weight(CK + which)

        @pl.loop(0, 3)
        def _(t):
            size = self.IMG.shape[0] // 3
            rows = pl.ds(pl.multiple_of(size * t, 16), size)
            self.KV[which, rows] = mm(self.IMG[rows], w).astype(LOW)

    def cross_forward(self, place):
        rows = pl.ds(pl.multiple_of(place * self.image_rows, 16), self.image_rows)
        for f in range(self.pairs // 2):
            at = slice(256 * f, 256 * f + 256)
            k, v = self.KV[0, rows, at], self.KV[1, rows, at]
            q = self.stacked_four(self.QA[place, :, at])
            s = mm_bt(k, q) * 0.125
            top = jnp.max(s, axis=0, keepdims=True)
            e = jnp.exp(s - top)
            low = e.astype(LOW)
            self.E[place, f] = low
            self.put_pair(self.ST, place, 2 * f, jnp.sum(e, axis=0, keepdims=True))
            self.put_pair(self.ST, place, 8 + 2 * f, top)
            self.put_pair(self.TOP, place, 2 * f, top)
            num = mm_at(low, v)
            self.NUM[place, :, at] = self.diagonal_four(num).astype(LOW)
        self.ST[place, 6:8] = jnp.ones((2, 128), F32)
        self.ST[place, 14:16] = jnp.zeros((2, 128), F32)

    def cross_backward(self, place):
        rows = pl.ds(pl.multiple_of(place * self.image_rows, 16), self.image_rows)
        for f in range(self.pairs // 2):
            at = slice(256 * f, 256 * f + 256)
            k, v = self.KV[0, rows, at], self.KV[1, rows, at]
            q = self.stacked_four(self.QA[place, :, at])
            g = self.stacked_four(self.GA[place, :, at])
            top = self.row_pair(self.TOP, place, 2 * f)
            share = jnp.exp(top - self.row_pair(self.DL, place, 8 + 2 * f))
            e = self.E[place, f].astype(F32) * share
            ds = e * (mm_bt(v, g) + self.row_pair(self.DL, place, 2 * f))
            ds = ds.astype(LOW)
            dq = mm_at(ds, k)
            self.NUM[place, :, at] = (self.diagonal_four(dq) * 0.125).astype(LOW)
            self.KV[0, rows, at] = (mm(ds, q) * 0.125).astype(LOW)
            self.KV[1, rows, at] = mm(e.astype(LOW), g).astype(LOW)

    def captions_of(self, owner):
        return pl.ds(owner * self.count, self.count)

    def caption(self, bits, j):
        return self.owner(bits) * self.count + j

    def partner(self, bit):
        return (self.wide, jnp.bitwise_xor(self.nar, bit))

    def owner(self, bits):
        return jnp.bitwise_xor(self.nar, bits)

    def once(self, key, copies):
        if key not in self.here:
            self.here.add(key)
            self.arrived(copies())

    def share_copies(self, refs, bit, bits, j):
        where = ((self.N + bits) // (2 * bit) - 1) * self.count + j
        place = self.caption(bits, j)
        peer = self.partner(bit)
        return [self.copy(ref.at[place], ref.at[place], sems, where, peer) for ref, sems in refs]

    def share_start(self, refs, j):
        bit = self.N // 2
        while bit:
            self.start(self.share_copies(refs, bit, 0, j))
            bit //= 2

    def share_wait(self, refs, bits, j):
        if bits:
            bit = bits & -bits
            key = (refs is self.queries, bits, j)
            self.once(key, lambda: self.share_copies(refs, bit, bits - bit, j))

    def share_pass(self, refs, j):
        bit = self.N // 2
        while bit:
            for bits in range(2 * bit, self.N, 2 * bit):
                self.share_wait(refs, bits, j)
                self.start(self.share_copies(refs, bit, bits, j))
            bit //= 2

    def merge_slot(self, bit, bits):
        return self.N - self.N // bit + bits // (2 * bit)

    def merge_copies(self, refs, bit, bits, j):
        slot = self.merge_slot(bit, bits)
        place = self.caption(bits + bit, j)
        where = slot * self.count + j
        peer = self.partner(bit)
        return [
            self.copy(ref.at[place], there.at[slot, j], sems, where, peer)
            for ref, there, sems in refs
        ]

    def merge_start(self, refs, bits, j, group):
        if bits % 2:
            self.start(self.merge_copies(refs, 1, bits - 1, j), group)

    def merge_part(self, refs, join, bit, bits, j, group):
        self.arrived(self.merge_copies(refs, bit, bits, j))
        join(self.caption(bits, j), self.merge_slot(bit, bits), j)
        if bits % (4 * bit):
            self.start(self.merge_copies(refs, 2 * bit, bits - 2 * bit, j), group)

    def merge_far(self, refs, join, j, group):
        bit = 1
        while bit < self.N:
            for bits in reversed(range(2 * bit, self.N, 2 * bit)):
                self.merge_part(refs, join, bit, bits, j, group)
            bit *= 2

    def merge_own(self, refs, join, j, group, low, high):
        bit = low
        while bit < high:
            self.merge_part(refs, join, bit, 0, j, group)
            bit *= 2

    def column(self, turned, p):
        return jnp.where(self.is_first, turned[:64, p : p + 1], turned[64:, p : p + 1])

    def turn(self, *rows):
        have = 8 * len(rows)
        return jnp.concatenate([*rows, jnp.zeros((128 - have, 128), F32)], axis=0).T

    def join_softmax(self, place, slot, j):
        total_a, top_a = self.ST[place, :8], self.ST[place, 8:]
        total_b, top_b = self.STR[slot, j, :8], self.STR[slot, j, 8:]
        top = jnp.maximum(top_a, top_b)
        share_a, share_b = jnp.exp(top_a - top), jnp.exp(top_b - top)
        self.ST[place, :8] = share_a * total_a + share_b * total_b
        self.ST[place, 8:] = top
        turned = self.turn(share_a, share_b)
        for p in range(self.pairs):
            at = slice(128 * p, 128 * p + 128)
            a = self.NUM[place, :, at].astype(F32) * self.column(turned, p)
            b = self.NUMR[slot, j, :, at].astype(F32) * self.column(turned, 8 + p)
            self.NUM[place, :, at] = (a + b).astype(LOW)

    def join_sum(self, place, slot, j):
        self.add_into(self.NUM.at[place], self.NUMR[slot, j])

    def attended(self, j):
        place = self.nar * self.count + j
        turned = self.turn(1.0 / self.ST[place, :8])
        self.SCT[j] = turned
        parts = []
        for p in range(self.pairs):
            at = slice(128 * p, 128 * p + 128)
            parts.append(self.NUM[place, :, at].astype(F32) * self.column(turned, p))
        return jnp.concatenate(parts, axis=1)

    def spread_grad(self, j, doc):
        lane = lax.broadcasted_iota(jnp.int32, (128, 128), 1)
        place = self.nar * self.count + j
        rows = self.rows_of(j)
        turned = self.SCT[j]
        inner = jnp.zeros((128, 128), F32)
        for p in range(self.pairs):
            at = slice(128 * p, 128 * p + 128)
            part = doc[:, at] * self.column(turned, p)
            self.GA[place, :, at] = part.astype(LOW)
            prod = part * self.OCF[rows, at]
            a = jnp.sum(jnp.where(self.is_first, prod, 0.0), axis=1, keepdims=True)
            b = jnp.sum(jnp.where(self.is_first, 0.0, prod), axis=1, keepdims=True)
            inner = jnp.where(lane == p, jnp.concatenate([a, b], axis=0), inner)
        self.DL[place, :8] = -inner.T[:8]
        self.DL[place, 8:] = self.ST[place, 8:]

    def rows_of(self, j):
        return slice(self.seq * j, self.seq * j + self.seq)

    def wide_copy(self, ref, sems, i, j):
        here = ref.at[self.c, 1 - self.x if i == 2 else self.x, self.rows_of(j)]
        peer = self.x_peer() if i == 0 else self.sibling()
        return self.copy(here, here, sems, i * self.count + j, peer)

    def keep_wide(self, ref, value, sems, j):
        ref[self.c, self.x, self.rows_of(j)] = value
        self.start([self.wide_copy(ref, sems, i, j) for i in range(2)])

    def wide_across(self, ref, sems, j):
        self.arrived([self.wide_copy(ref, sems, 0, j)])
        self.start([self.wide_copy(ref, sems, 2, j)])

    def wide_arrived(self, ref, sems):
        for j in range(self.count):
            self.arrived([self.wide_copy(ref, sems, i, j) for i in (1, 2)])

    def hidden_copy(self, ref, j, sems):
        here = ref.at[j, self.c]
        return self.copy(here, here, sems, j, self.sibling())

    def fold_copy(self, which, j):
        at = (which, self.rows_of(j))
        where = which * self.count + j
        return self.copy(self.FS.at[at], self.FR.at[at], self.s_fold, where, self.x_peer())

    def fold_start(self, which):
        self.start([self.fold_copy(which, j) for j in range(self.count)])

    def outward(self, name):
        sem = self.s_out[0].at[self.outs.index(name)]
        return pltpu.make_async_copy(getattr(self, name), self.outer[name], sem)

    def image_copy(self, back):
        src, dst = (self.IMG, self.outer["image_grad"]) if back else (self.outer["images"], self.IMG)
        return pltpu.make_async_copy(src, dst, self.s_image[0].at[0])

    def both_halves(self, value):
        low, high = value[: self.tokens], value[self.tokens :]
        west = self.x == 0
        return jnp.where(west, low, high), jnp.where(west, high, low)

    def do_begin(self):
        self.image_copy(False).start()
        self.pair_pack()
        self.enter()
        self.start(self.pair_copies())
        rows = [getattr(self, name)[...].astype(F32) for name in VECTORS]
        rows = jnp.concatenate(rows + [jnp.zeros((2, rows[0].shape[1]), F32)], axis=0)
        self.sum_start(0, 0, mm(rows.astype(LOW), self.placement(LOW, rows.shape[1])))
        self.pair_merge()
        self.inputs = self.captions[...].astype(F32)
        self.queries = [(self.QA, self.s_query)]
        self.numbers = [(self.NUM, self.NUMR, self.s_num), (self.ST, self.STR, self.s_st)]
        self.grads = [(self.GA, self.s_g), (self.DL, self.s_dl)]
        self.back = [(self.NUM, self.NUMR, self.s_dq)]

    def do_up0(self):
        self.start(self.up_copies(), "up")

    def do_vec(self, stage):
        self.sum_start(0, stage, self.sum_end(0, stage - 1))

    def do_g0(self):
        for j in range(self.count):
            self.keep_wide(self.G4, self.out_grad[self.rows_of(j)], self.s_g4, j)

    def do_g1(self):
        for j in range(self.count):
            self.wide_across(self.G4, self.s_g4, j)

    def do_mem(self, which):
        if "images" not in self.here:
            self.here.add("images")
            self.image_copy(False).wait()
        self.done(CK + which)
        self.memory_forward(which)

    def do_a1(self):
        vectors = self.sum_end(0, 3)
        self.gains = [vectors[i : i + 1] for i in (0, 2, 4)]
        self.shifts = [vectors[i : i + 1] for i in (1, 3, 5)]
        self.rstds = [None, None, []]
        self.r2 = []
        self.a1 = self.normed(0, self.inputs)
        self.keep_left(0, self.a1)

    def normed(self, which, value):
        hat, self.rstds[which], out = norm(value, self.gains[which], self.shifts[which])
        self.HAT[which] = hat
        return out.astype(LOW)

    def pulled(self, which, grad):
        return norm_pull(grad, self.HAT[which], self.rstds[which], self.gains[which])

    def do_qkv(self, which):
        self.done(which)
        self.QKV[which] = mm(self.a1, self.weight(which)).astype(LOW)

    def do_sa(self):
        self.mixed = self.self_attention()
        self.keep_left(1, self.mixed)

    def do_r1(self):
        self.done(SO)
        self.r1 = self.inputs + mm(self.mixed, self.weight(SO))
        self.a2 = self.normed(1, self.r1)
        self.keep_left(2, self.a2)

    def do_cq(self):
        self.done(CQ)
        query = mm(self.a2, self.weight(CQ)).astype(LOW)
        self.QA[self.captions_of(self.nar)] = query.reshape(self.count, 64, self.width)
        for j in range(self.count):
            self.share_start(self.queries, j)

    def do_q1(self, j):
        self.share_pass(self.queries, j)

    def do_cf(self, item):
        bits, j = divmod(item, self.count)
        self.share_wait(self.queries, bits, j)
        self.cross_forward(self.caption(bits, j))
        self.merge_start(self.numbers, bits, j, "numbers")

    def do_m1(self, j):
        self.merge_far(self.numbers, self.join_softmax, j, "numbers")

    def do_m2(self, j):
        self.merge_own(self.numbers, self.join_softmax, j, "numbers", 1, 2)

    def do_a3(self, j):
        self.merge_own(self.numbers, self.join_softmax, j, "numbers", 2, self.N)
        rows = self.rows_of(j)
        full = self.attended(j)
        self.OCF[rows] = full
        oc = full.astype(LOW)
        self.LHS[3, self.c, rows] = oc
        self.once("co", lambda: self.hand_copies(CO))
        r2 = self.r1[rows] + mm(oc, self.weight(CO))
        hat, rstd, out = norm(r2, self.gains[2], self.shifts[2])
        self.HAT[2, rows] = hat
        self.keep_wide(self.A3, out.astype(LOW), self.s_a3, j)
        self.r2.append(r2)
        self.rstds[2].append(rstd)
        if j == self.count - 1:
            self.send_left(3)

    def do_x1(self, j):
        self.wide_across(self.A3, self.s_a3, j)

    def do_hp(self):
        self.done(UP)
        a3 = self.A3[self.c].reshape(2 * self.tokens, self.width)
        for j in range(2):
            hidden = mm(a3, self.weight(UP + j))
            square = hidden * hidden
            tanh = jnp.tanh(GELU_A * hidden * (1.0 + GELU_B * square))
            act = (0.5 * hidden * (1.0 + tanh)).astype(LOW)
            self.SLOPE[j] = 0.5 * (1.0 + tanh) + 0.5 * hidden * (1.0 - tanh * tanh) * (
                GELU_A * (1.0 + 3.0 * GELU_B * square)
            )
            self.U[j, self.c] = act.reshape(2, self.tokens, self.width)
            self.start([self.hidden_copy(self.U, j, self.s_u)])

    def do_dg(self):
        self.wide_arrived(self.G4, self.s_g4)
        for j in range(2):
            self.hidden_copy(self.U, j, self.s_u).wait_recv()
        self.down_grad()

    def do_e3(self):
        self.done(DOWN)
        self.done(DOWN + 1)
        grad = self.G4[self.c].reshape(2 * self.tokens, self.width)
        e3 = 0.0
        for j in range(2):
            down = [self.HD[i, 2 * j : 2 * j + 2].reshape(self.width, 384) for i in range(2)]
            back = mm_bt(grad[:, :384], down[0]) + mm_bt(grad[:, 384:], down[1])
            dhp = (back * self.SLOPE[j]).astype(LOW)
            self.DH[j, self.c] = dhp.reshape(2, self.tokens, self.width)
            self.start([self.hidden_copy(self.DH, j, self.s_dh)])
            e3 = e3 + mm_bt(dhp, self.weight(UP + j))
        self.dr2 = []
        self.e3, other = self.both_halves(e3)
        self.FS[0] = other.astype(LOW)
        self.fold_start(0)

    def do_out(self):
        out = [0.0, 0.0]
        for j in range(2):
            act = self.U[j, self.c].reshape(2 * self.tokens, self.width)
            for i in range(2):
                down = self.HD[i, 2 * j : 2 * j + 2].reshape(self.width, 384)
                out[i] = out[i] + mm(act, down)
        own, other = self.both_halves(jnp.concatenate(out, axis=1))
        self.out = jnp.concatenate(self.r2, axis=0) + own
        self.FS[1] = other.astype(LOW)
        self.fold_start(1)

    def do_lo(self):
        self.arrived([self.fold_copy(1, j) for j in range(self.count)])
        self.layer_out[...] = (self.out + self.FR[1].astype(F32)).astype(LOW)
        self.outward("layer_out").start()

    def do_ug(self):
        self.wide_arrived(self.A3, self.s_a3)
        for j in range(2):
            self.hidden_copy(self.DH, j, self.s_dh).wait_recv()
        self.up_grad()

    def do_dr2(self, j):
        self.arrived([self.fold_copy(0, j)])
        rows = self.rows_of(j)
        e3 = self.e3[rows] + self.FR[0, rows].astype(F32)
        back, *vec = norm_pull(e3, self.HAT[2, rows], self.rstds[2][j], self.gains[2])
        self.vec3 = [a + b for a, b in zip(self.vec3, vec)] if j else vec
        dr2 = self.out_grad[rows].astype(F32) + back
        self.dr2.append(dr2)
        dcat = dr2.astype(LOW)
        self.RHS[5, self.c, rows] = dcat
        self.spread_grad(j, mm_bt(dcat, self.weight(CO)))
        self.share_start(self.grads, j)
        if j == self.count - 1:
            self.send_right(5)

    def do_p1(self, j):
        self.share_pass(self.grads, j)

    def do_cb(self, item):
        bits, j = divmod(item, self.count)
        self.share_wait(self.grads, bits, j)
        self.sent("numbers")
        self.cross_backward(self.caption(bits, j))
        self.merge_start(self.back, bits, j, "back")

    def do_n1(self, j):
        self.merge_far(self.back, self.join_sum, j, "back")

    def do_n2(self, j):
        self.merge_own(self.back, self.join_sum, j, "back", 1, 2)

    def do_dq(self):
        for j in range(self.count):
            self.merge_own(self.back, self.join_sum, j, "back", 2, self.N)
        dqc = self.NUM[self.captions_of(self.nar)].reshape(self.tokens, self.width)
        self.keep_right(4, dqc)
        back, *self.vec2 = self.pulled(1, mm_bt(dqc, self.weight(CQ)))
        self.dr1 = jnp.concatenate(self.dr2, axis=0) + back
        dattn = self.dr1.astype(LOW)
        self.keep_right(3, dattn)
        self.dos = mm_bt(dattn, self.weight(SO)).astype(LOW)

    def do_mo(self, which):
        self.memory_grad_other(which)

    def do_mw(self, which):
        self.memory_grad_own(which)

    def do_wg(self, unit):
        self.weight_grad(unit)

    def do_sb(self):
        e1 = 0.0
        for j, item in enumerate(self.self_attention_back(self.dos)):
            self.keep_right(j, item)
            e1 = e1 + mm_bt(item, self.weight(j))
        back, *vec = self.pulled(0, e1)
        self.input_grad[...] = (self.dr1 + back).astype(LOW)
        self.outward("input_grad").start()
        vec = vec + self.vec2 + self.vec3 + [jnp.zeros((2, self.width), F32)]
        self.sum_start(1, 0, jnp.concatenate(vec, axis=0))

    def do_sum(self, stage):
        self.sum_start(1, stage, self.sum_end(1, stage - 1))

    def do_img(self):
        @pl.loop(0, 3)
        def _(t):
            size = self.IMG.shape[0] // 3
            rows = pl.ds(pl.multiple_of(size * t, 16), size)
            part = mm_bt(self.KV[0, rows], self.weight(CK))
            part = part + mm_bt(self.KV[1, rows], self.weight(CV))
            self.IMG[rows] = part.astype(LOW)

        self.image_copy(True).start()

    def do_end(self):
        self.vec_grad[...] = lax.dot_general(
            self.sum_end(1, 3),
            self.placement(F32, 128),
            (((1,), (1,)), ((), ())),
            precision=lax.Precision.HIGHEST,
            preferred_element_type=F32,
        )
        self.outward("vec_grad").start()
        for unit in reversed(range(UNITS)):
            self.rs_done(unit)
            if unit == DOWN:
                self.outward("down_out").start()
        self.outward("block_grad").start()
        self.image_copy(True).wait()
        for name in self.outs:
            self.outward(name).wait()
        for group in list(self.started):
            self.sent(group)

    def run(self):
        steps = {
            Step.begin: self.do_begin,
            Step.up0: self.do_up0,
            Step.vec: self.do_vec,
            Step.g0: self.do_g0,
            Step.g1: self.do_g1,
            Step.mem: self.do_mem,
            Step.a1: self.do_a1,
            Step.qkv: self.do_qkv,
            Step.sa: self.do_sa,
            Step.r1: self.do_r1,
            Step.cq: self.do_cq,
            Step.q1: self.do_q1,
            Step.cf: self.do_cf,
            Step.m1: self.do_m1,
            Step.m2: self.do_m2,
            Step.a3: self.do_a3,
            Step.x1: self.do_x1,
            Step.hp: self.do_hp,
            Step.dg: self.do_dg,
            Step.e3: self.do_e3,
            Step.out: self.do_out,
            Step.lo: self.do_lo,
            Step.ug: self.do_ug,
            Step.dr2: self.do_dr2,
            Step.p1: self.do_p1,
            Step.cb: self.do_cb,
            Step.n1: self.do_n1,
            Step.n2: self.do_n2,
            Step.dq: self.do_dq,
            Step.mo: self.do_mo,
            Step.mw: self.do_mw,
            Step.wg: self.do_wg,
            Step.sb: self.do_sb,
            Step.sum: self.do_sum,
            Step.img: self.do_img,
            Step.end: self.do_end,
            Step.F: self.first,
            Step.S: self.second,
            Step.TA: lambda unit: self.third(unit, 0),
            Step.TB: lambda unit: self.third(unit, 1),
            Step.H: self.hand,
            Step.R1: self.rs_one,
            Step.RA: self.rs_two,
            Step.RB: lambda unit: self.rs_two(unit, 1),
            Step.R3: self.rs_three,
            Step.R4: self.rs_four,
            Step.RU: lambda unit: self.rs_up(),
        }
        for step, *place in ORDER:
            steps[step](*place)


def layer_call(lanes, narrow, captions, images, lengths, out_grad, *params):
    tokens, width = captions.shape
    count = tokens // 64
    groups = narrow * count
    image_rows = images.shape[0]
    pairs = width // 128
    ins = ["captions", "out_grad", "self_proj", "self_output"]
    ins += ["cross_query", "cross_memory", "cross_output", "hidden_up", "hidden_down", *VECTORS]
    given = dict(zip(ins, (captions, out_grad, *params)))
    outs = {
        "layer_out": ((tokens, width), LOW),
        "input_grad": ((tokens, width), LOW),
        "image_grad": ((image_rows, width), LOW),
        "block_grad": ((24, 12 * width), F32),
        "down_out": ((96, width), F32),
        "vec_grad": ((8, 128), F32),
    }
    results = [name for name in outs if name != "image_grad"]
    memory = {name: outs[name] for name in results}
    memory |= {
        "W": ((10, 4, 2, 2, 48, width), LOW),
        "HD": ((2, 4, 2, 192, 384), LOW),
        "HG": ((4, 2, 192, 384), LOW),
        "UPS": ((48, width), LOW),
        "UPR": ((48, width), LOW),
        "PA": ((2, 24 * UP, 384), LOW),
        "PB": ((2, 48, width), LOW),
        "IMG": ((image_rows, width), LOW),
        "KV": ((2, image_rows, width), LOW),
        "E": ((groups, pairs // 2, image_rows // groups, 256), LOW),
        "LHS": ((4, 2, tokens, width), LOW),
        "RHS": ((6, 2, tokens, width), LOW),
        "A3": ((2, 2, tokens, width), LOW),
        "G4": ((2, 2, tokens, width), LOW),
        "U": ((2, 2, 2, tokens, width), LOW),
        "DH": ((2, 2, 2, tokens, width), LOW),
        "FS": ((2, tokens, width), LOW),
        "FR": ((2, tokens, width), LOW),
        "R1": ((UP, 4, 2, 48, 384), LOW),
        "R2": ((UP, 4, 48, 384), LOW),
        "R3": ((UP, 3, 48, 384), LOW),
        "RU1": ((4, 2, 48, width), LOW),
        "RU3": ((3, 2, 48, width), LOW),
        "RH1": ((4, 96, 384), LOW),
        "RH3": ((3, 96, 384), LOW),
        "RL1": ((96, 384), LOW),
        "RL3": ((3, 2, 96, 384), LOW),
        "CM": ((2, 4, 2, 2, 48, 384), LOW),
        "CS": ((2, 4, 2, 2, 48, 384), LOW),
        "CP": ((2, 4, 2, 2, 48, 384), LOW),
        "SF": ((UP, 24, 384), F32),
        "SFU": ((2, 24, width), F32),
        "UPG": ((2, 24, 2 * width), F32),
        "SFH": ((96, 384), F32),
        "V": ((2, 4, 8, width), F32),
        "VR": ((2, 6, 8, width), F32),
        "QKV": ((3, tokens, width), LOW),
        "PS": ((HEADS // 2, 128, 256), F32),
        "HAT": ((3, tokens, width), F32),
        "SLOPE": ((2, 2 * tokens, width), F32),
        "OCF": ((tokens, width), F32),
        "QA": ((groups, 64, width), LOW),
        "NUM": ((groups, 64, width), LOW),
        "ST": ((groups, 16, 128), F32),
        "TOP": ((groups, 8, 128), F32),
        "NUMR": ((narrow - 1, count, 64, width), LOW),
        "STR": ((narrow - 1, count, 16, 128), F32),
        "SCT": ((count, 128, 128), F32),
        "GA": ((groups, 64, width), LOW),
        "DL": ((groups, 16, 128), F32),
    }
    signals = {
        "s_pair": (3,),
        "s_up": (2,),
        "s_z": (UNITS, 3),
        "s_two": (UP, 2),
        "s_three": (UNITS, 2),
        "s_hand": (UNITS,),
        "s_rs1": (UNITS, 2),
        "s_rs2": (UP, 2),
        "s_rs3": (UNITS, 3),
        "s_rs4": (UNITS,),
        "s_rs5": (2,),
        "s_vec": (2, 6),
        "s_left": (4,),
        "s_right": (6,),
        "s_a3": (3 * count,),
        "s_g4": (3 * count,),
        "s_u": (2,),
        "s_dh": (2,),
        "s_fold": (2 * count,),
        "s_memory": (2,),
        "s_query": ((narrow - 1) * count,),
        "s_num": ((narrow - 1) * count,),
        "s_st": ((narrow - 1) * count,),
        "s_g": ((narrow - 1) * count,),
        "s_dl": ((narrow - 1) * count,),
        "s_dq": ((narrow - 1) * count,),
        "s_image": (1,),
        "s_out": (len(results),),
    }
    scratch = [pltpu.VMEM(shape, kind) for shape, kind in memory.values()]
    for shape in signals.values():
        scratch += [pltpu.SemaphoreType.DMA(shape)] * 2

    def body(*refs):
        names = ["lengths", "images", *ins, *outs]
        outer = dict(zip(names, refs))
        named = dict(zip(memory, refs[len(names) :]))
        rest = refs[len(names) + len(memory) :]
        for i, name in enumerate(signals):
            named[name] = (rest[2 * i], rest[2 * i + 1])
        named |= {name: outer[name] for name in ["lengths", *ins]}
        named |= {"outer": outer, "outs": results}
        Layer(named, lanes, narrow).run()

    anywhere = pl.BlockSpec(memory_space=pl.ANY)
    vmem = pl.BlockSpec(memory_space=pltpu.VMEM)
    return pl.pallas_call(
        body,
        out_shape=[jax.ShapeDtypeStruct(shape, kind) for shape, kind in outs.values()],
        in_specs=[pl.BlockSpec(memory_space=pltpu.SMEM), anywhere] + [vmem] * len(ins),
        out_specs=[anywhere] * len(outs),
        scratch_shapes=scratch,
        compiler_params=pltpu.CompilerParams(
            collective_id=0, has_side_effects=True, vmem_limit_bytes=VMEM_LIMIT
        ),
        cost_estimate=pl.CostEstimate(
            flops=17 * 10**9, bytes_accessed=8 * 10**6, transcendentals=2 * 10**6
        ),
        name="layer",
    )(lengths, images, *given.values())


def deliver(ranges, arrays, block_grad, vec_grad, own):
    count = len(arrays)
    ins = [vec_grad, block_grad, *arrays]
    outs = [jax.ShapeDtypeStruct((1, own), F32)] * len(VECTORS)
    outs += [jax.ShapeDtypeStruct((block_grad.shape[0], b - a), F32) for a, b in ranges]
    outs += [jax.ShapeDtypeStruct(item.shape, item.dtype) for item in arrays]

    def body(*refs):
        given, found = refs[: len(ins)], refs[len(ins) : len(ins) + len(outs)]
        rest = refs[len(ins) + len(outs) :]
        held, rows, sems = rest[: len(ins)], rest[len(ins) : -1], rest[-1]
        copies = zip(given, held)
        into = [pltpu.make_async_copy(a, b, sems.at[i]) for i, (a, b) in enumerate(copies)]
        for item in into:
            item.start()
        views = [*rows, *[held[1].at[:, pl.ds(a, b - a)] for a, b in ranges], *held[2:]]
        back = [
            pltpu.make_async_copy(a, b, sems.at[len(ins) + i])
            for i, (a, b) in enumerate(zip(views, found))
        ]
        into[0].wait()
        for i, ref in enumerate(rows):
            ref[...] = held[0][i : i + 1, :own]
            back[i].start()
        into[1].wait()
        for item in back[len(rows) : len(rows) + len(ranges)]:
            item.start()
        for item, last in zip(into[2:], back[len(rows) + len(ranges) :]):
            item.wait()
            last.start()
        for item in back:
            item.wait()

    hold = [pltpu.VMEM(item.shape, item.dtype) for item in ins]
    hold += [pltpu.VMEM((1, own), F32)] * len(VECTORS)
    anywhere = pl.BlockSpec(memory_space=pl.ANY)
    return pl.pallas_call(
        body,
        out_shape=outs,
        in_specs=[anywhere] * len(ins),
        out_specs=[anywhere] * len(outs),
        scratch_shapes=hold + [pltpu.SemaphoreType.DMA((len(ins) + len(outs),))],
        compiler_params=pltpu.CompilerParams(vmem_limit_bytes=VMEM_LIMIT),
        name="deliver",
    )(*ins)


def lane_gather(value, lanes, narrow, axis):
    if lanes == 1:
        return value
    assert lanes % narrow == 0
    value = lax.all_gather(value, "narrow", axis=axis, tiled=True)
    step = 1
    wide_count = lax.axis_size("wide")
    while step * narrow < lanes:
        swap = [(i, i ^ step) for i in range(wide_count)]
        other = lax.ppermute(value, "wide", swap)
        low = (lax.axis_index("wide") // step) % 2 == 0
        first = jnp.where(low, value, other)
        second = jnp.where(low, other, value)
        value = jnp.concatenate([first, second], axis=axis)
        step *= 2
    return value


def lane_scatter(value, lanes, narrow, axis):
    if lanes == 1:
        return value
    wide_count = lax.axis_size("wide")
    step = lanes // narrow
    while step > 1:
        step //= 2
        swap = [(i, i ^ step) for i in range(wide_count)]
        first, second = jnp.split(value, 2, axis=axis)
        low = (lax.axis_index("wide") // step) % 2 == 0
        other = lax.ppermute(jnp.where(low, second, first), "wide", swap)
        value = jnp.where(low, first, second) + other
    return lax.psum_scatter(value, "narrow", scatter_dimension=axis, tiled=True)


def per_device(captions, images, lengths, out_grad, *params):
    narrow = lax.axis_size("narrow")
    devices = lax.axis_size("wide") * narrow
    lanes = devices // NODES
    count, seq_len, width = captions.shape
    tokens = count * seq_len
    params = [lane_gather(item, lanes, narrow, 0) for item in params]
    out, input_grad, image_grad, block_grad, down_grad, vec_grad = layer_call(
        lanes,
        narrow,
        captions.reshape(tokens, width),
        images.reshape(-1, width),
        lengths,
        out_grad.reshape(tokens, width),
        *params[:7],
        *[item.reshape(1, -1) for item in params[7:]],
    )
    block_grad = lane_scatter(block_grad, lanes, narrow, 0)
    down_grad = lane_scatter(down_grad, lanes, narrow, 0)
    if lanes > 1:
        vec_grad = lane_scatter(vec_grad[:, : width // NODES], lanes, narrow, 1)

    ends = (QS, SO, CK, CQ, CO, UP, UP + 4)
    ranges = [(width * a, width * b) for a, b in zip(ends, ends[1:])]
    arrays = [out, input_grad, image_grad, down_grad]
    own = width // devices
    found = deliver(ranges, arrays, block_grad, vec_grad, own)
    vectors, found = found[: len(VECTORS)], found[len(VECTORS) :]
    joint, self_out, memory, query, cross, up = found[:6]
    out, input_grad, image_grad, down_grad = found[6:]
    return (
        out.reshape(captions.shape),
        input_grad.reshape(captions.shape),
        image_grad.reshape(images.shape),
        joint,
        self_out,
        query,
        memory,
        cross,
        up,
        down_grad,
        *[item.reshape(-1) for item in vectors],
    )


def solution(mesh):
    both = ("wide", "narrow")
    rows = P(both, None)
    text = P(both, None, None)
    vector = P(both)
    image = P("wide", "narrow", None)
    in_specs = (text, image, vector, text) + (rows,) * 7 + (vector,) * 6
    out_specs = (text, text, image) + (rows,) * 7 + (vector,) * 6
    return jax.shard_map(
        per_device, mesh=mesh, in_specs=in_specs, out_specs=out_specs, check_vma=False
    )
```
